32 devices in a mesh: dp: 8 (over y, x, core), mp: 4 (over z).
Axes of the slice: x: 2, y: 2, z: 4, core: 2. Of those that a mesh axis runs over, the one named last changes fastest.
Arguments:
- inputs: bfloat16 [64, 128, 512], P('dp'), may hold values from -6 to 6
- encoder: bfloat16 [64, 512, 512], P('dp', 'mp'), may hold values from -6 to 6
- cotangent: bfloat16 [64, 128, 512], P('dp'), may hold values from -6 to 6
- target_segments: int32 [64, 128], P('dp'), may hold values from 0 to 2, never falling along the last dimension, each value on 1 to 64 neighbouring positions
- encoder_segments: int32 [64, 512], P('dp'), may hold values from 0 to 2, never falling along the last dimension, each value on 1 to 256 neighbouring positions
- query_weight: float32 [2, 512, 512], P(None, 'dp', 'mp'), may hold values from -0.0625 to 0.0625
- query_first: float32 [2, 512, 512], P(None, 'dp', 'mp'), may hold values from -640 to 640
- query_second: float32 [2, 512, 512], P(None, 'dp', 'mp'), may hold values from 32768 to 163840
- keyval_weight: float32 [2, 2, 512, 512], P(None, None, 'dp', 'mp'), may hold values from -0.25 to 0.25
- keyval_first: float32 [2, 2, 512, 512], P(None, None, 'dp', 'mp'), may hold values from -128 to 128
- keyval_second: float32 [2, 2, 512, 512], P(None, None, 'dp', 'mp'), may hold values from 1310.72 to 6553.6
- output_weight: float32 [2, 512, 512], P(None, 'mp', 'dp'), may hold values from -0.75 to 0.75
- output_first: float32 [2, 512, 512], P(None, 'mp', 'dp'), may hold values from -24 to 24
- output_second: float32 [2, 512, 512], P(None, 'mp', 'dp'), may hold values from 52.4288 to 262.144
- inner_weight: float32 [512, 2048], P('dp', 'mp'), may hold values from -0.25 to 0.25
- inner_first: float32 [512, 2048], P('dp', 'mp'), may hold values from -40 to 40
- inner_second: float32 [512, 2048], P('dp', 'mp'), may hold values from 163.84 to 819.2
- outer_weight: float32 [2048, 512], P('mp', 'dp'), may hold values from -0.1875 to 0.1875
- outer_first: float32 [2048, 512], P('mp', 'dp'), may hold values from -32 to 32
- outer_second: float32 [2048, 512], P('mp', 'dp'), may hold values from 122.88 to 573.44
- gains: float32 [3, 512], P(None, 'dp'), may hold values from 0.5 to 1.5
- gains_first: float32 [3, 512], P(None, 'dp'), may hold values from -256 to 256
- gains_second: float32 [3, 512], P(None, 'dp'), may hold values from 5242.88 to 26214.4
- bias_table: float32 [32, 8], P('dp', 'mp'), may hold values from -6 to 6
- table_first: float32 [32, 8], P('dp', 'mp'), may hold values from -448 to 448
- table_second: float32 [32, 8], P('dp', 'mp'), may hold values from 16384 to 81920
Outputs:
- outputs: bfloat16 [64, 128, 512], P('dp')
- input_grad: bfloat16 [64, 128, 512], P('dp')
- new_query_first: float32 [2, 512, 512], P(None, 'dp', 'mp')
- new_query_second: float32 [2, 512, 512], P(None, 'dp', 'mp')
- new_query_weight: float32 [2, 512, 512], P(None, 'dp', 'mp')
- new_keyval_first: float32 [2, 2, 512, 512], P(None, None, 'dp', 'mp')
- new_keyval_second: float32 [2, 2, 512, 512], P(None, None, 'dp', 'mp')
- new_keyval_weight: float32 [2, 2, 512, 512], P(None, None, 'dp', 'mp')
- new_output_first: float32 [2, 512, 512], P(None, 'mp', 'dp')
- new_output_second: float32 [2, 512, 512], P(None, 'mp', 'dp')
- new_output_weight: float32 [2, 512, 512], P(None, 'mp', 'dp')
- new_inner_first: float32 [512, 2048], P('dp', 'mp')
- new_inner_second: float32 [512, 2048], P('dp', 'mp')
- new_inner_weight: float32 [512, 2048], P('dp', 'mp')
- new_outer_first: float32 [2048, 512], P('mp', 'dp')
- new_outer_second: float32 [2048, 512], P('mp', 'dp')
- new_outer_weight: float32 [2048, 512], P('mp', 'dp')
- new_gains_first: float32 [3, 512], P(None, 'dp')
- new_gains_second: float32 [3, 512], P(None, 'dp')
- new_gains: float32 [3, 512], P(None, 'dp')
- new_table_first: float32 [32, 8], P('dp', 'mp')
- new_table_second: float32 [32, 8], P('dp', 'mp')
- new_table: float32 [32, 8], P('dp', 'mp')
The draws below stay inside these ranges and needn't reach their ends.
Inputs may be any that keep to these rules, and one draw needn't show every extreme that they name: `target_segments`: along each row the numbers never fall and every number from 0 to 2 occurs; target tokens of example s attend to the encoder tokens of example s of the same row. `encoder_segments`: along each row the numbers never fall and every number from 0 to 2 occurs.
All inputs are finite; a program needn't handle non-finite values.
Results may differ from the reference program's by a relative error of at most 0.02.
The reference program's roundings to bfloat16 on the way count: a program that leaves them out, or rounds other values in their place, can miss the bound.
Values may be sent and summed in bfloat16 or wider, within the bound.
No kernel may reach another device: no remote copies, remote signals or barrier semaphores. Data moves between devices by JAX's collectives and lax.ppermute only.
A program may use at most 128 MiB of HBM per device.

```python
import math
import jax
import jax.numpy as jnp
import numpy as np
from jax import lax

D = 512
HEADS = 8
HEAD_DIM = 64
FF = 2048
NB = 32
HD = 512
LT = 128
LE = 512
SEGS = 3
STEP = 10
SEQS = 64
TOKENS = 8192
N_MP = 4


def steps_of(rng, dims, pieces, low, largest):
    loudness, own = 1.0, jax.random.fold_in(rng, 6)
    for dim, shards_of in pieces:
        heights = jnp.exp(jax.random.uniform(jax.random.fold_in(own, dim), (shards_of,), jnp.float32, low / len(pieces), largest / len(pieces)))
        loudness = loudness * jnp.repeat(heights, dims[dim] // shards_of).reshape([-1 if axis == dim else 1 for axis in range(len(dims))])
    return loudness


def profile(count, total, most, lean):
    weights = [(1 << 20) // math.isqrt(standing ** lean) + 1 for standing in range(2, count + 1)]
    rest, holding = total - most - (count - 1), [1] * (count - 1)
    while rest > 0:
        free = [i for i in range(count - 1) if holding[i] < most]
        mass, budget = sum([weights[i] for i in free]), rest
        for i in free:
            addition = min(most - holding[i], max(1, budget * weights[i] // mass), rest)
            holding[i] = holding[i] + addition
            rest = rest - addition
    return np.array([most] + holding)


def uneven(own_key, count, total, bound, lean):
    if count == 2:
        one = jax.random.randint(own_key, (), max(1, total - bound), min(bound, total - 1) + 1)
        return jnp.stack([one, total - one])
    sizes = jnp.asarray(profile(count, total, bound, lean), jnp.int32)
    pairs = (count - 1) // 2
    donor, sink = sizes[1:1 + 2 * pairs:2], sizes[2:2 + 2 * pairs:2]
    margin = jnp.minimum(donor - 1, bound - sink)
    passed = jax.random.randint(jax.random.fold_in(own_key, 1), (pairs,), 0, 1 << 20) % (margin + 1)
    sizes = sizes.at[1:1 + 2 * pairs:2].set(donor - passed).at[2:2 + 2 * pairs:2].set(sink + passed)
    return sizes[jax.random.permutation(jax.random.fold_in(own_key, 2), count)]


def bell_draw(rng, shape, scale, reach, pieces=(), held_as=jnp.bfloat16):
    values = scale * jax.random.normal(rng, shape, jnp.float32)
    if pieces:
        values = values * steps_of(rng, shape, pieces, -0.22, 0.18)
    return jnp.clip(values, -reach, reach).astype(held_as)


def setup_inputs(seed: int = 0) -> dict:
    key_list = jax.random.split(jax.random.key(seed), 27)
    return {
        "inputs": bell_draw(key_list[0], (SEQS, LT, D), 1.0, 6.0, ((0, 8),)),
        "encoder": bell_draw(key_list[1], (SEQS, LE, D), 1.0, 6.0, ((0, 8), (1, 4))),
        "cotangent": bell_draw(key_list[2], (SEQS, LT, D), 1.0, 6.0, ((0, 8),)),
        "target_segments": jax.vmap(lambda own: jnp.searchsorted(jnp.cumsum(uneven(own, SEGS, LT, LT // 2, 1)), jnp.arange(LT), side="right"))(jax.random.split(key_list[3], SEQS)).reshape((SEQS, LT)).astype(jnp.int32),
        "encoder_segments": jax.vmap(lambda own: jnp.searchsorted(jnp.cumsum(uneven(own, SEGS, LE, LE // 2, 1)), jnp.arange(LE), side="right"))(jax.random.split(key_list[4], SEQS)).reshape((SEQS, LE)).astype(jnp.int32),
        "query_weight": bell_draw(key_list[5], (2, D, HD), (16 * D) ** -0.5, 0.0625, ((1, 8), (2, 4)), jnp.float32),
        "query_first": bell_draw(key_list[6], (2, D, HD), (1.1 * TOKENS ** 0.5), 640.0, ((1, 8), (2, 4)), jnp.float32),
        "query_second": jnp.clip(jnp.exp(math.log(163840.0) - 1.609438 * jax.random.uniform(key_list[7], (2, D, HD), jnp.float32) ** steps_of(key_list[7], (2, D, HD), ((1, 8), (2, 4)), -0.2, 0.2)), 32768.0, 163840.0),
        "keyval_weight": bell_draw(key_list[8], (2, 2, D, HD), D ** -0.5, 0.25, ((2, 8), (3, 4)), jnp.float32),
        "keyval_first": bell_draw(key_list[9], (2, 2, D, HD), (0.22 * TOKENS ** 0.5), 128.0, ((2, 8), (3, 4)), jnp.float32),
        "keyval_second": jnp.clip(jnp.exp(math.log(6553.6) - 1.609438 * jax.random.uniform(key_list[10], (2, 2, D, HD), jnp.float32) ** steps_of(key_list[10], (2, 2, D, HD), ((2, 8), (3, 4)), -0.2, 0.2)), 1310.72, 6553.6),
        "output_weight": bell_draw(key_list[11], (2, HD, D), (HD // 8) ** -0.5, 0.75, ((1, 4), (2, 8)), jnp.float32),
        "output_first": bell_draw(key_list[12], (2, HD, D), (0.045 * TOKENS ** 0.5), 24.0, ((1, 4), (2, 8)), jnp.float32),
        "output_second": jnp.clip(jnp.exp(math.log(262.144) - 1.609438 * jax.random.uniform(key_list[13], (2, HD, D), jnp.float32) ** steps_of(key_list[13], (2, HD, D), ((1, 4), (2, 8)), -0.2, 0.2)), 52.4288, 262.144),
        "inner_weight": bell_draw(key_list[14], (D, FF), D ** -0.5, 0.25, ((0, 8), (1, 4)), jnp.float32),
        "inner_first": bell_draw(key_list[15], (D, FF), (0.08 * TOKENS ** 0.5), 40.0, ((0, 8), (1, 4)), jnp.float32),
        "inner_second": jnp.clip(jnp.exp(math.log(819.2) - 1.609438 * jax.random.uniform(key_list[16], (D, FF), jnp.float32) ** steps_of(key_list[16], (D, FF), ((0, 8), (1, 4)), -0.2, 0.2)), 163.84, 819.2),
        "outer_weight": bell_draw(key_list[17], (FF, D), (FF // 2) ** -0.5, 0.1875, ((0, 4), (1, 8)), jnp.float32),
        "outer_first": bell_draw(key_list[18], (FF, D), (0.067 * TOKENS ** 0.5), 32.0, ((0, 4), (1, 8)), jnp.float32),
        "outer_second": jnp.clip(jnp.exp(math.log(573.44) - 1.5404451 * jax.random.uniform(key_list[19], (FF, D), jnp.float32) ** steps_of(key_list[19], (FF, D), ((0, 4), (1, 8)), -0.2, 0.2)), 122.88, 573.44),
        "gains": jnp.clip(1.0 + 0.1 * jax.random.normal(key_list[20], (3, D), jnp.float32), 0.5, 1.5),
        "gains_first": bell_draw(key_list[21], (3, D), (0.45 * TOKENS ** 0.5), 256.0, ((1, 8),), jnp.float32),
        "gains_second": jnp.clip(jnp.exp(math.log(26214.4) - 1.609438 * jax.random.uniform(key_list[22], (3, D), jnp.float32) ** steps_of(key_list[22], (3, D), ((1, 8),), -0.2, 0.2)), 5242.88, 26214.4),
        "bias_table": bell_draw(key_list[23], (NB, HEADS), 1.0, 6.0, ((0, 8), (1, 4)), jnp.float32),
        "table_first": bell_draw(key_list[24], (NB, HEADS), (0.8 * TOKENS ** 0.5), 448.0, ((0, 8), (1, 4)), jnp.float32),
        "table_second": jnp.clip(jnp.exp(math.log(81920.0) - 1.609438 * jax.random.uniform(key_list[25], (NB, HEADS), jnp.float32) ** steps_of(key_list[25], (NB, HEADS), ((0, 8), (1, 4)), -0.2, 0.2)), 16384.0, 81920.0),
    }


@jax.custom_vjp
def low(v):
    return lax.optimization_barrier(v.astype(jnp.bfloat16)).astype(jnp.float32)

@jax.custom_vjp
def low_back(v):
    return v

def low_keep(v):
    return (low(v), None)

def low_pass(kept, grad):
    return (grad,)

def back_keep(v):
    return (v, None)

def back_low(kept, grad):
    return (low(grad),)
low.defvjp(low_keep, low_pass)
low_back.defvjp(back_keep, back_low)
norm_eps = 1e-06
beta_first = 0.9
beta_second = 0.95
adam_eps = 1e-08
decay_weight = 0.1
rate_factor = 0.6
masked_value = -1000000000.0
bucket_edges = tuple((math.ceil(16 * 8 ** (number / 16)) for number in range(1, 16)))
step_decays = (decay_weight, decay_weight, decay_weight, decay_weight, decay_weight, 0.0, 0.0)
highest = lax.Precision.HIGHEST

def bucket_onehot(length):
    places = jnp.arange(length, dtype=jnp.int32)
    distance = jnp.maximum(places[:, None] - places[None, :], 0)
    bucket = jnp.minimum(distance, 16)
    for edge_value in bucket_edges:
        bucket = bucket + (distance >= edge_value).astype(jnp.int32)
    return (bucket[:, :, None] == jnp.arange(NB, dtype=jnp.int32)[None, None, :]).astype(jnp.float32)

def root_norm(values, gain_vector):
    return values * lax.rsqrt(lax.optimization_barrier(jnp.mean(values * values, axis=-1, keepdims=True)) + norm_eps) * gain_vector

def spread(normed):
    return jnp.broadcast_to(normed, (N_MP,) + normed.shape)

def project(shared, weight):
    grouped = weight.reshape(weight.shape[0], N_MP, HEADS // N_MP, HEAD_DIM)
    return low(low_back(jnp.einsum('gbtd,dghe->gbthe', shared, grouped, precision=highest)))

def project_encoder(encoder, weight):
    grouped = weight.reshape(weight.shape[0], N_MP, HEADS // N_MP, HEAD_DIM)
    return low(low_back(jnp.einsum('btd,dghe->gbthe', encoder, grouped, precision=highest)))

def attend(queries, key_rows, values, score_bias, allowed):
    scores = low_back(jnp.einsum('gbqhe,gbkhe->gbhqk', queries, key_rows, precision=highest))
    logits = jnp.where(allowed, scores + score_bias, masked_value)
    row_peak = lax.optimization_barrier(jnp.max(logits, axis=-1, keepdims=True))
    exp_terms = jnp.exp(logits - row_peak)
    attn_probs = low(exp_terms / lax.optimization_barrier(jnp.sum(exp_terms, axis=-1, keepdims=True)))
    return low(low_back(jnp.einsum('gbhqk,gbkhe->gbqhe', attn_probs, values, precision=highest)))

def merge_heads(attn_mixed, weight):
    grouped = weight.reshape(N_MP, HEADS // N_MP, HEAD_DIM, weight.shape[1])
    partial_value = jnp.einsum('gbthe,ghed->gbtd', attn_mixed, grouped, precision=highest)
    return low_back(lax.optimization_barrier(jnp.sum(partial_value, axis=0)))

def layer(inputs, encoder, target_segments, encoder_segments, params):
    query_low, keyval_low, output_low, inner_low, outer_low, gain_low, table_low = [low(weight_item) for weight_item in params]
    length = inputs.shape[1]
    score_bias = jnp.einsum('qkb,bn->nqk', bucket_onehot(length), table_low, precision=highest)
    score_bias = score_bias.reshape(N_MP, 1, HEADS // N_MP, length, length)
    places = jnp.arange(length)
    causal = places[:, None] >= places[None, :]
    same_target = target_segments[:, :, None] == target_segments[:, None, :]
    self_allowed = (causal[None] & same_target)[None, :, None]
    cross_allowed = (target_segments[:, :, None] == encoder_segments[:, None, :])[None, :, None]
    shared = spread(low(root_norm(inputs, gain_low[0])))
    attn_mixed = attend(project(shared, query_low[0]), project(shared, keyval_low[0, 0]), project(shared, keyval_low[0, 1]), score_bias, self_allowed)
    after_self = inputs + merge_heads(attn_mixed, output_low[0])
    shared = spread(low(root_norm(after_self, gain_low[1])))
    attn_mixed = attend(project(shared, query_low[1]), project_encoder(encoder, keyval_low[1, 0]), project_encoder(encoder, keyval_low[1, 1]), 0.0, cross_allowed)
    after_cross = after_self + merge_heads(attn_mixed, output_low[1])
    shared = spread(low(root_norm(after_cross, gain_low[2])))
    before = low_back(jnp.einsum('gbtd,dgc->gbtc', shared, inner_low.reshape(D, N_MP, -1), precision=highest))
    hidden = low(jax.nn.gelu(before, approximate=True))
    partial_value = jnp.einsum('gbtc,gcd->gbtd', hidden, outer_low.reshape(N_MP, -1, D), precision=highest)
    return after_cross + low_back(lax.optimization_barrier(jnp.sum(partial_value, axis=0)))

def adam_step(weight, first, second, grad, rate, decay):
    new_first = beta_first * first + (1.0 - beta_first) * grad
    new_second = beta_second * second + (1.0 - beta_second) * grad * grad
    ratio = new_first / (1.0 - beta_first ** STEP) / (jnp.sqrt(new_second / (1.0 - beta_second ** STEP)) + adam_eps)
    return (new_first, new_second, weight - rate * (ratio + decay * weight))

def step_rates():
    return (rate_factor * (16 * D) ** (-0.5), rate_factor * D ** (-0.5), rate_factor * (HD // 8) ** (-0.5), rate_factor * D ** (-0.5), rate_factor * (FF // 2) ** (-0.5), rate_factor, rate_factor)

def reference(inputs, encoder, cotangent, target_segments, encoder_segments, query_weight, query_first, query_second, keyval_weight, keyval_first, keyval_second, output_weight, output_first, output_second, inner_weight, inner_first, inner_second, outer_weight, outer_first, outer_second, gains, gains_first, gains_second, bias_table, table_first, table_second):
    params = (query_weight, keyval_weight, output_weight, inner_weight, outer_weight, gains, bias_table)
    firsts = (query_first, keyval_first, output_first, inner_first, outer_first, gains_first, table_first)
    seconds = (query_second, keyval_second, output_second, inner_second, outer_second, gains_second, table_second)
    per_block = min(SEQS, max(1, 4096 // LT))

    def shaped(tensor):
        return tensor.reshape((SEQS // per_block, per_block) + tensor.shape[1:])

    def one_block(totals, slices):
        block_inputs, block_encoder, block_cotangent, block_targets, block_sources = slices

        def forward(inputs_full, params_full):
            return layer(inputs_full, block_encoder.astype(jnp.float32), block_targets, block_sources, params_full)
        result, pullback = jax.vjp(forward, block_inputs.astype(jnp.float32), params)
        grad_inputs, param_grads = pullback(block_cotangent.astype(jnp.float32))
        return (jax.tree.map(jnp.add, totals, param_grads), (result.astype(jnp.bfloat16), grad_inputs.astype(jnp.bfloat16)))
    slices = (shaped(inputs), shaped(encoder), shaped(cotangent), shaped(target_segments), shaped(encoder_segments))
    totals, stacked = lax.scan(one_block, jax.tree.map(jnp.zeros_like, params), slices)
    outputs = stacked[0].reshape(SEQS, LT, D)
    input_grad = stacked[1].reshape(SEQS, LT, D)
    updated = [adam_step(*param_entry) for param_entry in zip(params, firsts, seconds, totals, step_rates(), step_decays)]
    return (outputs, input_grad, updated[0][0], updated[0][1], updated[0][2], updated[1][0], updated[1][1], updated[1][2], updated[2][0], updated[2][1], updated[2][2], updated[3][0], updated[3][1], updated[3][2], updated[4][0], updated[4][1], updated[4][2], updated[5][0], updated[5][1], updated[5][2], updated[6][0], updated[6][1], updated[6][2])
```

```python
import functools
import math

import jax
import jax.numpy as jnp
from jax import lax
from jax.experimental import pallas as pl
from jax.experimental.pallas import tpu as pltpu
from jax.sharding import PartitionSpec as P

D = 512
HEADS = 8
HEAD_DIM = 64
FF = 2048
NB = 32
HD = 512
STEP = 10
PAIRS = HEADS // 2
PAIR = 2 * HEAD_DIM
HIDDEN = FF // PAIRS
EXTRA = 16
VMEM_BYTES = 56 * 1024 * 1024

norm_eps = 1e-06
beta_first = 0.9
beta_second = 0.95
adam_eps = 1e-08
decay_weight = 0.1
rate_factor = 0.6
masked_value = -1000000000.0
bucket_edges = tuple((math.ceil(16 * 8 ** (number / 16)) for number in range(1, 16)))
step_decays = (decay_weight, decay_weight, decay_weight, decay_weight, decay_weight, 0.0, 0.0)
gelu_slope = math.sqrt(2.0 / math.pi)
gelu_cubic = 0.044715

f32 = jnp.float32
bf16 = jnp.bfloat16
ALL = ("dp", "mp")
VM = pltpu.VMEM


def dot_nn(a, b):
    return lax.dot_general(a, b, (((1,), (0,)), ((), ())), preferred_element_type=f32)


def dot_nt(a, b):
    return lax.dot_general(a, b, (((1,), (1,)), ((), ())), preferred_element_type=f32)


def dot_tn(a, b):
    return lax.dot_general(a, b, (((0,), (0,)), ((), ())), preferred_element_type=f32)


def root_scale(values):
    return lax.rsqrt(jnp.mean(values * values, axis=-1, keepdims=True) + norm_eps)


def root_back(values, gain, grad):
    scale = root_scale(values)
    grad_gain = jnp.sum(grad * values * scale, axis=0, keepdims=True)
    weighted = grad * gain
    along = jnp.sum(weighted * values, axis=-1, keepdims=True)
    inverse = 1.0 / values.shape[-1]
    return scale * weighted - values * (scale * scale * scale * along * inverse), grad_gain


def stack_heads(pair):
    lane = lax.broadcasted_iota(jnp.int32, pair.shape, 1)
    zero = jnp.zeros_like(pair)
    return jnp.concatenate(
        (jnp.where(lane < HEAD_DIM, pair, zero), jnp.where(lane >= HEAD_DIM, pair, zero)), axis=0
    )


def unstack_heads(stacked):
    half = stacked.shape[0] // 2
    top, bottom = stacked[:half], stacked[half:]
    lane = lax.broadcasted_iota(jnp.int32, top.shape, 1)
    return jnp.where(lane < HEAD_DIM, top, bottom)


def column_of(row):
    return jnp.transpose(jnp.broadcast_to(row, (128, row.shape[1])))


def doubled(mask_value):
    return jnp.concatenate((mask_value, mask_value), axis=1)


def attend(query, key, value, bias, allowed):
    scores = dot_nt(key, stack_heads(query))
    if bias is not None:
        scores = scores + bias
    scores = jnp.where(allowed, scores, masked_value)
    peak = jnp.max(scores, axis=0, keepdims=True)
    terms = jnp.exp(scores - peak)
    total = jnp.sum(terms, axis=0, keepdims=True)
    probs = (terms * (1.0 / total)).astype(bf16)
    mixed = unstack_heads(dot_tn(probs, value))
    return mixed.astype(bf16), peak + jnp.log(total)


def attend_back(query, key, value, bias, allowed, log_total, grad_mixed):
    query_stack, grad_stack = stack_heads(query), stack_heads(grad_mixed)
    scores = dot_nt(key, query_stack)
    if bias is not None:
        scores = scores + bias
    scores = jnp.where(allowed, scores, masked_value)
    probs = jnp.exp(scores - log_total)
    grad_probs = dot_nt(value, grad_stack)
    grad_value = dot_nn(probs.astype(bf16), grad_stack)
    along = jnp.sum(grad_probs * probs, axis=0, keepdims=True)
    grad_scores = probs * (grad_probs - along)
    low_scores = grad_scores.astype(bf16)
    grad_key = dot_nn(low_scores, query_stack)
    grad_query = unstack_heads(dot_tn(low_scores, key))
    return (
        grad_query.astype(bf16),
        grad_key.astype(bf16),
        grad_value.astype(bf16),
        grad_scores,
    )


def weight_copies(slots, weights, tab, sems):
    copies = []
    for number, slot in enumerate(slots):
        rows = weights.shape[1] // len(slots)
        start = pl.multiple_of(tab[number] * rows, rows)
        copies.append(
            pltpu.make_async_copy(
                slot.at[:, pl.ds(0, rows), :], weights.at[:, pl.ds(start, rows), :], sems.at[number]
            )
        )
    return copies


def extra_copies(slots, extras, rows, sems):
    return [
        pltpu.make_async_copy(slot.at[:, pl.ds(rows, EXTRA), :], extras.at[number], sems.at[number])
        for number, slot in enumerate(slots)
    ]


def permute_rows(source, target, tab, n_slots):
    rows = source.shape[0] // n_slots
    for number in range(n_slots):
        start = pl.multiple_of(tab[number] * rows, rows)
        target[number * rows : (number + 1) * rows, :] = source[pl.ds(start, rows), :]


def slot_part(outs, number):
    for out in outs:
        if number < out.shape[0]:
            return out, number
        number -= out.shape[0]
    raise ValueError


def write_slots(outs, n_slots, pair, grad):
    rows = grad.shape[0] // n_slots
    low = grad.astype(bf16)
    for number in range(n_slots):
        out, place = slot_part(outs, number)
        out[place, pair, 0:rows, :] = low[number * rows : (number + 1) * rows]


def toeplitz(row, length):
    return pltpu.roll(jnp.broadcast_to(row, (length, row.shape[1])), 0, 1, stride=1, stride_axis=0)


def bias_of(tab, falls, pair, length):
    head = tab[16 + pair] * 2
    return jnp.concatenate(
        [toeplitz(falls[pl.ds(head + side, 1), :], length) for side in range(2)], axis=1
    )


def fold_diagonals(grad):
    length = grad.shape[1]
    folded = grad[0:8]
    for start in range(8, grad.shape[0], 8):
        folded = folded + pltpu.roll(grad[start : start + 8], length - start, 1)
    row = lax.broadcasted_iota(jnp.int32, folded.shape, 0)
    for bit in (1, 2, 4):
        folded = jnp.where(row & bit != 0, pltpu.roll(folded, length - bit, 1), folded)
    return jnp.sum(folded, axis=0, keepdims=True)


def self_masks(tab, targets, row, length):
    segments = targets[pl.ds(tab[24] + row, 1), :].astype(f32)
    column = column_of(segments)
    keys = lax.broadcasted_iota(jnp.int32, (length, length), 0)
    queries = lax.broadcasted_iota(jnp.int32, (length, length), 1)
    return doubled(
        jnp.where((column == segments) & (queries >= keys), 1.0, 0.0)
    ) > 0.5


def cross_masks(tab, targets, sources, row, n_pieces, piece_tab):
    segments = targets[pl.ds(tab[24] + row, 1), :].astype(f32)
    width = sources.shape[1] // n_pieces
    chosen = lax.broadcasted_iota(jnp.int32, (sources.shape[0], width), 0) == tab[24] + row
    parts = []
    for i in range(n_pieces):
        start = pl.multiple_of(tab[piece_tab + i] * width, 128)
        slab = sources[:, pl.ds(start, width)].astype(f32)
        parts.append(jnp.sum(jnp.where(chosen, slab, 0.0), axis=0, keepdims=True))
    column = column_of(jnp.concatenate(parts, axis=1) if n_pieces > 1 else parts[0])
    return doubled(jnp.where(column == segments, 1.0, 0.0)) > 0.5


def self_forward_kernel(n_slots, rows_held, tab, targets, onehot, x_all, *refs):
    slots, refs = refs[:n_slots], refs[n_slots:]
    after, normed, query, key, value, mixed, totals, gains, falls = refs[:9]
    weights, extras, x_rows, sems, extra_sems, x_sem = refs[9:]
    length = x_all.shape[1]
    fetch_x = pltpu.make_async_copy(x_all.at[pl.ds(tab[24], rows_held)], x_rows, x_sem)
    fetch_extra = extra_copies(slots, extras, D // n_slots, extra_sems)
    fetch = weight_copies(slots, weights, tab, sems)
    for copy in [fetch_x] + fetch_extra + fetch:
        copy.start()
    for copy in fetch_extra:
        copy.wait()
    tile = jnp.zeros((EXTRA, D), f32)
    for number in range(n_slots):
        for pair in range(PAIRS):
            tile = tile + extras[number, pair].astype(f32)
    gains[...] = tile[0:8]
    falls[...] = dot_nn(tile[8:16, 0:128].astype(bf16), onehot[...])
    fetch_x.wait()
    resident = x_rows[...].reshape(rows_held * length, D).astype(f32)
    low = (resident * root_scale(resident) * tile[0:1]).astype(bf16)
    normed[...] = low
    for copy in fetch:
        copy.wait()
    for pair in range(PAIRS):
        projected = dot_nn(low, weights[pair, :, 0 : 3 * PAIR]).astype(bf16)
        query[pair] = projected[:, 0:PAIR]
        key[pair] = projected[:, PAIR : 2 * PAIR]
        value[pair] = projected[:, 2 * PAIR :]
    allowed = [self_masks(tab, targets, row, length) for row in range(rows_held)]
    total = resident
    for pair in range(PAIRS):
        bias = bias_of(tab, falls, pair, length)
        for row in range(rows_held):
            span = slice(row * length, (row + 1) * length)
            mix, log_total = attend(
                query[pair, span], key[pair, span], value[pair, span], bias, allowed[row]
            )
            mixed[pair, span] = mix
            totals[pair, row : row + 1, :] = log_total
        total = total + dot_nt(mixed[pair], weights[pair, :, 3 * PAIR :])
    after[...] = total


def encoder_copies(pieces, encoder, tab, rows_held, sems):
    width = encoder.shape[1] // len(pieces)
    copies = []
    for number, piece in enumerate(pieces):
        start = tab[24] if piece.shape[0] > rows_held else 0
        copies.append(
            pltpu.make_async_copy(
                piece.at[pl.ds(start, rows_held)],
                encoder.at[:, pl.ds(number * width, width), :],
                sems.at[number],
            )
        )
    return copies


def cross_forward_kernel(n_slots, n_pieces, rows_held, tab, targets, sources, gains, before, *refs):
    slots, pieces, refs = refs[:n_slots], refs[n_slots : n_slots + n_pieces], refs[n_slots + n_pieces :]
    after, normed, query, key, value, mixed, totals, encoder = refs[:8]
    weights, sems, piece_sems = refs[8:]
    length = before.shape[0] // rows_held
    source_length = sources.shape[1]
    fetch_pieces = encoder_copies(pieces, encoder, tab, rows_held, piece_sems)
    fetch = weight_copies(slots, weights, tab, sems)
    for copy in fetch_pieces + fetch:
        copy.start()
    resident = before[...]
    low = (resident * root_scale(resident) * gains[1:2]).astype(bf16)
    normed[...] = low
    allowed = [
        cross_masks(tab, targets, sources, row, n_pieces, 16 if n_pieces > 1 else 25)
        for row in range(rows_held)
    ]
    for copy in fetch_pieces + fetch:
        copy.wait()
    source = encoder[...].reshape(rows_held * source_length, D)
    total = resident
    for pair in range(PAIRS):
        query[pair] = dot_nn(low, weights[pair, :, 0:PAIR]).astype(bf16)
        projected = dot_nn(source, weights[pair, :, PAIR : 3 * PAIR]).astype(bf16)
        key[pair] = projected[:, 0:PAIR]
        value[pair] = projected[:, PAIR:]
        for row in range(rows_held):
            span = slice(row * length, (row + 1) * length)
            wide = slice(row * source_length, (row + 1) * source_length)
            mix, log_total = attend(
                query[pair, span], key[pair, wide], value[pair, wide], None, allowed[row]
            )
            mixed[pair, span] = mix
            totals[pair, row : row + 1, :] = log_total
        total = total + dot_nt(mixed[pair], weights[pair, :, 3 * PAIR :])
    after[...] = total


def feed_kernel(n_slots, n_outs, rows_held, tab, gains, before, c_all, *refs):
    slots, refs = refs[:n_slots], refs[n_slots:]
    low_out, grad_before, grad_gain = refs[:3]
    outs, refs = refs[3 : 3 + n_outs], refs[3 + n_outs :]
    weights, c_rows, turned, normed_turned, c_turned, sems, c_sem = refs
    fetch_c = pltpu.make_async_copy(c_all.at[pl.ds(tab[24], rows_held)], c_rows, c_sem)
    fetch = weight_copies(slots, weights, tab, sems)
    fetch_c.start()
    for copy in fetch:
        copy.start()
    resident = before[...]
    gain = gains[2:3]
    low = (resident * root_scale(resident) * gain).astype(bf16)
    turned[...] = jnp.transpose(low)
    permute_rows(turned, normed_turned, tab, n_slots)
    fetch_c.wait()
    cotangent = c_rows[...].reshape(resident.shape)
    turned[...] = jnp.transpose(cotangent)
    permute_rows(turned, c_turned, tab, n_slots)
    for copy in fetch:
        copy.wait()
    total = resident
    grad_normed = jnp.zeros_like(resident)
    for pair in range(PAIRS):
        inner, outer = weights[pair, :, 0:HIDDEN], weights[pair, :, HIDDEN:]
        u = dot_nn(low, inner)
        squared = u * u
        bent = jnp.tanh(gelu_slope * (u + gelu_cubic * u * squared))
        hidden = (0.5 * u * (1.0 + bent)).astype(bf16)
        slope = 0.5 * (1.0 + bent) + 0.5 * u * (1.0 - bent * bent) * gelu_slope * (
            1.0 + 3.0 * gelu_cubic * squared
        )
        total = total + dot_nt(hidden, outer)
        grad_u = (dot_nn(cotangent, outer) * slope).astype(bf16)
        grad_normed = grad_normed + dot_nt(grad_u, inner)
        write_slots(
            outs,
            n_slots,
            pair,
            jnp.concatenate(
                (dot_nn(normed_turned[...], grad_u), dot_nn(c_turned[...], hidden)), axis=1
            ),
        )
    low_out[...] = total.astype(bf16)
    through, gain_part = root_back(resident, gain, grad_normed)
    grad_before[...] = cotangent.astype(f32) + through
    grad_gain[...] = gain_part


def cross_back_kernel(
    n_slots, n_pieces, n_outs, rows_held, tab, targets, sources, gains, grad_after, before, *refs
):
    normed, query, key, value, mixed, totals, encoder = refs[:7]
    slots, refs = refs[7 : 7 + n_slots], refs[7 + n_slots :]
    grad_before, grad_gain = refs[:2]
    outs, refs = refs[2 : 2 + n_outs], refs[2 + n_outs :]
    weights, turned, low_turned, normed_turned, wide_turned, encoder_turned, d_key, d_value, sems = refs
    length = before.shape[0] // rows_held
    source_length = sources.shape[1]
    fetch = weight_copies(slots, weights, tab, sems)
    for copy in fetch:
        copy.start()
    grad_in = grad_after[...]
    low = grad_in.astype(bf16)
    turned[...] = jnp.transpose(low)
    permute_rows(turned, low_turned, tab, n_slots)
    turned[...] = jnp.transpose(normed[...])
    permute_rows(turned, normed_turned, tab, n_slots)
    wide_turned[...] = jnp.transpose(encoder[...].reshape(rows_held * source_length, D))
    permute_rows(wide_turned, encoder_turned, tab, n_slots)
    allowed = [
        cross_masks(tab, targets, sources, row, n_pieces, 16 if n_pieces > 1 else 25)
        for row in range(rows_held)
    ]
    for copy in fetch:
        copy.wait()
    grad_normed = jnp.zeros_like(grad_in)
    for pair in range(PAIRS):
        grad_mixed = dot_nn(low, weights[pair, :, 3 * PAIR :]).astype(bf16)
        d_queries = []
        for row in range(rows_held):
            span = slice(row * length, (row + 1) * length)
            wide = slice(row * source_length, (row + 1) * source_length)
            d_query, d_key[wide], d_value[wide], _ = attend_back(
                query[pair, span],
                key[pair, wide],
                value[pair, wide],
                None,
                allowed[row],
                totals[pair, row : row + 1, :],
                grad_mixed[span],
            )
            d_queries.append(d_query)
        d_query = jnp.concatenate(d_queries, axis=0) if rows_held > 1 else d_queries[0]
        grad_normed = grad_normed + dot_nt(d_query, weights[pair, :, 0:PAIR])
        write_slots(
            outs,
            n_slots,
            pair,
            jnp.concatenate(
                (
                    dot_nn(normed_turned[...], d_query),
                    dot_nn(encoder_turned[...], d_key[...]),
                    dot_nn(encoder_turned[...], d_value[...]),
                    dot_nn(low_turned[...], mixed[pair]),
                ),
                axis=1,
            ),
        )
    through, gain_part = root_back(before[...], gains[1:2], grad_normed)
    grad_before[...] = grad_in + through
    grad_gain[...] = gain_part


def self_back_kernel(
    n_slots, n_outs, rows_held, tab, targets, onehot, gains, falls, gain_two, gain_three, grad_after, x_all, *refs
):
    normed, query, key, value, mixed, totals = refs[:6]
    slots, refs = refs[6 : 6 + n_slots], refs[6 + n_slots :]
    low_grad = refs[0]
    outs, refs = refs[1 : 1 + n_outs], refs[1 + n_outs :]
    weights, x_rows, turned, low_turned, normed_turned, bias_rows, sems, x_sem = refs
    length = x_all.shape[1]
    fetch_x = pltpu.make_async_copy(x_all.at[pl.ds(tab[24], rows_held)], x_rows, x_sem)
    fetch = weight_copies(slots, weights, tab, sems)
    for copy in fetch + [fetch_x]:
        copy.start()
    grad_in = grad_after[...]
    low = grad_in.astype(bf16)
    turned[...] = jnp.transpose(low)
    permute_rows(turned, low_turned, tab, n_slots)
    turned[...] = jnp.transpose(normed[...])
    permute_rows(turned, normed_turned, tab, n_slots)
    allowed = [self_masks(tab, targets, row, length) for row in range(rows_held)]
    for copy in fetch:
        copy.wait()
    grad_normed = jnp.zeros_like(grad_in)
    for pair in range(PAIRS):
        bias = bias_of(tab, falls, pair, length)
        grad_mixed = dot_nn(low, weights[pair, :, 3 * PAIR :]).astype(bf16)
        parts = []
        grad_bias = jnp.zeros((length, 2 * length), f32)
        for row in range(rows_held):
            span = slice(row * length, (row + 1) * length)
            d_query, d_key, d_value, grad_scores = attend_back(
                query[pair, span],
                key[pair, span],
                value[pair, span],
                bias,
                allowed[row],
                totals[pair, row : row + 1, :],
                grad_mixed[span],
            )
            parts.append(jnp.concatenate((d_query, d_key, d_value), axis=1))
            grad_bias = grad_bias + grad_scores
        for side in range(2):
            diagonal = fold_diagonals(grad_bias[:, side * length : (side + 1) * length])
            bias_rows[pl.ds(tab[16 + pair] * 2 + side, 1), :] = diagonal
        joined = jnp.concatenate(parts, axis=0) if rows_held > 1 else parts[0]
        grad_normed = grad_normed + dot_nt(joined, weights[pair, :, 0 : 3 * PAIR])
        write_slots(
            outs,
            n_slots,
            pair,
            jnp.concatenate(
                (dot_nn(normed_turned[...], joined), dot_nn(low_turned[...], mixed[pair])), axis=1
            ),
        )
    fetch_x.wait()
    resident = x_rows[...].reshape(grad_in.shape).astype(f32)
    through, gain_one = root_back(resident, gains[0:1], grad_normed)
    low_grad[...] = (grad_in + through).astype(bf16)
    table = lax.dot_general(
        bias_rows[...],
        onehot[...].astype(f32),
        (((1,), (1,)), ((), ())),
        precision=lax.Precision.HIGHEST,
        preferred_element_type=f32,
    )
    blank = jnp.zeros((5, D), f32)
    table = jnp.concatenate((table, jnp.zeros((8, D - 128), f32)), axis=1)
    tile = jnp.concatenate((gain_one, gain_two[...], gain_three[...], blank, table), axis=0).astype(bf16)
    rows = D // n_slots
    for number in range(n_slots):
        out, place = slot_part(outs, number)
        for pair in range(PAIRS):
            out[place, pair, rows : rows + EXTRA, :] = tile


def pack_kernel(query, keyval, output, inner, outer, tile, own_self, own_cross, own_feed):
    rows = query.shape[1]
    for number, own in enumerate((own_self, own_cross)):
        parts = (query[number], keyval[number, 0], keyval[number, 1], output[number])
        own[0:rows, :] = jnp.concatenate(parts, axis=1).astype(bf16)
    own_self[rows : rows + EXTRA, :] = tile[...].astype(bf16)
    own_feed[...] = jnp.concatenate((inner[...], outer[...]), axis=1).astype(bf16)


def spread_kernel(rows_held, tab, *refs):
    pieces, out = refs[:-1], refs[-1]
    for number, piece in enumerate(pieces):
        out[pl.ds(tab[16 + number] * rows_held, rows_held)] = piece[...]


def shape(dims, dtype):
    return jax.ShapeDtypeStruct(dims, dtype)


def dma_sems(count):
    return pltpu.SemaphoreType.DMA((count,))


def call(kernel, operands, outs, scratch, flops=0):
    spaces = {"smem": pltpu.SMEM, "vmem": pltpu.VMEM, "any": pl.ANY}
    arrays = [array for array, _ in operands]
    moved = sum(a.size * a.dtype.itemsize for a in arrays) + sum(
        math.prod(o.shape) * o.dtype.itemsize for o in outs
    )
    return pl.pallas_call(
        kernel,
        out_shape=tuple(outs),
        in_specs=[pl.BlockSpec(memory_space=spaces[place]) for _, place in operands],
        out_specs=tuple(pl.BlockSpec(memory_space=pltpu.VMEM) for _ in outs),
        scratch_shapes=scratch,
        compiler_params=pltpu.CompilerParams(vmem_limit_bytes=VMEM_BYTES),
        cost_estimate=pl.CostEstimate(flops=flops, bytes_accessed=moved, transcendentals=0),
    )(*arrays)


def bucket_onehot(length):
    distance = jnp.arange(length, dtype=jnp.int32)
    bucket = jnp.minimum(distance, 16)
    for edge_value in bucket_edges:
        bucket = bucket + (distance >= edge_value).astype(jnp.int32)
    return (jnp.arange(128, dtype=jnp.int32)[:, None] == bucket[None, :]).astype(bf16)


def adam_step(weight, first, second, grad, rate, decay):
    new_first = beta_first * first + (1.0 - beta_first) * grad
    new_second = beta_second * second + (1.0 - beta_second) * grad * grad
    ratio = (
        new_first
        / (1.0 - beta_first**STEP)
        / (jnp.sqrt(new_second / (1.0 - beta_second**STEP)) + adam_eps)
    )
    return (new_first, new_second, weight - rate * (ratio + decay * weight))


def step_rates():
    return (
        rate_factor * (16 * D) ** (-0.5),
        rate_factor * D ** (-0.5),
        rate_factor * (HD // 8) ** (-0.5),
        rate_factor * D ** (-0.5),
        rate_factor * (FF // 2) ** (-0.5),
        rate_factor,
        rate_factor,
    )


class TreePlan:
    n_slots = 8
    out_slots = (4, 4)

    def __init__(self, n_dp, n_mp):
        self.n_dp, self.n_mp = n_dp, n_mp

    def pairs(self, target):
        n_mp = self.n_mp
        return [
            (d * n_mp + m, t * n_mp + s)
            for d in range(self.n_dp)
            for m in range(n_mp)
            for t, s in (target(d, m),)
        ]

    def hop_z(self, array, number):
        return lax.ppermute(array, ALL, self.pairs(lambda d, m: (d, m ^ number)))

    def hop_core(self, array):
        return lax.ppermute(array, ALL, self.pairs(lambda d, m: (d ^ 1, m)))

    def hop_first(self, array):
        return lax.ppermute(array, ALL, self.pairs(lambda d, m: (d ^ (4 if d & 1 else 2), m)))

    def hop_second(self, array):
        return lax.ppermute(array, ALL, self.pairs(lambda d, m: (d ^ (2 if d & 1 else 4), m)))

    def table(self, place_dp, place_mp, rows_held):
        core = place_dp & 1
        first, second = 2 + 2 * core, 4 - 2 * core
        own = [place_dp ^ (a * first) ^ (b * second) for b in range(2) for a in range(2)]
        peer = [place_dp ^ 1 ^ (a * second) ^ (b * first) for b in range(2) for a in range(2)]
        return own + peer, [place_mp ^ j for j in range(4)]

    def gather(self, own):
        base = jnp.stack([own] + [self.hop_z(own, number) for number in (1, 2, 3)])
        near, far = self.hop_first(base), self.hop_second(base)
        both = self.hop_second(near)
        slots = [base, near, far, both]
        return slots + [self.hop_core(slot) for slot in slots]

    def reduce(self, parts):
        own, peer = parts
        half = self.hop_core(peer).astype(f32) + own.astype(f32)
        kept = half[0:2] + self.hop_second(half[2:4].astype(bf16)).astype(f32)
        kept = kept[0] + self.hop_first(kept[1].astype(bf16)).astype(f32)
        low = kept.astype(bf16)
        total = kept[0]
        for number in (1, 2, 3):
            total = total + self.hop_z(low[number], number).astype(f32)
        return total, total[D // self.n_dp :]

    def encoder_pieces(self, encoder, place_mp, rows_held):
        sent = [
            self.hop_z(
                lax.dynamic_slice_in_dim(encoder, (place_mp ^ number) * rows_held, rows_held, 0), number
            )
            for number in (1, 2, 3)
        ]
        return [encoder] + sent

    def spread(self, tab, piece, rows_held):
        pieces = [piece] + [self.hop_z(piece, number) for number in (1, 2, 3)]
        out = shape((rows_held * self.n_mp,) + piece.shape[1:], piece.dtype)
        (result,) = call(
            functools.partial(spread_kernel, rows_held),
            [(tab, "smem")] + [(array, "vmem") for array in pieces],
            [out],
            [],
        )
        return result


class PlainPlan:
    n_slots = 1
    out_slots = (1,)

    def __init__(self, n_dp, n_mp):
        self.n_dp, self.n_mp = n_dp, n_mp

    def table(self, place_dp, place_mp, rows_held):
        return [0], [0, 1, 2, 3]

    def gather(self, own):
        rows = D // self.n_dp
        kinds = 4 if own.shape[1] * self.n_mp == 4 * HD else 2
        full = lax.all_gather(own[:rows], ("mp", "dp"), axis=0, tiled=True)
        full = full.reshape(self.n_mp, D, kinds, -1).transpose(2, 1, 0, 3)
        full = full.reshape(kinds, D, PAIRS, -1).transpose(2, 1, 0, 3).reshape(PAIRS, D, -1)
        return [full]

    def reduce(self, parts):
        grads = parts[0][0]
        kinds = 4 if grads.shape[2] == 4 * PAIR else 2
        full = grads[:, :D].reshape(PAIRS, D, kinds, -1).transpose(2, 1, 0, 3)
        full = full.reshape(kinds, D, self.n_mp, -1).transpose(2, 1, 0, 3)
        total = lax.psum_scatter(
            full.reshape(self.n_mp * D, -1), ("mp", "dp"), scatter_dimension=0, tiled=True
        ).astype(f32)
        return total, lax.psum(grads[0, D:].astype(f32), ALL) if grads.shape[1] > D else None

    def encoder_pieces(self, encoder, place_mp, rows_held):
        return [lax.all_to_all(encoder, "mp", split_axis=0, concat_axis=1, tiled=True)]

    def spread(self, tab, piece, rows_held):
        return lax.all_gather(piece, "mp", axis=0, tiled=True)


def shards(
    plan,
    inputs,
    encoder,
    cotangent,
    target_segments,
    encoder_segments,
    query_weight,
    query_first,
    query_second,
    keyval_weight,
    keyval_first,
    keyval_second,
    output_weight,
    output_first,
    output_second,
    inner_weight,
    inner_first,
    inner_second,
    outer_weight,
    outer_first,
    outer_second,
    gains,
    gains_first,
    gains_second,
    bias_table,
    table_first,
    table_second,
):
    n_slots, out_slots = plan.n_slots, plan.out_slots
    n_outs = len(out_slots)
    seq_count, length, _ = inputs.shape
    source_length = encoder_segments.shape[1]
    rows_held = seq_count // plan.n_mp
    tokens, sources = rows_held * length, rows_held * source_length
    place_dp, place_mp = lax.axis_index("dp"), lax.axis_index("mp")
    slot_table, pair_table = plan.table(place_dp, place_mp, rows_held)
    entries = slot_table + [0] * (16 - len(slot_table)) + pair_table + [0] * 4
    entries = entries + [place_mp * rows_held] + [0] * 7
    tab = jnp.stack([jnp.asarray(entry, jnp.int32) for entry in entries])
    onehot = bucket_onehot(length)

    width = gains.shape[1]
    lanes = jnp.arange(D, dtype=jnp.int32)
    gain_tile = jnp.where(
        ((lanes // width == place_dp) & (place_mp == 0))[None], jnp.tile(gains, (1, plan.n_dp)), 0.0
    )
    gain_tile = jnp.concatenate((gain_tile, jnp.zeros((5, D), f32)))
    bands, heads = bias_table.shape
    spread_table = jnp.tile(bias_table.T, (plan.n_mp, D // bands))
    head_number = jnp.arange(HEADS, dtype=jnp.int32)[:, None]
    table_tile = jnp.where(
        (head_number // heads == place_mp) & (lanes[None] // bands == place_dp), spread_table, 0.0
    )
    tile = jnp.concatenate((gain_tile, table_tile))
    columns = query_weight.shape[2]
    rows = D // plan.n_dp

    output_turned = output_weight.transpose(0, 2, 1)
    outer_turned = outer_weight.T
    if plan.n_slots == 8:
        own_self, own_cross, own_feed = call(
            pack_kernel,
            [
                (query_weight, "vmem"),
                (keyval_weight, "vmem"),
                (output_turned, "vmem"),
                (inner_weight, "vmem"),
                (outer_turned, "vmem"),
                (tile, "vmem"),
            ],
            [
                shape((rows + EXTRA, D), bf16),
                shape((rows, D), bf16),
                shape((rows, 2 * HIDDEN), bf16),
            ],
            [],
        )
        self_slots = plan.gather(own_self)
    else:
        own_self, own_cross = (
            jnp.concatenate(
                (query_weight[i], keyval_weight[i, 0], keyval_weight[i, 1], output_turned[i]), axis=1
            ).astype(bf16)
            for i in range(2)
        )
        own_feed = jnp.concatenate((inner_weight, outer_turned), axis=1).astype(bf16)
        (self_weights,) = plan.gather(own_self)
        small = lax.psum(tile.astype(bf16).astype(f32), ALL).astype(bf16)[None]
        small = jnp.concatenate((small, jnp.zeros((PAIRS - 1, EXTRA, D), bf16)))
        self_slots = [jnp.concatenate((self_weights, small), axis=1)]
    pieces = plan.encoder_pieces(encoder, place_mp, rows_held)
    cross_slots = plan.gather(own_cross)
    feed_slots = plan.gather(own_feed)
    n_pieces = len(pieces)

    def anys(arrays):
        return [(array, "any") for array in arrays]

    def vmems(arrays):
        return [(array, "vmem") for array in arrays]

    flat = (tokens, D)
    paired = (PAIRS, tokens, PAIR)
    wide = (PAIRS, sources, PAIR)
    stats = shape((PAIRS, rows_held, 2 * length), f32)
    attn_weights = VM((PAIRS, D, 4 * PAIR), bf16)

    after_self, normed_one, q_one, k_one, v_one, mix_one, sum_one, gain_rows, falls = call(
        functools.partial(self_forward_kernel, n_slots, rows_held),
        [(tab, "smem")] + vmems((target_segments, onehot)) + anys([inputs] + list(self_slots)),
        [shape(flat, f32), shape(flat, bf16)]
        + [shape(paired, bf16)] * 4
        + [stats, shape((8, D), f32), shape((8, length), f32)],
        [
            attn_weights,
            VM((n_slots, PAIRS, EXTRA, D), bf16),
            VM((rows_held, length, D), bf16),
            dma_sems(n_slots),
            dma_sems(n_slots),
            pltpu.SemaphoreType.DMA,
        ],
        flops=2 * tokens * D * 2048,
    )
    after_cross, normed_two, q_two, k_two, v_two, mix_two, sum_two, source_rows = call(
        functools.partial(cross_forward_kernel, n_slots, n_pieces, rows_held),
        [(tab, "smem")]
        + vmems((target_segments, encoder_segments, gain_rows, after_self))
        + anys(list(cross_slots) + list(pieces)),
        [
            shape(flat, f32),
            shape(flat, bf16),
            shape(paired, bf16),
            shape(wide, bf16),
            shape(wide, bf16),
            shape(paired, bf16),
            stats,
            shape((rows_held, source_length, D), bf16),
        ],
        [attn_weights, dma_sems(n_slots), dma_sems(n_pieces)],
        flops=2 * tokens * D * 2048 + 2 * sources * D * 1024,
    )

    def grad_outs(extra, width_out):
        return [
            shape((count, PAIRS, D // n_slots + extra, width_out), bf16) for count in out_slots
        ]

    feed_result = call(
        functools.partial(feed_kernel, n_slots, n_outs, rows_held),
        [(tab, "smem")] + vmems((gain_rows, after_cross)) + anys([cotangent] + list(feed_slots)),
        [shape(flat, bf16), shape(flat, f32), shape((1, D), f32)] + grad_outs(0, 2 * HIDDEN),
        [
            VM((PAIRS, D, 2 * HIDDEN), bf16),
            VM((rows_held, length, D), bf16),
            VM((D, tokens), bf16),
            VM((D, tokens), bf16),
            VM((D, tokens), bf16),
            dma_sems(n_slots),
            pltpu.SemaphoreType.DMA,
        ],
        flops=12 * tokens * D * FF,
    )
    low_out, grad_second, gain_three = feed_result[:3]
    grad_feed, _ = plan.reduce(feed_result[3:])
    outputs = plan.spread(tab, low_out.reshape(rows_held, length, D), rows_held)
    cross_result = call(
        functools.partial(cross_back_kernel, n_slots, n_pieces, n_outs, rows_held),
        [(tab, "smem")]
        + vmems(
            (
                target_segments,
                encoder_segments,
                gain_rows,
                grad_second,
                after_self,
                normed_two,
                q_two,
                k_two,
                v_two,
                mix_two,
                sum_two,
                source_rows,
            )
        )
        + anys(cross_slots),
        [shape(flat, f32), shape((1, D), f32)] + grad_outs(0, 4 * PAIR),
        [
            attn_weights,
            VM((D, tokens), bf16),
            VM((D, tokens), bf16),
            VM((D, tokens), bf16),
            VM((D, sources), bf16),
            VM((D, sources), bf16),
            VM((sources, PAIR), bf16),
            VM((sources, PAIR), bf16),
            dma_sems(n_slots),
        ],
        flops=4 * tokens * D * 2048 + 4 * sources * D * 1024,
    )
    grad_first, gain_two = cross_result[:2]
    grad_cross, _ = plan.reduce(cross_result[2:])
    self_result = call(
        functools.partial(self_back_kernel, n_slots, n_outs, rows_held),
        [(tab, "smem")]
        + vmems((target_segments, onehot, gain_rows, falls, gain_two, gain_three, grad_first))
        + anys([inputs])
        + vmems((normed_one, q_one, k_one, v_one, mix_one, sum_one))
        + anys(self_slots),
        [shape(flat, bf16)] + grad_outs(EXTRA, 4 * PAIR),
        [
            attn_weights,
            VM((rows_held, length, D), bf16),
            VM((D, tokens), bf16),
            VM((D, tokens), bf16),
            VM((D, tokens), bf16),
            VM((8, length), f32),
            dma_sems(n_slots),
            pltpu.SemaphoreType.DMA,
        ],
        flops=4 * tokens * D * 2048,
    )
    grad_self, tile = plan.reduce(self_result[1:])
    input_grad = plan.spread(tab, self_result[0].reshape(rows_held, length, D), rows_held)

    def kind(grads, number):
        return grads[:rows, number * columns : (number + 1) * columns]

    hidden = inner_weight.shape[1]
    grads = (
        jnp.stack((kind(grad_self, 0), kind(grad_cross, 0))),
        jnp.stack(
            (
                jnp.stack((kind(grad_self, 1), kind(grad_self, 2))),
                jnp.stack((kind(grad_cross, 1), kind(grad_cross, 2))),
            )
        ),
        jnp.stack((kind(grad_self, 3).T, kind(grad_cross, 3).T)),
        grad_feed[:, :hidden],
        grad_feed[:, hidden:].T,
        lax.dynamic_slice_in_dim(tile[0:3], place_dp * width, width, 1),
        lax.dynamic_slice(tile, (8 + place_mp * heads, place_dp * bands), (heads, bands)).T,
    )
    params = (
        query_weight,
        keyval_weight,
        output_weight,
        inner_weight,
        outer_weight,
        gains,
        bias_table,
    )
    firsts = (
        query_first,
        keyval_first,
        output_first,
        inner_first,
        outer_first,
        gains_first,
        table_first,
    )
    seconds = (
        query_second,
        keyval_second,
        output_second,
        inner_second,
        outer_second,
        gains_second,
        table_second,
    )
    updated = [
        adam_step(*param_entry)
        for param_entry in zip(params, firsts, seconds, grads, step_rates(), step_decays)
    ]
    return (outputs, input_grad) + tuple(array for triple in updated for array in triple)


def solution(mesh):
    n_dp, n_mp = mesh.shape["dp"], mesh.shape["mp"]
    plan = (TreePlan if (n_dp, n_mp) == (8, 4) else PlainPlan)(n_dp, n_mp)
    by_query, by_keyval = P(None, "dp", "mp"), P(None, None, "dp", "mp")
    by_output, by_inner, by_outer = P(None, "mp", "dp"), P("dp", "mp"), P("mp", "dp")
    weights = (by_query,) * 3 + (by_keyval,) * 3 + (by_output,) * 3 + (by_inner,) * 3
    weights = weights + (by_outer,) * 3 + (P(None, "dp"),) * 3 + (P("dp", "mp"),) * 3
    tokens = P("dp", None, None)
    return jax.shard_map(
        functools.partial(shards, plan),
        mesh=mesh,
        in_specs=(tokens, P("dp", "mp", None), tokens, P("dp", None), P("dp", None)) + weights,
        out_specs=(tokens, tokens) + weights,
        check_vma=False,
    )
```

```python
import functools
import math

import jax
import jax.numpy as jnp
import numpy as np
from jax import lax
from jax.experimental import pallas as pl
from jax.experimental.pallas import tpu as pltpu
from jax.sharding import PartitionSpec as P

D = 512
HEADS = 8
HEAD_DIM = 64
FF = 2048
NB = 32
HD = 512
STEP = 10
PAIRS = HEADS // 2
PAIR = 2 * HEAD_DIM
HIDDEN = FF // PAIRS
EXTRA = 16
GROUPS = tuple((i, i + 1) for i in range(0, PAIRS, 2))
VMEM_BYTES = 56 * 1024 * 1024

norm_eps = 1e-06
beta_first = 0.9
beta_second = 0.95
adam_eps = 1e-08
decay_weight = 0.1
rate_factor = 0.6
masked_value = -1000000000.0
bucket_edges = tuple((math.ceil(16 * 8 ** (number / 16)) for number in range(1, 16)))
step_decays = (decay_weight, decay_weight, decay_weight, decay_weight, decay_weight, 0.0, 0.0)
gelu_slope = math.sqrt(2.0 / math.pi)
gelu_cubic = 0.044715

f32 = jnp.float32
bf16 = jnp.bfloat16
ALL = ("dp", "mp")
VM = pltpu.VMEM


def dot_nn(a, b):
    return lax.dot_general(a, b, (((1,), (0,)), ((), ())), preferred_element_type=f32)


def dot_nt(a, b):
    return lax.dot_general(a, b, (((1,), (1,)), ((), ())), preferred_element_type=f32)


def dot_tn(a, b):
    return lax.dot_general(a, b, (((0,), (0,)), ((), ())), preferred_element_type=f32)


def root_scale(values):
    return lax.rsqrt(jnp.mean(values * values, axis=-1, keepdims=True) + norm_eps)


def root_back(values, gain, grad):
    scale = root_scale(values)
    grad_gain = jnp.sum(grad * values * scale, axis=0, keepdims=True)
    weighted = grad * gain
    along = jnp.sum(weighted * values, axis=-1, keepdims=True)
    inverse = 1.0 / values.shape[-1]
    return scale * weighted - values * (scale * scale * scale * along * inverse), grad_gain


def stack_heads(pair):
    lane = lax.broadcasted_iota(jnp.int32, pair.shape, 1)
    zero = jnp.zeros_like(pair)
    return jnp.concatenate(
        (jnp.where(lane < HEAD_DIM, pair, zero), jnp.where(lane >= HEAD_DIM, pair, zero)), axis=0
    )


def unstack_heads(stacked):
    half = stacked.shape[0] // 2
    top, bottom = stacked[:half], stacked[half:]
    lane = lax.broadcasted_iota(jnp.int32, top.shape, 1)
    return jnp.where(lane < HEAD_DIM, top, bottom)


def column_of(row):
    return jnp.transpose(jnp.broadcast_to(row, (128, row.shape[1])))


def doubled(mask_value):
    return jnp.concatenate((mask_value, mask_value), axis=1)


def masked_scores(units):
    scores = [dot_nt(key, query) for query, key, _, _ in units]
    scores = [s if unit[2] is None else s + unit[2] for s, unit in zip(scores, units)]
    return [jnp.where(unit[3], s, masked_value) for s, unit in zip(scores, units)]


def attend(units):
    scores = masked_scores([(stack_heads(u[0]), u[1], u[3], u[4]) for u in units])
    peaks = [jnp.max(s, axis=0, keepdims=True) for s in scores]
    terms = [jnp.exp(s - peak) for s, peak in zip(scores, peaks)]
    sums = [jnp.sum(t, axis=0, keepdims=True) for t in terms]
    probs = [(t * (1.0 / total)).astype(bf16) for t, total in zip(terms, sums)]
    mixes = [dot_tn(p, u[2]) for p, u in zip(probs, units)]
    mixes = [unstack_heads(m).astype(bf16) for m in mixes]
    return mixes, [peak + jnp.log(total) for peak, total in zip(peaks, sums)]


def attend_back(units):
    queries = [stack_heads(u[0]) for u in units]
    grads = [stack_heads(u[6]) for u in units]
    scores = masked_scores([(q, u[1], u[3], u[4]) for q, u in zip(queries, units)])
    grad_probs = [dot_nt(u[2], g) for u, g in zip(units, grads)]
    probs = [jnp.exp(s - u[5]) for s, u in zip(scores, units)]
    grad_values = [dot_nn(p.astype(bf16), g).astype(bf16) for p, g in zip(probs, grads)]
    along = [jnp.sum(g * p, axis=0, keepdims=True) for g, p in zip(grad_probs, probs)]
    grad_scores = [p * (g - t) for p, g, t in zip(probs, grad_probs, along)]
    low = [g.astype(bf16) for g in grad_scores]
    grad_keys = [dot_nn(x, q).astype(bf16) for x, q in zip(low, queries)]
    grad_queries = [unstack_heads(dot_tn(x, u[1])).astype(bf16) for x, u in zip(low, units)]
    return grad_queries, grad_keys, grad_values, grad_scores


def weight_copies(slots, weights, tab, sems, first=0):
    copies = []
    for pair in range(PAIRS):
        row = []
        for number, slot in enumerate(slots):
            rows = weights.shape[1] // len(slots)
            start = pl.multiple_of(tab[number] * rows, rows)
            row.append(
                pltpu.make_async_copy(
                    slot.at[pair, pl.ds(0, rows), pl.ds(first, weights.shape[2])],
                    weights.at[pair, pl.ds(start, rows), :],
                    sems.at[number, pair],
                )
            )
        copies.append(row)
    for row in copies:
        for copy in row:
            copy.start()
    return copies


def wait_for(copies):
    for copy in copies:
        copy.wait()


def extra_copies(slots, extras, rows, sems):
    return [
        pltpu.make_async_copy(slot.at[:, pl.ds(rows, EXTRA), pl.ds(0, D)], extras.at[number], sems.at[number])
        for number, slot in enumerate(slots)
    ]


def permute_rows(source, target, tab, n_slots):
    rows = source.shape[0] // n_slots
    for number in range(n_slots):
        start = pl.multiple_of(tab[number] * rows, rows)
        target[number * rows : (number + 1) * rows, :] = source[pl.ds(start, rows), :]


class SlotWriter:
    def __init__(self, outs, held, sems):
        self.outs, self.held, self.sems = outs, held, sems
        self.copies = []

    def send(self, pair, first, rows, sem):
        begin = 0
        for place, out in enumerate(self.outs):
            copy = pltpu.make_async_copy(
                self.held.at[pl.ds(begin, out.shape[0]), pair, pl.ds(first, rows), :],
                out.at[:, pair, pl.ds(first, rows), :],
                self.sems.at[place, sem],
            )
            copy.start()
            self.copies.append(copy)
            begin += out.shape[0]

    def write(self, pair, grads):
        n_slots = self.held.shape[0]
        first = 0
        for grad in grads:
            rows, width = grad.shape[0] // n_slots, grad.shape[1]
            low = grad.astype(bf16)
            for number in range(n_slots):
                part = low[number * rows : (number + 1) * rows]
                self.held[number, pair, 0:rows, first : first + width] = part
            first += width
        self.send(pair, 0, rows, pair)

    def finish(self):
        wait_for(self.copies)


def toeplitz(row, length):
    return pltpu.roll(jnp.broadcast_to(row, (length, row.shape[1])), 0, 1, stride=1, stride_axis=0)


def bias_of(tab, falls, pair, length):
    head = tab[16 + pair] * 2
    return jnp.concatenate(
        [toeplitz(falls[pl.ds(head + side, 1), :], length) for side in range(2)], axis=1
    )


def fold_diagonals(grad):
    length = grad.shape[1]
    folded = grad[0:8]
    for start in range(8, grad.shape[0], 8):
        folded = folded + pltpu.roll(grad[start : start + 8], length - start, 1)
    row = lax.broadcasted_iota(jnp.int32, folded.shape, 0)
    for bit in (1, 2, 4):
        folded = jnp.where(row & bit != 0, pltpu.roll(folded, length - bit, 1), folded)
    return jnp.sum(folded, axis=0, keepdims=True)


def self_masks(tab, targets, row, length):
    segments = targets[pl.ds(tab[24] + row, 1), :].astype(f32)
    column = column_of(segments)
    keys = lax.broadcasted_iota(jnp.int32, (length, length), 0)
    queries = lax.broadcasted_iota(jnp.int32, (length, length), 1)
    return doubled(
        jnp.where((column == segments) & (queries >= keys), 1.0, 0.0)
    ) > 0.5


def cross_masks(tab, targets, sources, row, n_pieces, piece_tab):
    segments = targets[pl.ds(tab[24] + row, 1), :].astype(f32)
    width = sources.shape[1] // n_pieces
    chosen = lax.broadcasted_iota(jnp.int32, (sources.shape[0], width), 0) == tab[24] + row
    parts = []
    for i in range(n_pieces):
        start = pl.multiple_of(tab[piece_tab + i] * width, 128)
        slab = sources[:, pl.ds(start, width)].astype(f32)
        parts.append(jnp.sum(jnp.where(chosen, slab, 0.0), axis=0, keepdims=True))
    column = column_of(jnp.concatenate(parts, axis=1) if n_pieces > 1 else parts[0])
    return doubled(jnp.where(column == segments, 1.0, 0.0)) > 0.5


def self_forward_kernel(n_slots, n_after, rows_held, tab, targets, onehot, x_all, *refs):
    slots, refs = refs[:n_slots], refs[n_slots + n_after :]
    after, normed, query, key, value, mixed, totals, gains, falls = refs[:9]
    weights, extras, x_rows, sems, extra_sems, x_sem = refs[9:]
    length = x_all.shape[1]
    fetch_x = pltpu.make_async_copy(x_all.at[pl.ds(tab[24], rows_held)], x_rows, x_sem)
    fetch_extra = extra_copies(slots, extras, D // n_slots, extra_sems)
    for copy in [fetch_x] + fetch_extra:
        copy.start()
    fetch = weight_copies(slots, weights, tab, sems)
    wait_for(fetch_extra)
    tile = jnp.zeros((EXTRA, D), f32)
    for number in range(n_slots):
        for pair in range(PAIRS):
            tile = tile + extras[number, pair].astype(f32)
    gains[...] = tile[0:8]
    falls[...] = dot_nn(tile[8:16, 0:128].astype(bf16), onehot[...])
    fetch_x.wait()
    resident = x_rows[...].reshape(rows_held * length, D).astype(f32)
    low = (resident * root_scale(resident) * tile[0:1]).astype(bf16)
    normed[...] = low
    allowed = [self_masks(tab, targets, row, length) for row in range(rows_held)]
    total = resident
    for group in GROUPS:
        for pair in group:
            wait_for(fetch[pair])
            projected = dot_nn(low, weights[pair, :, 0 : 3 * PAIR]).astype(bf16)
            query[pair] = projected[:, 0:PAIR]
            key[pair] = projected[:, PAIR : 2 * PAIR]
            value[pair] = projected[:, 2 * PAIR :]
        places = [(pair, row, slice(row * length, (row + 1) * length)) for pair in group for row in range(rows_held)]
        biases = {pair: bias_of(tab, falls, pair, length) for pair in group}
        mixes, logs = attend(
            [
                (query[pair, span], key[pair, span], value[pair, span], biases[pair], allowed[row])
                for pair, row, span in places
            ]
        )
        for (pair, row, span), mix, log_total in zip(places, mixes, logs):
            mixed[pair, span] = mix
            totals[pair, row : row + 1, :] = log_total
        for pair in group:
            total = total + dot_nt(mixed[pair], weights[pair, :, 3 * PAIR :])
    after[...] = total


def encoder_copies(pieces, encoder, tab, rows_held, sems):
    width = encoder.shape[1] // len(pieces)
    copies = []
    for number, piece in enumerate(pieces):
        start = tab[24] if piece.shape[0] > rows_held else 0
        copies.append(
            pltpu.make_async_copy(
                piece.at[pl.ds(start, rows_held)],
                encoder.at[:, pl.ds(number * width, width), :],
                sems.at[number],
            )
        )
    return copies


def cross_forward_kernel(n_slots, n_pieces, rows_held, tab, targets, sources, gains, before, *refs):
    slots, pieces, refs = refs[:n_slots], refs[n_slots : n_slots + n_pieces], refs[n_slots + n_pieces :]
    after, normed, query, key, value, mixed, totals, encoder = refs[:8]
    weights, sems, piece_sems = refs[8:]
    length = before.shape[0] // rows_held
    source_length = sources.shape[1]
    fetch_pieces = encoder_copies(pieces, encoder, tab, rows_held, piece_sems)
    for copy in fetch_pieces:
        copy.start()
    fetch = weight_copies(slots, weights, tab, sems, 4 * PAIR)
    resident = before[...]
    low = (resident * root_scale(resident) * gains[1:2]).astype(bf16)
    normed[...] = low
    allowed = [
        cross_masks(tab, targets, sources, row, n_pieces, 16 if n_pieces > 1 else 28)
        for row in range(rows_held)
    ]
    wait_for(fetch_pieces)
    source = encoder[...].reshape(rows_held * source_length, D)
    total = resident
    for group in GROUPS:
        for pair in group:
            wait_for(fetch[pair])
            query[pair] = dot_nn(low, weights[pair, :, 0:PAIR]).astype(bf16)
            projected = dot_nn(source, weights[pair, :, PAIR : 3 * PAIR]).astype(bf16)
            key[pair] = projected[:, 0:PAIR]
            value[pair] = projected[:, PAIR:]
        places = [(pair, row) for pair in group for row in range(rows_held)]
        spans = [slice(row * length, (row + 1) * length) for row in range(rows_held)]
        wides = [slice(row * source_length, (row + 1) * source_length) for row in range(rows_held)]
        mixes, logs = attend(
            [
                (query[pair, spans[row]], key[pair, wides[row]], value[pair, wides[row]], None, allowed[row])
                for pair, row in places
            ]
        )
        for (pair, row), mix, log_total in zip(places, mixes, logs):
            mixed[pair, spans[row]] = mix
            totals[pair, row : row + 1, :] = log_total
        for pair in group:
            total = total + dot_nt(mixed[pair], weights[pair, :, 3 * PAIR :])
    after[...] = total


def feed_kernel(n_slots, n_outs, rows_held, tab, gains, before, c_all, *refs):
    slots, refs = refs[:n_slots], refs[n_slots:]
    low_out, grad_before, grad_gain = refs[:3]
    outs, refs = refs[3 : 3 + n_outs], refs[3 + n_outs :]
    weights, c_rows, turned, normed_turned, again, c_turned, held, sems, c_sem, out_sems = refs
    fetch_c = pltpu.make_async_copy(c_all.at[pl.ds(tab[24], rows_held)], c_rows, c_sem)
    fetch = weight_copies(slots, weights, tab, sems)
    fetch_c.start()
    resident = before[...]
    gain = gains[2:3]
    low = (resident * root_scale(resident) * gain).astype(bf16)
    turned[...] = jnp.transpose(low)
    permute_rows(turned, normed_turned, tab, n_slots)
    fetch_c.wait()
    cotangent = c_rows[...].reshape(resident.shape)
    again[...] = jnp.transpose(cotangent)
    permute_rows(again, c_turned, tab, n_slots)
    writer = SlotWriter(outs, held, out_sems)
    total = resident
    grad_normed = jnp.zeros_like(resident)
    for pair in range(PAIRS):
        wait_for(fetch[pair])
        inner, outer = weights[pair, :, 0:HIDDEN], weights[pair, :, HIDDEN:]
        u = dot_nn(low, inner)
        squared = u * u
        bent = jnp.tanh(gelu_slope * (u + gelu_cubic * u * squared))
        hidden = (0.5 * u * (1.0 + bent)).astype(bf16)
        slope = 0.5 * (1.0 + bent) + 0.5 * u * (1.0 - bent * bent) * gelu_slope * (
            1.0 + 3.0 * gelu_cubic * squared
        )
        total = total + dot_nt(hidden, outer)
        grad_u = (dot_nn(cotangent, outer) * slope).astype(bf16)
        grad_normed = grad_normed + dot_nt(grad_u, inner)
        writer.write(pair, (dot_nn(normed_turned[...], grad_u), dot_nn(c_turned[...], hidden)))
    low_out[...] = total.astype(bf16)
    through, gain_part = root_back(resident, gain, grad_normed)
    grad_before[...] = cotangent.astype(f32) + through
    grad_gain[...] = gain_part
    writer.finish()


def cross_back_kernel(
    n_slots, n_pieces, rows_held, tab, targets, sources, gains, grad_after, before, *refs
):
    query, key, value, totals = refs[:4]
    slots, refs = refs[4 : 4 + n_slots], refs[4 + n_slots :]
    grad_before, grad_gain, d_query, d_key, d_value, weights, sems = refs
    length = before.shape[0] // rows_held
    source_length = sources.shape[1]
    fetch = weight_copies(slots, weights, tab, sems, 4 * PAIR)
    grad_in = grad_after[...]
    low = grad_in.astype(bf16)
    allowed = [
        cross_masks(tab, targets, sources, row, n_pieces, 16 if n_pieces > 1 else 28)
        for row in range(rows_held)
    ]
    spans = [slice(row * length, (row + 1) * length) for row in range(rows_held)]
    wides = [slice(row * source_length, (row + 1) * source_length) for row in range(rows_held)]
    grad_normed = jnp.zeros_like(grad_in)
    for group in GROUPS:
        wait_for([copy for pair in group for copy in fetch[pair]])
        grad_mixed = {pair: dot_nn(low, weights[pair, :, 3 * PAIR :]).astype(bf16) for pair in group}
        places = [(pair, row) for pair in group for row in range(rows_held)]
        results = attend_back(
            [
                (
                    query[pair, spans[row]],
                    key[pair, wides[row]],
                    value[pair, wides[row]],
                    None,
                    allowed[row],
                    totals[pair, row : row + 1, :],
                    grad_mixed[pair][spans[row]],
                )
                for pair, row in places
            ]
        )
        for (pair, row), one, two, three, _ in zip(places, *results):
            d_query[pair, spans[row]] = one
            d_key[pair, wides[row]] = two
            d_value[pair, wides[row]] = three
        for pair in group:
            grad_normed = grad_normed + dot_nt(d_query[pair], weights[pair, :, 0:PAIR])
    through, gain_part = root_back(before[...], gains[1:2], grad_normed)
    grad_before[...] = grad_in + through
    grad_gain[...] = gain_part


def cross_weights_kernel(
    n_slots, n_outs, n_after, tab, grad_after, normed, mixed, encoder, d_query, d_key, d_value, *refs
):
    refs = refs[n_after:]
    outs, refs = refs[:n_outs], refs[n_outs:]
    turned, low_turned, again, normed_turned, wide_turned, encoder_turned, held, out_sems = refs
    writer = SlotWriter(outs, held, out_sems)
    turned[...] = jnp.transpose(grad_after[...].astype(bf16))
    permute_rows(turned, low_turned, tab, n_slots)
    again[...] = jnp.transpose(normed[...])
    permute_rows(again, normed_turned, tab, n_slots)
    wide_turned[...] = jnp.transpose(encoder[...].reshape(wide_turned.shape[1], D))
    permute_rows(wide_turned, encoder_turned, tab, n_slots)
    for pair in range(PAIRS):
        writer.write(
            pair,
            (
                dot_nn(normed_turned[...], d_query[pair]),
                dot_nn(encoder_turned[...], d_key[pair]),
                dot_nn(encoder_turned[...], d_value[pair]),
                dot_nn(low_turned[...], mixed[pair]),
            ),
        )
    writer.finish()


def self_back_kernel(
    n_slots, n_outs, n_after, rows_held, tab, targets, onehot, gains, falls, gain_two, gain_three, grad_after, low_out, x_all, *refs
):
    normed, query, key, value, mixed, totals = refs[:6]
    slots, refs = refs[6 : 6 + n_slots], refs[6 + n_slots + n_after :]
    low_grad = refs[0]
    outs, refs = refs[1 : 1 + n_outs], refs[1 + n_outs :]
    weights, x_rows, turned, low_turned, again, normed_turned, bias_rows, held, sems, x_sem, out_sems = refs
    writer = SlotWriter(outs, held, out_sems)
    length = x_all.shape[1]
    fetch_x = pltpu.make_async_copy(x_all.at[pl.ds(tab[24], rows_held)], x_rows, x_sem)
    fetch = weight_copies(slots, weights, tab, sems)
    fetch_x.start()
    grad_in = grad_after[...]
    low = grad_in.astype(bf16)
    turned[...] = jnp.transpose(low)
    permute_rows(turned, low_turned, tab, n_slots)
    again[...] = jnp.transpose(normed[...])
    permute_rows(again, normed_turned, tab, n_slots)
    allowed = [self_masks(tab, targets, row, length) for row in range(rows_held)]
    grad_normed = jnp.zeros_like(grad_in)
    spans = [slice(row * length, (row + 1) * length) for row in range(rows_held)]
    for group in GROUPS:
        wait_for([copy for pair in group for copy in fetch[pair]])
        grad_mixed = {pair: dot_nn(low, weights[pair, :, 3 * PAIR :]).astype(bf16) for pair in group}
        biases = {pair: bias_of(tab, falls, pair, length) for pair in group}
        places = [(pair, row) for pair in group for row in range(rows_held)]
        results = attend_back(
            [
                (
                    query[pair, spans[row]],
                    key[pair, spans[row]],
                    value[pair, spans[row]],
                    biases[pair],
                    allowed[row],
                    totals[pair, row : row + 1, :],
                    grad_mixed[pair][spans[row]],
                )
                for pair, row in places
            ]
        )
        parts = {place: result for place, *result in zip(places, *results)}
        for pair in group:
            joined = [jnp.concatenate(parts[pair, row][:3], axis=1) for row in range(rows_held)]
            joined = jnp.concatenate(joined, axis=0) if rows_held > 1 else joined[0]
            grad_normed = grad_normed + dot_nt(joined, weights[pair, :, 0 : 3 * PAIR])
            writer.write(
                pair, (dot_nn(normed_turned[...], joined), dot_nn(low_turned[...], mixed[pair]))
            )
            grad_bias = sum(parts[pair, row][3] for row in range(rows_held))
            for side in range(2):
                diagonal = fold_diagonals(grad_bias[:, side * length : (side + 1) * length])
                bias_rows[pl.ds(tab[16 + pair] * 2 + side, 1), :] = diagonal
    fetch_x.wait()
    resident = x_rows[...].reshape(grad_in.shape).astype(f32)
    through, gain_one = root_back(resident, gains[0:1], grad_normed)
    low_grad[0:rows_held] = low_out[...].reshape(x_rows.shape)
    low_grad[rows_held:] = (grad_in + through).astype(bf16).reshape(x_rows.shape)
    table = lax.dot_general(
        bias_rows[...],
        onehot[...].astype(f32),
        (((1,), (1,)), ((), ())),
        precision=lax.Precision.HIGHEST,
        preferred_element_type=f32,
    )
    blank = jnp.zeros((5, D), f32)
    table = jnp.concatenate((table, jnp.zeros((8, D - 128), f32)), axis=1)
    tile = jnp.concatenate((gain_one, gain_two[...], gain_three[...], blank, table), axis=0).astype(bf16)
    rows = D // n_slots
    for pair in range(PAIRS):
        for number in range(n_slots):
            held[number, pair, rows : rows + EXTRA, :] = tile
        writer.send(pair, rows, EXTRA, PAIRS + pair)
    writer.finish()


def pack_attention_kernel(n_dp, tab, query, keyval, output, gains, table, own):
    rows, width = query.shape[1], gains.shape[1]
    place_dp, place_mp = tab[25], tab[26]
    parts = []
    for number in range(2):
        parts += [query[number], keyval[number, 0], keyval[number, 1], output[number]]
    own[0:rows, :] = jnp.concatenate(parts, axis=1).astype(bf16)
    wide = jnp.concatenate([gains[...]] * n_dp, axis=1)
    lane = lax.broadcasted_iota(jnp.int32, wide.shape, 1)
    wide = jnp.where((lane // width == place_dp) & (place_mp == 0), wide, 0.0)
    heads, bands = table.shape
    lane = lax.broadcasted_iota(jnp.int32, (bands, D), 1)
    band = lax.broadcasted_iota(jnp.int32, (bands, D), 0)
    at_band = jnp.where(lane == place_dp * bands + band, 1.0, 0.0).astype(bf16)
    head = lax.broadcasted_iota(jnp.int32, (HEADS, heads), 0)
    column = lax.broadcasted_iota(jnp.int32, (HEADS, heads), 1)
    at_head = jnp.where(head == place_mp * heads + column, 1.0, 0.0).astype(bf16)
    placed = dot_nn(at_head, dot_nn(table[...].astype(bf16), at_band).astype(bf16))
    blank = jnp.zeros((HEADS - wide.shape[0], D), f32)
    tile = jnp.concatenate((wide, blank, placed), axis=0).astype(bf16)
    own[rows : rows + EXTRA, 0:D] = tile
    own[rows : rows + EXTRA, D:] = jnp.zeros_like(tile)


def pack_feed_kernel(inner, outer, *refs):
    refs[-1][...] = jnp.concatenate((inner[...], outer[...]), axis=1).astype(bf16)


def split_encoder_kernel(rows_held, tab, encoder, *refs):
    outs, sems = refs[:-1], refs[-1]
    copies = [
        pltpu.make_async_copy(
            encoder.at[pl.ds(tab[17 + number] * rows_held, rows_held)], out, sems.at[number]
        )
        for number, out in enumerate(outs)
    ]
    for copy in copies:
        copy.start()
    for copy in copies:
        copy.wait()


def stack_kernel(count, *refs):
    out = refs[-1]
    for number in range(count):
        out[number] = refs[number][...]


def stack_through_kernel(count, *refs):
    stack_kernel(count, *refs[:-1])


def spread_kernel(rows_held, tab, *refs):
    pieces, outs = refs[:4], refs[-2:]
    for number, piece in enumerate(pieces):
        for side, out in enumerate(outs):
            here = piece[side * rows_held : (side + 1) * rows_held]
            out[pl.ds(tab[16 + number] * rows_held, rows_held)] = here


def shape(dims, dtype):
    return jax.ShapeDtypeStruct(dims, dtype)


def dma_sems(*counts):
    return pltpu.SemaphoreType.DMA(counts)


def anys(arrays):
    return [(array, "any") for array in arrays]


def vmems(arrays):
    return [(array, "vmem") for array in arrays]


def call(kernel, operands, outs, scratch, micros=1, aliases=None, any_outs=()):
    spaces = {"smem": pltpu.SMEM, "vmem": pltpu.VMEM, "any": pl.ANY}
    arrays = [array for array, _ in operands]
    moved = sum(a.size * a.dtype.itemsize for a in arrays) + sum(
        math.prod(o.shape) * o.dtype.itemsize for o in outs
    )
    return pl.pallas_call(
        kernel,
        out_shape=tuple(outs),
        in_specs=[pl.BlockSpec(memory_space=spaces[place]) for _, place in operands],
        out_specs=tuple(
            pl.BlockSpec(memory_space=pl.ANY if i in any_outs or i in (aliases or {}).values() else pltpu.VMEM)
            for i in range(len(outs))
        ),
        input_output_aliases=aliases or {},
        scratch_shapes=scratch,
        compiler_params=pltpu.CompilerParams(vmem_limit_bytes=VMEM_BYTES),
        cost_estimate=pl.CostEstimate(flops=int(micros * 1.15e9), bytes_accessed=moved if micros else 0, transcendentals=0),
    )(*arrays)


def bucket_onehot(length):
    distance = np.arange(length)
    bucket = np.minimum(distance, 16)
    for edge_value in bucket_edges:
        bucket = bucket + (distance >= edge_value)
    return jnp.asarray(np.arange(128)[:, None] == bucket[None, :], bf16)


def adam_step(weight, first, second, grad, rate, decay):
    new_first = beta_first * first + (1.0 - beta_first) * grad
    new_second = beta_second * second + (1.0 - beta_second) * grad * grad
    ratio = (
        new_first
        / (1.0 - beta_first**STEP)
        / (jnp.sqrt(new_second / (1.0 - beta_second**STEP)) + adam_eps)
    )
    return (new_first, new_second, weight - rate * (ratio + decay * weight))


def step_rates():
    return (
        rate_factor * (16 * D) ** (-0.5),
        rate_factor * D ** (-0.5),
        rate_factor * (HD // 8) ** (-0.5),
        rate_factor * D ** (-0.5),
        rate_factor * (FF // 2) ** (-0.5),
        rate_factor,
        rate_factor,
    )


def gate_kernel(*refs):
    pass


def gate(array, after):
    (same,) = call(
        gate_kernel, anys([array] + list(after)), [shape(array.shape, array.dtype)], [], aliases={0: 0}
    )
    return same


def fold(arrived, kept, after=()):
    if after:
        kept = gate(kept, after)
    half = arrived.shape[0] // 2
    parts = [(arrived[i : i + half], kept[i : i + half]) for i in (half, 0)]
    if half == 1:
        parts = [(x[0], y[0]) for x, y in parts]
    return [(x.astype(f32) + y.astype(f32)).astype(bf16) for x, y in parts]


class TreePlan:
    n_slots = 8
    out_slots = (4, 4)
    order = (0, 2, 1, 3)

    def __init__(self, n_dp, n_mp):
        self.n_dp, self.n_mp = n_dp, n_mp

    def pairs(self, target):
        n_mp = self.n_mp
        return [
            (d * n_mp + m, t * n_mp + s)
            for d in range(self.n_dp)
            for m in range(n_mp)
            for t, s in (target(d, m),)
        ]

    def hop_z(self, array, number):
        return lax.ppermute(array, ALL, self.pairs(lambda d, m: (d, m ^ number)))

    def hop_core(self, array):
        return lax.ppermute(array, ALL, self.pairs(lambda d, m: (d ^ 1, m)))

    def hop_first(self, array):
        return lax.ppermute(array, ALL, self.pairs(lambda d, m: (d ^ (4 if d & 1 else 2), m)))

    def hop_second(self, array):
        return lax.ppermute(array, ALL, self.pairs(lambda d, m: (d ^ (2 if d & 1 else 4), m)))

    def table(self, place_dp, place_mp, rows_held):
        core = place_dp & 1
        first, second = 2 + 2 * core, 4 - 2 * core
        own = [place_dp ^ (a * first) ^ (b * second) for b in range(2) for a in range(2)]
        peer = [place_dp ^ 1 ^ (a * second) ^ (b * first) for b in range(2) for a in range(2)]
        return own + peer, [place_mp ^ j for j in self.order]

    def along_z(self, own, after=()):
        across, near = self.hop_z(own, 2), self.hop_z(own, 1)
        if after:
            across = gate(across, after)
        return [own, across, near, self.hop_z(across, 1)]

    def stack(self, pieces, after=()):
        (base,) = call(
            functools.partial(stack_kernel, len(pieces)),
            vmems(pieces) + anys(after),
            [shape((len(pieces),) + pieces[0].shape, bf16)],
            [],
        )
        return base

    def stack_through(self, pieces, through):
        return call(
            functools.partial(stack_through_kernel, len(pieces)),
            vmems(pieces) + anys([through]),
            [shape((len(pieces),) + pieces[0].shape, bf16), shape(through.shape, bf16)],
            [],
            aliases={len(pieces): 1},
        )

    def in_plane(self, base, near, far):
        slots = [base, near, far, self.hop_second(near)]
        return slots + [self.hop_core(slot) for slot in slots]

    def attention_shard(self, tab, query, keyval, output, gains, table):
        rows, columns = query.shape[1:]
        (own,) = call(
            functools.partial(pack_attention_kernel, self.n_dp),
            [(tab, "smem")] + vmems((query, keyval, output, gains, table)),
            [shape((rows + EXTRA, 8 * columns), bf16)],
            [],
        )
        return own

    def feed_shard(self, inner, outer, after):
        (own,) = call(
            pack_feed_kernel,
            vmems((inner, outer)) + anys(after),
            [shape((inner.shape[0], 2 * inner.shape[1]), bf16)],
            [],
        )
        return own

    def weights(self, tab, query, keyval, output, inner, outer, gains, table, encoder, rows_held):
        attention = self.along_z(self.attention_shard(tab, query, keyval, output, gains, table))
        parts = call(
            functools.partial(split_encoder_kernel, rows_held),
            [(tab, "smem")] + anys([encoder]),
            [shape((rows_held,) + encoder.shape[1:], bf16)] * 3,
            [dma_sems(3)],
        )
        own_feed = self.feed_shard(inner, outer, [attention[1], parts[0]])
        feed = self.along_z(own_feed)
        base = self.stack(attention, [own_feed])
        near, far = self.hop_first(base), self.hop_second(base)
        feed_base, near = self.stack_through(feed, near)
        attention = self.in_plane(base, near, far)
        sources = [encoder] + [self.hop_z(part, j) for part, j in zip(parts, self.order[1:])]
        feed = self.in_plane(feed_base, self.hop_first(feed_base), self.hop_second(feed_base))
        return attention, feed, sources, feed_base

    def reduce_core(self, parts, after=()):
        own, peer = parts
        return fold(self.hop_core(peer), own, after)

    def reduce_second(self, pair, after=()):
        return fold(self.hop_second(pair[0]), pair[1], after)

    def reduce_first(self, pair, after=()):
        return fold(self.hop_first(pair[0]), pair[1], after)

    def reduce_near(self, pair, after=()):
        return fold(self.hop_z(pair[0], 1), pair[1], after)

    def reduce_across(self, pair, after=()):
        sent, kept = pair
        if after:
            kept = gate(kept, after)
        total = self.hop_z(sent, 2).astype(f32) + kept.astype(f32)
        return total, total[D // self.n_dp :]

    def finish(self, tab, rows_out, feed, cross, own):
        feed = self.reduce_first(feed, [cross[0]])
        own = self.reduce_second(own, [feed[0]])
        cross = self.reduce_core(cross, [own[0]])
        pieces = self.along_z(rows_out, [cross[0]])
        feed = self.reduce_near(feed, [cross[0]])
        own = self.reduce_first(own, [feed[0]])
        cross = self.reduce_second(cross, [own[0]])
        feed = self.reduce_across(feed, [cross[0]])
        own = self.reduce_near(own, [cross[0]])
        cross = self.reduce_first(cross, [own[0]])
        cross = self.reduce_near(cross)
        rows = self.spread(tab, pieces, [cross[0]])
        return rows, [feed, self.reduce_across(cross), self.reduce_across(own, [cross[0]])]

    def spread(self, tab, pieces, after):
        piece = pieces[0]
        half = piece.shape[0] // 2
        out = shape((half * self.n_mp,) + piece.shape[1:], piece.dtype)
        return call(
            functools.partial(spread_kernel, half),
            [(tab, "smem")] + vmems(pieces) + anys(after),
            [out, out],
            [],
        )


class PlainPlan:
    n_slots = 1
    out_slots = (1,)

    def __init__(self, n_dp, n_mp):
        self.n_dp, self.n_mp = n_dp, n_mp

    def table(self, place_dp, place_mp, rows_held):
        return [0], [0, 1, 2, 3]

    def gather(self, own, kinds):
        full = lax.all_gather(own, ("mp", "dp"), axis=0, tiled=True)
        full = full.reshape(self.n_mp, D, kinds, -1).transpose(2, 1, 0, 3)
        return full.reshape(kinds, D, PAIRS, -1).transpose(2, 1, 0, 3).reshape(PAIRS, D, -1)

    def weights(self, tab, query, keyval, output, inner, outer, gains, table, encoder, rows_held):
        place_dp, place_mp = lax.axis_index("dp"), lax.axis_index("mp")
        parts = []
        for i in range(2):
            parts += [query[i], keyval[i, 0], keyval[i, 1], output[i]]
        attention = self.gather(jnp.concatenate(parts, axis=1).astype(bf16), 8)
        feed = self.gather(jnp.concatenate((inner, outer), axis=1).astype(bf16), 2)
        width = gains.shape[1]
        tile = jnp.zeros((EXTRA, D), f32)
        spot = jnp.where(place_mp == 0, gains, 0.0)
        tile = lax.dynamic_update_slice(tile, spot, (0, place_dp * width))
        heads, bands = table.shape
        tile = lax.dynamic_update_slice(tile, table, (8 + place_mp * heads, place_dp * bands))
        tile = lax.psum(tile.astype(bf16).astype(f32), ALL).astype(bf16)
        tile = jnp.concatenate((tile, jnp.zeros_like(tile)), axis=1)[None]
        tile = jnp.concatenate((tile, jnp.zeros((PAIRS - 1,) + tile.shape[1:], bf16)))
        sources = lax.all_to_all(encoder, "mp", split_axis=0, concat_axis=1, tiled=True)
        return [jnp.concatenate((attention, tile), axis=1)], [feed], [sources], feed

    def reduce_core(self, parts):
        return parts

    def reduce(self, grads):
        kinds = 4 if grads.shape[2] == 4 * PAIR else 2
        full = grads[:, :D].reshape(PAIRS, D, kinds, -1).transpose(2, 1, 0, 3)
        full = full.reshape(kinds, D, self.n_mp, -1).transpose(2, 1, 0, 3)
        total = lax.psum_scatter(
            full.reshape(self.n_mp * D, -1), ("mp", "dp"), scatter_dimension=0, tiled=True
        ).astype(f32)
        return total, lax.psum(grads[0, D:].astype(f32), ALL) if grads.shape[1] > D else None

    def finish(self, tab, rows_out, feed, cross, own):
        half = rows_out.shape[0] // 2
        rows = [
            lax.all_gather(rows_out[i : i + half], "mp", axis=0, tiled=True) for i in (0, half)
        ]
        return rows, [self.reduce(parts[0][0]) for parts in (feed, cross, own)]

    def reduce_second(self, parts):
        return parts


def shards(
    plan,
    inputs,
    encoder,
    cotangent,
    target_segments,
    encoder_segments,
    query_weight,
    query_first,
    query_second,
    keyval_weight,
    keyval_first,
    keyval_second,
    output_weight,
    output_first,
    output_second,
    inner_weight,
    inner_first,
    inner_second,
    outer_weight,
    outer_first,
    outer_second,
    gains,
    gains_first,
    gains_second,
    bias_table,
    table_first,
    table_second,
):
    n_slots, out_slots = plan.n_slots, plan.out_slots
    n_outs = len(out_slots)
    seq_count, length, _ = inputs.shape
    source_length = encoder_segments.shape[1]
    rows_held = seq_count // plan.n_mp
    tokens, sources = rows_held * length, rows_held * source_length
    place_dp, place_mp = lax.axis_index("dp"), lax.axis_index("mp")
    slot_table, pair_table = plan.table(place_dp, place_mp, rows_held)
    entries = slot_table + [0] * (16 - len(slot_table)) + pair_table + [0] * 4
    entries = entries + [place_mp * rows_held, place_dp, place_mp] + [0] * 5
    tab = jnp.stack([jnp.asarray(entry, jnp.int32) for entry in entries])
    onehot = bucket_onehot(length)
    attn_slots, feed_slots, pieces, feed_base = plan.weights(
        tab,
        query_weight,
        keyval_weight,
        output_weight.transpose(0, 2, 1),
        inner_weight,
        outer_weight.T,
        gains,
        bias_table.T,
        encoder,
        rows_held,
    )
    n_pieces = len(pieces)
    rows, columns = query_weight.shape[1:]
    width = gains.shape[1]
    bands, heads = bias_table.shape

    flat = (tokens, D)
    paired = (PAIRS, tokens, PAIR)
    wide = (PAIRS, sources, PAIR)
    stats = shape((PAIRS, rows_held, 2 * length), f32)
    attn_weights = VM((PAIRS, D, 4 * PAIR), bf16)

    after_self, normed_one, q_one, k_one, v_one, mix_one, sum_one, gain_rows, falls = call(
        functools.partial(self_forward_kernel, n_slots, 1, rows_held),
        [(tab, "smem")] + vmems((target_segments, onehot)) + anys([inputs] + attn_slots + [feed_base]),
        [shape(flat, f32), shape(flat, bf16)]
        + [shape(paired, bf16)] * 4
        + [stats, shape((8, D), f32), shape((8, length), f32)],
        [
            attn_weights,
            VM((n_slots, PAIRS, EXTRA, D), bf16),
            VM((rows_held, length, D), bf16),
            dma_sems(n_slots, PAIRS),
            dma_sems(n_slots),
            pltpu.SemaphoreType.DMA,
        ],
        micros=6,
    )
    after_cross, normed_two, q_two, k_two, v_two, mix_two, sum_two, source_rows = call(
        functools.partial(cross_forward_kernel, n_slots, n_pieces, rows_held),
        [(tab, "smem")]
        + vmems((target_segments, encoder_segments, gain_rows, after_self))
        + anys(attn_slots + pieces),
        [
            shape(flat, f32),
            shape(flat, bf16),
            shape(paired, bf16),
            shape(wide, bf16),
            shape(wide, bf16),
            shape(paired, bf16),
            stats,
            shape((rows_held, source_length, D), bf16),
        ],
        [attn_weights, dma_sems(n_slots, PAIRS), dma_sems(n_pieces)],
        micros=11,
    )

    def grad_outs(extra, width_out):
        return [
            shape((count, PAIRS, D // n_slots + extra, width_out), bf16) for count in out_slots
        ]

    feed_result = call(
        functools.partial(feed_kernel, n_slots, n_outs, rows_held),
        [(tab, "smem")] + vmems((gain_rows, after_cross)) + anys([cotangent] + feed_slots),
        [shape(flat, bf16), shape(flat, f32), shape((1, D), f32)] + grad_outs(0, 2 * HIDDEN),
        [
            VM((PAIRS, D, 2 * HIDDEN), bf16),
            VM((rows_held, length, D), bf16),
            VM((D, tokens), bf16),
            VM((D, tokens), bf16),
            VM((D, tokens), bf16),
            VM((D, tokens), bf16),
            VM((n_slots, PAIRS, D // n_slots, 2 * HIDDEN), bf16),
            dma_sems(n_slots, PAIRS),
            pltpu.SemaphoreType.DMA,
            dma_sems(n_outs, PAIRS),
        ],
        any_outs=range(3, 3 + n_outs),
        micros=10,
    )
    low_out, grad_second, gain_three = feed_result[:3]
    core_feed = plan.reduce_core(feed_result[3:])
    grad_first, gain_two, dq_two, dk_two, dv_two = call(
        functools.partial(cross_back_kernel, n_slots, n_pieces, rows_held),
        [(tab, "smem")]
        + vmems((target_segments, encoder_segments, gain_rows, grad_second, after_self))
        + vmems((q_two, k_two, v_two, sum_two))
        + anys(attn_slots),
        [shape(flat, f32), shape((1, D), f32), shape(paired, bf16), shape(wide, bf16), shape(wide, bf16)],
        [attn_weights, dma_sems(n_slots, PAIRS)],
        micros=10,
    )
    self_result = call(
        functools.partial(self_back_kernel, n_slots, n_outs, 1, rows_held),
        [(tab, "smem")]
        + vmems((target_segments, onehot, gain_rows, falls, gain_two, gain_three, grad_first, low_out))
        + anys([inputs])
        + vmems((normed_one, q_one, k_one, v_one, mix_one, sum_one))
        + anys(attn_slots + [core_feed[0]]),
        [shape((2 * rows_held, length, D), bf16)] + grad_outs(EXTRA, 4 * PAIR),
        [
            attn_weights,
            VM((rows_held, length, D), bf16),
            VM((D, tokens), bf16),
            VM((D, tokens), bf16),
            VM((D, tokens), bf16),
            VM((D, tokens), bf16),
            VM((8, length), f32),
            VM((n_slots, PAIRS, D // n_slots + EXTRA, 4 * PAIR), bf16),
            dma_sems(n_slots, PAIRS),
            pltpu.SemaphoreType.DMA,
            dma_sems(n_outs, 2 * PAIRS),
        ],
        any_outs=range(1, 1 + n_outs),
        micros=10,
    )
    second_feed = plan.reduce_second(core_feed)
    core_self = plan.reduce_core(self_result[1:])
    cross_grads = call(
        functools.partial(cross_weights_kernel, n_slots, n_outs, 2),
        [(tab, "smem")]
        + vmems((grad_second, normed_two, mix_two, source_rows, dq_two, dk_two, dv_two))
        + anys([second_feed[0], core_self[0]]),
        grad_outs(0, 4 * PAIR),
        [
            VM((D, tokens), bf16),
            VM((D, tokens), bf16),
            VM((D, tokens), bf16),
            VM((D, tokens), bf16),
            VM((D, sources), bf16),
            VM((D, sources), bf16),
            VM((n_slots, PAIRS, D // n_slots, 4 * PAIR), bf16),
            dma_sems(n_outs, PAIRS),
        ],
        any_outs=range(n_outs),
        micros=7,
    )
    (outputs, input_grad), ((grad_feed, _), (grad_cross, _), (grad_self, tile)) = plan.finish(
        tab, self_result[0], second_feed, cross_grads, core_self
    )

    def kind(grads, number):
        return grads[:rows, number * columns : (number + 1) * columns]

    hidden = inner_weight.shape[1]
    grads = (
        jnp.stack((kind(grad_self, 0), kind(grad_cross, 0))),
        jnp.stack(
            (
                jnp.stack((kind(grad_self, 1), kind(grad_self, 2))),
                jnp.stack((kind(grad_cross, 1), kind(grad_cross, 2))),
            )
        ),
        jnp.stack((kind(grad_self, 3).T, kind(grad_cross, 3).T)),
        grad_feed[:, :hidden],
        grad_feed[:, hidden:].T,
        lax.dynamic_slice_in_dim(tile[0:3], place_dp * width, width, 1),
        lax.dynamic_slice(tile, (8 + place_mp * heads, place_dp * bands), (heads, bands)).T,
    )
    params = (
        query_weight,
        keyval_weight,
        output_weight,
        inner_weight,
        outer_weight,
        gains,
        bias_table,
    )
    firsts = (
        query_first,
        keyval_first,
        output_first,
        inner_first,
        outer_first,
        gains_first,
        table_first,
    )
    seconds = (
        query_second,
        keyval_second,
        output_second,
        inner_second,
        outer_second,
        gains_second,
        table_second,
    )
    updated = [
        adam_step(*param_entry)
        for param_entry in zip(params, firsts, seconds, grads, step_rates(), step_decays)
    ]
    return (outputs, input_grad) + tuple(array for triple in updated for array in triple)


def solution(mesh):
    n_dp, n_mp = mesh.shape["dp"], mesh.shape["mp"]
    plan = (TreePlan if (n_dp, n_mp) == (8, 4) else PlainPlan)(n_dp, n_mp)
    by_query, by_keyval = P(None, "dp", "mp"), P(None, None, "dp", "mp")
    by_output, by_inner, by_outer = P(None, "mp", "dp"), P("dp", "mp"), P("mp", "dp")
    weights = (by_query,) * 3 + (by_keyval,) * 3 + (by_output,) * 3 + (by_inner,) * 3
    weights = weights + (by_outer,) * 3 + (P(None, "dp"),) * 3 + (P("dp", "mp"),) * 3
    tokens = P("dp", None, None)
    return jax.shard_map(
        functools.partial(shards, plan),
        mesh=mesh,
        in_specs=(tokens, P("dp", "mp", None), tokens, P("dp", None), P("dp", None)) + weights,
        out_specs=(tokens, tokens) + weights,
        check_vma=False,
    )
```

```python
import functools
import math

import jax
import jax.numpy as jnp
import numpy as np
from jax import lax
from jax.experimental import pallas as pl
from jax.experimental.pallas import tpu as pltpu
from jax.sharding import PartitionSpec as P

D = 512
HEADS = 8
HEAD_DIM = 64
FF = 2048
NB = 32
HD = 512
STEP = 10
PAIRS = HEADS // 2
PAIR = 2 * HEAD_DIM
HIDDEN = FF // PAIRS
EXTRA = 16
GROUPS = tuple((i, i + 1) for i in range(0, PAIRS, 2))
VMEM_BYTES = 56 * 1024 * 1024

norm_eps = 1e-06
beta_first = 0.9
beta_second = 0.95
adam_eps = 1e-08
decay_weight = 0.1
rate_factor = 0.6
masked_value = -1000000000.0
bucket_edges = tuple((math.ceil(16 * 8 ** (number / 16)) for number in range(1, 16)))
step_decays = (decay_weight, decay_weight, decay_weight, decay_weight, decay_weight, 0.0, 0.0)
gelu_slope = math.sqrt(2.0 / math.pi)
gelu_cubic = 0.044715

f32 = jnp.float32
bf16 = jnp.bfloat16
ALL = ("dp", "mp")
VM = pltpu.VMEM


def dot_nn(a, b):
    return lax.dot_general(a, b, (((1,), (0,)), ((), ())), preferred_element_type=f32)


def dot_nt(a, b):
    return lax.dot_general(a, b, (((1,), (1,)), ((), ())), preferred_element_type=f32)


def dot_tn(a, b):
    return lax.dot_general(a, b, (((0,), (0,)), ((), ())), preferred_element_type=f32)


def root_scale(values):
    return lax.rsqrt(jnp.mean(values * values, axis=-1, keepdims=True) + norm_eps)


def root_back(values, gain, grad):
    scale = root_scale(values)
    grad_gain = jnp.sum(grad * values * scale, axis=0, keepdims=True)
    weighted = grad * gain
    along = jnp.sum(weighted * values, axis=-1, keepdims=True)
    inverse = 1.0 / values.shape[-1]
    return scale * weighted - values * (scale * scale * scale * along * inverse), grad_gain


def stack_heads(pair):
    lane = lax.broadcasted_iota(jnp.int32, pair.shape, 1)
    zero = jnp.zeros_like(pair)
    return jnp.concatenate(
        (jnp.where(lane < HEAD_DIM, pair, zero), jnp.where(lane >= HEAD_DIM, pair, zero)), axis=0
    )


def unstack_heads(stacked):
    half = stacked.shape[0] // 2
    top, bottom = stacked[:half], stacked[half:]
    lane = lax.broadcasted_iota(jnp.int32, top.shape, 1)
    return jnp.where(lane < HEAD_DIM, top, bottom)


def column_of(row):
    return jnp.transpose(jnp.broadcast_to(row, (128, row.shape[1])))


def doubled(mask_value):
    return jnp.concatenate((mask_value, mask_value), axis=1)


def masked_scores(units):
    scores = [dot_nt(key, query) for query, key, _, _ in units]
    scores = [s if unit[2] is None else s + unit[2] for s, unit in zip(scores, units)]
    return [jnp.where(unit[3], s, masked_value) for s, unit in zip(scores, units)]


def attend(units):
    scores = masked_scores([(stack_heads(u[0]), u[1], u[3], u[4]) for u in units])
    peaks = [jnp.max(s, axis=0, keepdims=True) for s in scores]
    terms = [jnp.exp(s - peak) for s, peak in zip(scores, peaks)]
    sums = [jnp.sum(t, axis=0, keepdims=True) for t in terms]
    probs = [(t * (1.0 / total)).astype(bf16) for t, total in zip(terms, sums)]
    mixes = [dot_tn(p, u[2]) for p, u in zip(probs, units)]
    mixes = [unstack_heads(m).astype(bf16) for m in mixes]
    return mixes, [peak + jnp.log(total) for peak, total in zip(peaks, sums)]


def attend_back(units):
    queries = [stack_heads(u[0]) for u in units]
    grads = [stack_heads(u[6]) for u in units]
    scores = masked_scores([(q, u[1], u[3], u[4]) for q, u in zip(queries, units)])
    grad_probs = [dot_nt(u[2], g) for u, g in zip(units, grads)]
    probs = [jnp.exp(s - u[5]) for s, u in zip(scores, units)]
    grad_values = [dot_nn(p.astype(bf16), g).astype(bf16) for p, g in zip(probs, grads)]
    along = [jnp.sum(g * p, axis=0, keepdims=True) for g, p in zip(grad_probs, probs)]
    grad_scores = [p * (g - t) for p, g, t in zip(probs, grad_probs, along)]
    low = [g.astype(bf16) for g in grad_scores]
    grad_keys = [dot_nn(x, q).astype(bf16) for x, q in zip(low, queries)]
    grad_queries = [unstack_heads(dot_tn(x, u[1])).astype(bf16) for x, u in zip(low, units)]
    return grad_queries, grad_keys, grad_values, grad_scores


def weight_copies(slots, weights, tab, sems, first=0):
    copies = []
    for pair in range(PAIRS):
        row = []
        for number, slot in enumerate(slots):
            rows = weights.shape[1] // len(slots)
            start = pl.multiple_of(tab[number] * rows, rows)
            row.append(
                pltpu.make_async_copy(
                    slot.at[pair, pl.ds(0, rows), pl.ds(first, weights.shape[2])],
                    weights.at[pair, pl.ds(start, rows), :],
                    sems.at[number, pair],
                )
            )
        copies.append(row)
    for row in copies:
        for copy in row:
            copy.start()
    return copies


def wait_for(copies):
    for copy in copies:
        copy.wait()


def extra_copies(slots, extras, rows, sems):
    return [
        pltpu.make_async_copy(slot.at[:, pl.ds(rows, EXTRA), pl.ds(0, D)], extras.at[number], sems.at[number])
        for number, slot in enumerate(slots)
    ]


def permute_rows(source, target, tab, n_slots):
    rows = source.shape[0] // n_slots
    for number in range(n_slots):
        start = pl.multiple_of(tab[number] * rows, rows)
        target[number * rows : (number + 1) * rows, :] = source[pl.ds(start, rows), :]


class SlotWriter:
    def __init__(self, outs, held, sems):
        self.outs, self.held, self.sems = outs, held, sems
        self.copies = []

    def send(self, pair, first, rows, sem):
        begin = 0
        for place, out in enumerate(self.outs):
            copy = pltpu.make_async_copy(
                self.held.at[pl.ds(begin, out.shape[0]), pair, pl.ds(first, rows), :],
                out.at[:, pair, pl.ds(first, rows), :],
                self.sems.at[place, sem],
            )
            copy.start()
            self.copies.append(copy)
            begin += out.shape[0]

    def write(self, pair, grads):
        n_slots = self.held.shape[0]
        first = 0
        for grad in grads:
            rows, width = grad.shape[0] // n_slots, grad.shape[1]
            low = grad.astype(bf16)
            for number in range(n_slots):
                part = low[number * rows : (number + 1) * rows]
                self.held[number, pair, 0:rows, first : first + width] = part
            first += width
        self.send(pair, 0, rows, pair)

    def finish(self):
        wait_for(self.copies)


def toeplitz(row, length):
    return pltpu.roll(jnp.broadcast_to(row, (length, row.shape[1])), 0, 1, stride=1, stride_axis=0)


def bias_of(tab, falls, pair, length):
    head = tab[16 + pair] * 2
    return jnp.concatenate(
        [toeplitz(falls[pl.ds(head + side, 1), :], length) for side in range(2)], axis=1
    )


def fold_diagonals(grad):
    length = grad.shape[1]
    folded = grad[0:8]
    for start in range(8, grad.shape[0], 8):
        folded = folded + pltpu.roll(grad[start : start + 8], length - start, 1)
    row = lax.broadcasted_iota(jnp.int32, folded.shape, 0)
    for bit in (1, 2, 4):
        folded = jnp.where(row & bit != 0, pltpu.roll(folded, length - bit, 1), folded)
    return jnp.sum(folded, axis=0, keepdims=True)


def self_masks(tab, targets, row, length):
    segments = targets[pl.ds(tab[24] + row, 1), :].astype(f32)
    column = column_of(segments)
    keys = lax.broadcasted_iota(jnp.int32, (length, length), 0)
    queries = lax.broadcasted_iota(jnp.int32, (length, length), 1)
    return doubled(
        jnp.where((column == segments) & (queries >= keys), 1.0, 0.0)
    ) > 0.5


def cross_masks(tab, targets, sources, row, n_pieces, piece_tab):
    segments = targets[pl.ds(tab[24] + row, 1), :].astype(f32)
    width = sources.shape[1] // n_pieces
    chosen = lax.broadcasted_iota(jnp.int32, (sources.shape[0], width), 0) == tab[24] + row
    parts = []
    for i in range(n_pieces):
        start = pl.multiple_of(tab[piece_tab + i] * width, 128)
        slab = sources[:, pl.ds(start, width)].astype(f32)
        parts.append(jnp.sum(jnp.where(chosen, slab, 0.0), axis=0, keepdims=True))
    column = column_of(jnp.concatenate(parts, axis=1) if n_pieces > 1 else parts[0])
    return doubled(jnp.where(column == segments, 1.0, 0.0)) > 0.5


def self_forward_kernel(n_slots, n_after, rows_held, tab, targets, onehot, x_all, *refs):
    slots, refs = refs[:n_slots], refs[n_slots + n_after :]
    after, normed, query, key, value, mixed, totals, gains, falls = refs[:9]
    weights, extras, x_rows, sems, extra_sems, x_sem = refs[9:]
    length = x_all.shape[1]
    fetch_x = pltpu.make_async_copy(x_all.at[pl.ds(tab[24], rows_held)], x_rows, x_sem)
    fetch_extra = extra_copies(slots, extras, D // n_slots, extra_sems)
    for copy in [fetch_x] + fetch_extra:
        copy.start()
    fetch = weight_copies(slots, weights, tab, sems)
    wait_for(fetch_extra)
    tile = jnp.zeros((EXTRA, D), f32)
    for number in range(n_slots):
        for pair in range(PAIRS):
            tile = tile + extras[number, pair].astype(f32)
    gains[...] = tile[0:8]
    falls[...] = dot_nn(tile[8:16, 0:128].astype(bf16), onehot[...])
    fetch_x.wait()
    resident = x_rows[...].reshape(rows_held * length, D).astype(f32)
    low = (resident * root_scale(resident) * tile[0:1]).astype(bf16)
    normed[...] = low
    allowed = [self_masks(tab, targets, row, length) for row in range(rows_held)]
    total = resident
    for group in GROUPS:
        for pair in group:
            wait_for(fetch[pair])
            projected = dot_nn(low, weights[pair, :, 0 : 3 * PAIR]).astype(bf16)
            query[pair] = projected[:, 0:PAIR]
            key[pair] = projected[:, PAIR : 2 * PAIR]
            value[pair] = projected[:, 2 * PAIR :]
        places = [(pair, row, slice(row * length, (row + 1) * length)) for pair in group for row in range(rows_held)]
        biases = {pair: bias_of(tab, falls, pair, length) for pair in group}
        mixes, logs = attend(
            [
                (query[pair, span], key[pair, span], value[pair, span], biases[pair], allowed[row])
                for pair, row, span in places
            ]
        )
        for (pair, row, span), mix, log_total in zip(places, mixes, logs):
            mixed[pair, span] = mix
            totals[pair, row : row + 1, :] = log_total
        for pair in group:
            total = total + dot_nt(mixed[pair], weights[pair, :, 3 * PAIR :])
    after[...] = total


def encoder_copies(pieces, encoder, tab, rows_held, sems):
    width = encoder.shape[1] // len(pieces)
    copies = []
    for number, piece in enumerate(pieces):
        start = tab[24] if piece.shape[0] > rows_held else 0
        copies.append(
            pltpu.make_async_copy(
                piece.at[pl.ds(start, rows_held)],
                encoder.at[:, pl.ds(number * width, width), :],
                sems.at[number],
            )
        )
    return copies


def cross_forward_kernel(n_slots, n_pieces, rows_held, tab, targets, sources, gains, before, *refs):
    slots, pieces, refs = refs[:n_slots], refs[n_slots : n_slots + n_pieces], refs[n_slots + n_pieces :]
    after, normed, query, key, value, mixed, totals, encoder = refs[:8]
    weights, sems, piece_sems = refs[8:]
    length = before.shape[0] // rows_held
    source_length = sources.shape[1]
    fetch_pieces = encoder_copies(pieces, encoder, tab, rows_held, piece_sems)
    for copy in fetch_pieces:
        copy.start()
    fetch = weight_copies(slots, weights, tab, sems, 4 * PAIR)
    resident = before[...]
    low = (resident * root_scale(resident) * gains[1:2]).astype(bf16)
    normed[...] = low
    allowed = [
        cross_masks(tab, targets, sources, row, n_pieces, 16 if n_pieces > 1 else 28)
        for row in range(rows_held)
    ]
    wait_for(fetch_pieces)
    source = encoder[...].reshape(rows_held * source_length, D)
    total = resident
    for group in GROUPS:
        for pair in group:
            wait_for(fetch[pair])
            query[pair] = dot_nn(low, weights[pair, :, 0:PAIR]).astype(bf16)
            projected = dot_nn(source, weights[pair, :, PAIR : 3 * PAIR]).astype(bf16)
            key[pair] = projected[:, 0:PAIR]
            value[pair] = projected[:, PAIR:]
        places = [(pair, row) for pair in group for row in range(rows_held)]
        spans = [slice(row * length, (row + 1) * length) for row in range(rows_held)]
        wides = [slice(row * source_length, (row + 1) * source_length) for row in range(rows_held)]
        mixes, logs = attend(
            [
                (query[pair, spans[row]], key[pair, wides[row]], value[pair, wides[row]], None, allowed[row])
                for pair, row in places
            ]
        )
        for (pair, row), mix, log_total in zip(places, mixes, logs):
            mixed[pair, spans[row]] = mix
            totals[pair, row : row + 1, :] = log_total
        for pair in group:
            total = total + dot_nt(mixed[pair], weights[pair, :, 3 * PAIR :])
    after[...] = total


def feed_kernel(n_slots, n_outs, rows_held, tab, gains, before, c_all, *refs):
    slots, refs = refs[:n_slots], refs[n_slots:]
    low_out, grad_before, grad_gain = refs[:3]
    outs, refs = refs[3 : 3 + n_outs], refs[3 + n_outs :]
    weights, c_rows, turned, normed_turned, again, c_turned, held, sems, c_sem, out_sems = refs
    fetch_c = pltpu.make_async_copy(c_all.at[pl.ds(tab[24], rows_held)], c_rows, c_sem)
    fetch = weight_copies(slots, weights, tab, sems)
    fetch_c.start()
    resident = before[...]
    gain = gains[2:3]
    low = (resident * root_scale(resident) * gain).astype(bf16)
    turned[...] = jnp.transpose(low)
    permute_rows(turned, normed_turned, tab, n_slots)
    fetch_c.wait()
    cotangent = c_rows[...].reshape(resident.shape)
    again[...] = jnp.transpose(cotangent)
    permute_rows(again, c_turned, tab, n_slots)
    writer = SlotWriter(outs, held, out_sems)
    total = resident
    grad_normed = jnp.zeros_like(resident)
    for pair in range(PAIRS):
        wait_for(fetch[pair])
        inner, outer = weights[pair, :, 0:HIDDEN], weights[pair, :, HIDDEN:]
        u = dot_nn(low, inner)
        squared = u * u
        bent = jnp.tanh(gelu_slope * (u + gelu_cubic * u * squared))
        hidden = (0.5 * u * (1.0 + bent)).astype(bf16)
        slope = 0.5 * (1.0 + bent) + 0.5 * u * (1.0 - bent * bent) * gelu_slope * (
            1.0 + 3.0 * gelu_cubic * squared
        )
        total = total + dot_nt(hidden, outer)
        grad_u = (dot_nn(cotangent, outer) * slope).astype(bf16)
        grad_normed = grad_normed + dot_nt(grad_u, inner)
        writer.write(pair, (dot_nn(normed_turned[...], grad_u), dot_nn(c_turned[...], hidden)))
    low_out[...] = total.astype(bf16)
    through, gain_part = root_back(resident, gain, grad_normed)
    grad_before[...] = cotangent.astype(f32) + through
    grad_gain[...] = gain_part
    writer.finish()


def cross_back_kernel(
    n_slots, n_pieces, rows_held, tab, targets, sources, gains, grad_after, before, *refs
):
    query, key, value, totals = refs[:4]
    slots, refs = refs[4 : 4 + n_slots], refs[4 + n_slots :]
    grad_before, grad_gain, d_query, d_key, d_value, weights, sems = refs
    length = before.shape[0] // rows_held
    source_length = sources.shape[1]
    fetch = weight_copies(slots, weights, tab, sems, 4 * PAIR)
    grad_in = grad_after[...]
    low = grad_in.astype(bf16)
    allowed = [
        cross_masks(tab, targets, sources, row, n_pieces, 16 if n_pieces > 1 else 28)
        for row in range(rows_held)
    ]
    spans = [slice(row * length, (row + 1) * length) for row in range(rows_held)]
    wides = [slice(row * source_length, (row + 1) * source_length) for row in range(rows_held)]
    grad_normed = jnp.zeros_like(grad_in)
    for group in GROUPS:
        wait_for([copy for pair in group for copy in fetch[pair]])
        grad_mixed = {pair: dot_nn(low, weights[pair, :, 3 * PAIR :]).astype(bf16) for pair in group}
        places = [(pair, row) for pair in group for row in range(rows_held)]
        results = attend_back(
            [
                (
                    query[pair, spans[row]],
                    key[pair, wides[row]],
                    value[pair, wides[row]],
                    None,
                    allowed[row],
                    totals[pair, row : row + 1, :],
                    grad_mixed[pair][spans[row]],
                )
                for pair, row in places
            ]
        )
        for (pair, row), one, two, three, _ in zip(places, *results):
            d_query[pair, spans[row]] = one
            d_key[pair, wides[row]] = two
            d_value[pair, wides[row]] = three
        for pair in group:
            grad_normed = grad_normed + dot_nt(d_query[pair], weights[pair, :, 0:PAIR])
    through, gain_part = root_back(before[...], gains[1:2], grad_normed)
    grad_before[...] = grad_in + through
    grad_gain[...] = gain_part


def cross_weights_kernel(
    n_slots, n_outs, n_after, tab, grad_after, normed, mixed, encoder, d_query, d_key, d_value, *refs
):
    refs = refs[n_after:]
    outs, refs = refs[:n_outs], refs[n_outs:]
    turned, low_turned, again, normed_turned, wide_turned, encoder_turned, held, out_sems = refs
    writer = SlotWriter(outs, held, out_sems)
    turned[...] = jnp.transpose(grad_after[...].astype(bf16))
    permute_rows(turned, low_turned, tab, n_slots)
    again[...] = jnp.transpose(normed[...])
    permute_rows(again, normed_turned, tab, n_slots)
    wide_turned[...] = jnp.transpose(encoder[...].reshape(wide_turned.shape[1], D))
    permute_rows(wide_turned, encoder_turned, tab, n_slots)
    for pair in range(PAIRS):
        writer.write(
            pair,
            (
                dot_nn(normed_turned[...], d_query[pair]),
                dot_nn(encoder_turned[...], d_key[pair]),
                dot_nn(encoder_turned[...], d_value[pair]),
                dot_nn(low_turned[...], mixed[pair]),
            ),
        )
    writer.finish()


def self_back_kernel(
    n_slots, n_outs, n_after, rows_held, tab, targets, onehot, gains, falls, gain_two, gain_three, grad_after, x_all, *refs
):
    normed, query, key, value, mixed, totals = refs[:6]
    slots, refs = refs[6 : 6 + n_slots], refs[6 + n_slots + n_after :]
    low_grad = refs[0]
    outs, refs = refs[1 : 1 + n_outs], refs[1 + n_outs :]
    weights, x_rows, turned, low_turned, again, normed_turned, bias_rows, held, sems, x_sem, out_sems = refs
    writer = SlotWriter(outs, held, out_sems)
    length = x_all.shape[1]
    fetch_x = pltpu.make_async_copy(x_all.at[pl.ds(tab[24], rows_held)], x_rows, x_sem)
    fetch = weight_copies(slots, weights, tab, sems)
    fetch_x.start()
    grad_in = grad_after[...]
    low = grad_in.astype(bf16)
    turned[...] = jnp.transpose(low)
    permute_rows(turned, low_turned, tab, n_slots)
    again[...] = jnp.transpose(normed[...])
    permute_rows(again, normed_turned, tab, n_slots)
    allowed = [self_masks(tab, targets, row, length) for row in range(rows_held)]
    grad_normed = jnp.zeros_like(grad_in)
    spans = [slice(row * length, (row + 1) * length) for row in range(rows_held)]
    for group in GROUPS:
        wait_for([copy for pair in group for copy in fetch[pair]])
        grad_mixed = {pair: dot_nn(low, weights[pair, :, 3 * PAIR :]).astype(bf16) for pair in group}
        biases = {pair: bias_of(tab, falls, pair, length) for pair in group}
        places = [(pair, row) for pair in group for row in range(rows_held)]
        results = attend_back(
            [
                (
                    query[pair, spans[row]],
                    key[pair, spans[row]],
                    value[pair, spans[row]],
                    biases[pair],
                    allowed[row],
                    totals[pair, row : row + 1, :],
                    grad_mixed[pair][spans[row]],
                )
                for pair, row in places
            ]
        )
        parts = {place: result for place, *result in zip(places, *results)}
        for pair in group:
            joined = [jnp.concatenate(parts[pair, row][:3], axis=1) for row in range(rows_held)]
            joined = jnp.concatenate(joined, axis=0) if rows_held > 1 else joined[0]
            grad_normed = grad_normed + dot_nt(joined, weights[pair, :, 0 : 3 * PAIR])
            writer.write(
                pair, (dot_nn(normed_turned[...], joined), dot_nn(low_turned[...], mixed[pair]))
            )
            grad_bias = sum(parts[pair, row][3] for row in range(rows_held))
            for side in range(2):
                diagonal = fold_diagonals(grad_bias[:, side * length : (side + 1) * length])
                bias_rows[pl.ds(tab[16 + pair] * 2 + side, 1), :] = diagonal
    fetch_x.wait()
    resident = x_rows[...].reshape(grad_in.shape).astype(f32)
    through, gain_one = root_back(resident, gains[0:1], grad_normed)
    low_grad[...] = (grad_in + through).astype(bf16)
    table = lax.dot_general(
        bias_rows[...],
        onehot[...].astype(f32),
        (((1,), (1,)), ((), ())),
        precision=lax.Precision.HIGHEST,
        preferred_element_type=f32,
    )
    blank = jnp.zeros((5, D), f32)
    table = jnp.concatenate((table, jnp.zeros((8, D - 128), f32)), axis=1)
    tile = jnp.concatenate((gain_one, gain_two[...], gain_three[...], blank, table), axis=0).astype(bf16)
    rows = D // n_slots
    for pair in range(PAIRS):
        for number in range(n_slots):
            held[number, pair, rows : rows + EXTRA, :] = tile
        writer.send(pair, rows, EXTRA, PAIRS + pair)
    writer.finish()


def pack_attention_kernel(n_dp, tab, query, keyval, output, gains, table, own):
    rows, width = query.shape[1], gains.shape[1]
    place_dp, place_mp = tab[25], tab[26]
    parts = []
    for number in range(2):
        parts += [query[number], keyval[number, 0], keyval[number, 1], output[number]]
    own[0:rows, :] = jnp.concatenate(parts, axis=1).astype(bf16)
    wide = jnp.concatenate([gains[...]] * n_dp, axis=1)
    lane = lax.broadcasted_iota(jnp.int32, wide.shape, 1)
    wide = jnp.where((lane // width == place_dp) & (place_mp == 0), wide, 0.0)
    heads, bands = table.shape
    lane = lax.broadcasted_iota(jnp.int32, (bands, D), 1)
    band = lax.broadcasted_iota(jnp.int32, (bands, D), 0)
    at_band = jnp.where(lane == place_dp * bands + band, 1.0, 0.0).astype(bf16)
    head = lax.broadcasted_iota(jnp.int32, (HEADS, heads), 0)
    column = lax.broadcasted_iota(jnp.int32, (HEADS, heads), 1)
    at_head = jnp.where(head == place_mp * heads + column, 1.0, 0.0).astype(bf16)
    placed = dot_nn(at_head, dot_nn(table[...].astype(bf16), at_band).astype(bf16))
    blank = jnp.zeros((HEADS - wide.shape[0], D), f32)
    tile = jnp.concatenate((wide, blank, placed), axis=0).astype(bf16)
    own[rows : rows + EXTRA, 0:D] = tile
    own[rows : rows + EXTRA, D:] = jnp.zeros_like(tile)


def pack_feed_kernel(inner, outer, *refs):
    refs[-1][...] = jnp.concatenate((inner[...], outer[...]), axis=1).astype(bf16)


def split_encoder_kernel(rows_held, tab, encoder, *refs):
    outs, sems = refs[:-1], refs[-1]
    copies = [
        pltpu.make_async_copy(
            encoder.at[pl.ds(tab[17 + number] * rows_held, rows_held)], out, sems.at[number]
        )
        for number, out in enumerate(outs)
    ]
    for copy in copies:
        copy.start()
    for copy in copies:
        copy.wait()


def stack_kernel(count, *refs):
    out = refs[-1]
    for number in range(count):
        out[number] = refs[number][...]


def stack_through_kernel(count, *refs):
    stack_kernel(count, *refs[:-1])


def spread_kernel(rows_held, tab, *refs):
    for side, out in enumerate(refs[-2:]):
        for number, piece in enumerate(refs[4 * side : 4 * side + 4]):
            out[pl.ds(tab[16 + number] * rows_held, rows_held)] = piece[...]


def shape(dims, dtype):
    return jax.ShapeDtypeStruct(dims, dtype)


def dma_sems(*counts):
    return pltpu.SemaphoreType.DMA(counts)


def anys(arrays):
    return [(array, "any") for array in arrays]


def vmems(arrays):
    return [(array, "vmem") for array in arrays]


def call(kernel, operands, outs, scratch, micros=1, aliases=None, any_outs=(), room=2):
    spaces = {"smem": pltpu.SMEM, "vmem": pltpu.VMEM, "any": pl.ANY}
    arrays = [array for array, _ in operands]
    held = [a for a, place in operands if place == "vmem"]
    held += [o for i, o in enumerate(outs) if i not in any_outs and i not in (aliases or {}).values()]
    held += [x for x in scratch if hasattr(x, "shape") and hasattr(x, "dtype") and x.dtype in (f32, bf16)]
    vmem = sum(math.prod(x.shape) * jnp.dtype(x.dtype).itemsize for x in held) + room * 2**20
    moved = sum(a.size * a.dtype.itemsize for a in arrays) + sum(
        math.prod(o.shape) * o.dtype.itemsize for o in outs
    )
    return pl.pallas_call(
        kernel,
        out_shape=tuple(outs),
        in_specs=[pl.BlockSpec(memory_space=spaces[place]) for _, place in operands],
        out_specs=tuple(
            pl.BlockSpec(memory_space=pl.ANY if i in any_outs or i in (aliases or {}).values() else pltpu.VMEM)
            for i in range(len(outs))
        ),
        input_output_aliases=aliases or {},
        scratch_shapes=scratch,
        compiler_params=pltpu.CompilerParams(vmem_limit_bytes=min(vmem, VMEM_BYTES)),
        cost_estimate=pl.CostEstimate(flops=int(micros * 1.15e9), bytes_accessed=moved if micros else 0, transcendentals=0),
    )(*arrays)


def bucket_onehot(length):
    distance = np.arange(length)
    bucket = np.minimum(distance, 16)
    for edge_value in bucket_edges:
        bucket = bucket + (distance >= edge_value)
    return jnp.asarray(np.arange(128)[:, None] == bucket[None, :], bf16)


def adam_step(weight, first, second, grad, rate, decay):
    new_first = beta_first * first + (1.0 - beta_first) * grad
    new_second = beta_second * second + (1.0 - beta_second) * grad * grad
    ratio = (
        new_first
        / (1.0 - beta_first**STEP)
        / (jnp.sqrt(new_second / (1.0 - beta_second**STEP)) + adam_eps)
    )
    return (new_first, new_second, weight - rate * (ratio + decay * weight))


def step_rates():
    return (
        rate_factor * (16 * D) ** (-0.5),
        rate_factor * D ** (-0.5),
        rate_factor * (HD // 8) ** (-0.5),
        rate_factor * D ** (-0.5),
        rate_factor * (FF // 2) ** (-0.5),
        rate_factor,
        rate_factor,
    )


def gate_kernel(*refs):
    pass


def gate(array, after, micros=1):
    (same,) = call(
        gate_kernel,
        anys([array] + list(after)),
        [shape(array.shape, array.dtype)],
        [],
        micros=micros,
        aliases={0: 0},
    )
    return same


def fold_kernel(arrived, kept, *refs):
    sent, stays = refs[-2:]
    half = arrived.shape[0] // 2
    both = [(arrived[i : i + half], kept[i : i + half]) for i in (half, 0)]
    for out, (x, y) in zip((sent, stays), both):
        out[...] = (x.astype(f32) + y.astype(f32)).astype(bf16).reshape(out.shape)


def fold(arrived, kept, after=(), plain=True, micros=1):
    half = arrived.shape[0] // 2
    dims = ((half,) if half > 1 else ()) + arrived.shape[1:]
    if not plain:
        return call(
            fold_kernel, vmems((arrived, kept)) + anys(after), [shape(dims, bf16)] * 2, [], micros=0
        )
    if after:
        kept = gate(kept, after, micros)
    parts = [(arrived[i : i + half].reshape(dims), kept[i : i + half].reshape(dims)) for i in (half, 0)]
    return [(x.astype(f32) + y.astype(f32)).astype(bf16) for x, y in parts]


class TreePlan:
    n_slots = 8
    out_slots = (4, 4)
    order = (0, 2, 1, 3)

    def __init__(self, n_dp, n_mp):
        self.n_dp, self.n_mp = n_dp, n_mp

    def pairs(self, target):
        n_mp = self.n_mp
        return [
            (d * n_mp + m, t * n_mp + s)
            for d in range(self.n_dp)
            for m in range(n_mp)
            for t, s in (target(d, m),)
        ]

    def hop_z(self, array, number):
        return lax.ppermute(array, ALL, self.pairs(lambda d, m: (d, m ^ number)))

    def hop_core(self, array):
        return lax.ppermute(array, ALL, self.pairs(lambda d, m: (d ^ 1, m)))

    def hop_first(self, array):
        return lax.ppermute(array, ALL, self.pairs(lambda d, m: (d ^ (4 if d & 1 else 2), m)))

    def hop_second(self, array):
        return lax.ppermute(array, ALL, self.pairs(lambda d, m: (d ^ (2 if d & 1 else 4), m)))

    def table(self, place_dp, place_mp, rows_held):
        core = place_dp & 1
        first, second = 2 + 2 * core, 4 - 2 * core
        own = [place_dp ^ (a * first) ^ (b * second) for b in range(2) for a in range(2)]
        peer = [place_dp ^ 1 ^ (a * second) ^ (b * first) for b in range(2) for a in range(2)]
        return own + peer, [place_mp ^ j for j in self.order]

    def along_z(self, own):
        return [own, self.hop_z(own, 2), self.hop_z(own, 1)]

    def whole_z(self, pieces, after=()):
        own, across, near = pieces
        if after:
            across = gate(across, after)
        return [own, across, near, self.hop_z(across, 1)]

    def stack(self, pieces, after=()):
        (base,) = call(
            functools.partial(stack_kernel, len(pieces)),
            vmems(pieces) + anys(after),
            [shape((len(pieces),) + pieces[0].shape, bf16)],
            [],
        )
        return base

    def stack_through(self, pieces, through):
        return call(
            functools.partial(stack_through_kernel, len(pieces)),
            vmems(pieces) + anys([through]),
            [shape((len(pieces),) + pieces[0].shape, bf16), shape(through.shape, bf16)],
            [],
            aliases={len(pieces): 1},
        )

    def in_plane(self, base, near, far):
        slots = [base, near, far, self.hop_second(near)]
        return slots + [self.hop_core(slot) for slot in slots]

    def attention_shard(self, tab, query, keyval, output, gains, table):
        rows, columns = query.shape[1:]
        (own,) = call(
            functools.partial(pack_attention_kernel, self.n_dp),
            [(tab, "smem")] + vmems((query, keyval, output, gains, table)),
            [shape((rows + EXTRA, 8 * columns), bf16)],
            [],
            room=56,
        )
        return own

    def feed_shard(self, inner, outer, after):
        (own,) = call(
            pack_feed_kernel,
            vmems((inner, outer)) + anys(after),
            [shape((inner.shape[0], 2 * inner.shape[1]), bf16)],
            [],
        )
        return own

    def weights(self, tab, query, keyval, output, inner, outer, gains, table, encoder, rows_held):
        attention = self.whole_z(
            self.along_z(self.attention_shard(tab, query, keyval, output, gains, table))
        )
        parts = call(
            functools.partial(split_encoder_kernel, rows_held),
            [(tab, "smem")] + anys([encoder]),
            [shape((rows_held,) + encoder.shape[1:], bf16)] * 3,
            [dma_sems(3)],
        )
        own_feed = self.feed_shard(inner, outer, [attention[1], parts[0]])
        feed = self.whole_z(self.along_z(own_feed))
        base = self.stack(attention, [own_feed])
        near, far = self.hop_first(base), self.hop_second(base)
        feed_base, near = self.stack_through(feed, near)
        attention = self.in_plane(base, near, far)
        sources = [encoder] + [self.hop_z(part, j) for part, j in zip(parts, self.order[1:])]
        feed = self.in_plane(feed_base, self.hop_first(feed_base), self.hop_second(feed_base))
        return attention, feed, sources, feed_base

    def reduce_core(self, parts, *how):
        own, peer = parts
        return fold(self.hop_core(peer), own, *how)

    def reduce_second(self, pair, *how):
        return fold(self.hop_second(pair[0]), pair[1], *how)

    def reduce_first(self, pair, *how):
        return fold(self.hop_first(pair[0]), pair[1], *how)

    def reduce_near(self, pair, *how):
        return fold(self.hop_z(pair[0], 1), pair[1], *how)

    def reduce_across(self, pair, after=()):
        sent, kept = pair
        if after:
            kept = gate(kept, after)
        total = self.hop_z(sent, 2).astype(f32) + kept.astype(f32)
        return total, total[D // self.n_dp :]

    def finish(self, tab, outputs, row_grads, feed, cross, own):
        row_grads = self.along_z(row_grads)
        feed = self.reduce_first(feed, [cross[0]])
        own = self.reduce_second(own, [feed[0]])
        cross = self.reduce_core(cross, [own[0], outputs[3]] + row_grads[1:], True, 20)
        row_grads = self.whole_z(row_grads, [cross[0]])
        feed = self.reduce_near(feed, [cross[0]])
        own = self.reduce_first(own, [feed[0]])
        cross = self.reduce_second(cross, [own[0]])
        feed = self.reduce_across(feed, [cross[0]])
        own = self.reduce_near(own, [cross[0]])
        cross = self.reduce_first(cross, [own[0]])
        cross = self.reduce_near(cross)
        own = self.reduce_across(own, [cross[0]])
        return self.spread(tab, outputs + row_grads, [own[0]]), [feed, self.reduce_across(cross), own]

    def spread(self, tab, pieces, after):
        rows_held = pieces[0].shape[0]
        out = shape((rows_held * self.n_mp,) + pieces[0].shape[1:], pieces[0].dtype)
        return call(
            functools.partial(spread_kernel, rows_held),
            [(tab, "smem")] + vmems(pieces) + anys(after),
            [out, out],
            [],
            micros=0,
        )


class PlainPlan:
    n_slots = 1
    out_slots = (1,)

    def __init__(self, n_dp, n_mp):
        self.n_dp, self.n_mp = n_dp, n_mp

    def table(self, place_dp, place_mp, rows_held):
        return [0], [0, 1, 2, 3]

    def gather(self, own, kinds):
        full = lax.all_gather(own, ("mp", "dp"), axis=0, tiled=True)
        full = full.reshape(self.n_mp, D, kinds, -1).transpose(2, 1, 0, 3)
        return full.reshape(kinds, D, PAIRS, -1).transpose(2, 1, 0, 3).reshape(PAIRS, D, -1)

    def weights(self, tab, query, keyval, output, inner, outer, gains, table, encoder, rows_held):
        place_dp, place_mp = lax.axis_index("dp"), lax.axis_index("mp")
        parts = []
        for i in range(2):
            parts += [query[i], keyval[i, 0], keyval[i, 1], output[i]]
        attention = self.gather(jnp.concatenate(parts, axis=1).astype(bf16), 8)
        feed = self.gather(jnp.concatenate((inner, outer), axis=1).astype(bf16), 2)
        width = gains.shape[1]
        tile = jnp.zeros((EXTRA, D), f32)
        spot = jnp.where(place_mp == 0, gains, 0.0)
        tile = lax.dynamic_update_slice(tile, spot, (0, place_dp * width))
        heads, bands = table.shape
        tile = lax.dynamic_update_slice(tile, table, (8 + place_mp * heads, place_dp * bands))
        tile = lax.psum(tile.astype(bf16).astype(f32), ALL).astype(bf16)
        tile = jnp.concatenate((tile, jnp.zeros_like(tile)), axis=1)[None]
        tile = jnp.concatenate((tile, jnp.zeros((PAIRS - 1,) + tile.shape[1:], bf16)))
        sources = lax.all_to_all(encoder, "mp", split_axis=0, concat_axis=1, tiled=True)
        return [jnp.concatenate((attention, tile), axis=1)], [feed], [sources], feed

    def reduce_core(self, parts, *how):
        return parts

    def reduce(self, grads):
        kinds = 4 if grads.shape[2] == 4 * PAIR else 2
        full = grads[:, :D].reshape(PAIRS, D, kinds, -1).transpose(2, 1, 0, 3)
        full = full.reshape(kinds, D, self.n_mp, -1).transpose(2, 1, 0, 3)
        total = lax.psum_scatter(
            full.reshape(self.n_mp * D, -1), ("mp", "dp"), scatter_dimension=0, tiled=True
        ).astype(f32)
        return total, lax.psum(grads[0, D:].astype(f32), ALL) if grads.shape[1] > D else None

    def along_z(self, own):
        return [own]

    def finish(self, tab, outputs, row_grads, feed, cross, own):
        rows = [lax.all_gather(x, "mp", axis=0, tiled=True) for x in (outputs[0], row_grads)]
        return rows, [self.reduce(parts[0][0]) for parts in (feed, cross, own)]

    def reduce_second(self, parts, after):
        return parts

    def whole_z(self, pieces, after):
        return pieces


def shards(
    plan,
    inputs,
    encoder,
    cotangent,
    target_segments,
    encoder_segments,
    query_weight,
    query_first,
    query_second,
    keyval_weight,
    keyval_first,
    keyval_second,
    output_weight,
    output_first,
    output_second,
    inner_weight,
    inner_first,
    inner_second,
    outer_weight,
    outer_first,
    outer_second,
    gains,
    gains_first,
    gains_second,
    bias_table,
    table_first,
    table_second,
):
    n_slots, out_slots = plan.n_slots, plan.out_slots
    n_outs = len(out_slots)
    seq_count, length, _ = inputs.shape
    source_length = encoder_segments.shape[1]
    rows_held = seq_count // plan.n_mp
    tokens, sources = rows_held * length, rows_held * source_length
    place_dp, place_mp = lax.axis_index("dp"), lax.axis_index("mp")
    slot_table, pair_table = plan.table(place_dp, place_mp, rows_held)
    entries = slot_table + [0] * (16 - len(slot_table)) + pair_table + [0] * 4
    entries = entries + [place_mp * rows_held, place_dp, place_mp] + [0] * 5
    tab = jnp.stack([jnp.asarray(entry, jnp.int32) for entry in entries])
    onehot = bucket_onehot(length)
    attn_slots, feed_slots, pieces, feed_base = plan.weights(
        tab,
        query_weight,
        keyval_weight,
        output_weight.transpose(0, 2, 1),
        inner_weight,
        outer_weight.T,
        gains,
        bias_table.T,
        encoder,
        rows_held,
    )
    n_pieces = len(pieces)
    rows, columns = query_weight.shape[1:]
    width = gains.shape[1]
    bands, heads = bias_table.shape

    flat = (tokens, D)
    paired = (PAIRS, tokens, PAIR)
    wide = (PAIRS, sources, PAIR)
    stats = shape((PAIRS, rows_held, 2 * length), f32)
    attn_weights = VM((PAIRS, D, 4 * PAIR), bf16)

    after_self, normed_one, q_one, k_one, v_one, mix_one, sum_one, gain_rows, falls = call(
        functools.partial(self_forward_kernel, n_slots, 1, rows_held),
        [(tab, "smem")] + vmems((target_segments, onehot)) + anys([inputs] + attn_slots + [feed_base]),
        [shape(flat, f32), shape(flat, bf16)]
        + [shape(paired, bf16)] * 4
        + [stats, shape((8, D), f32), shape((8, length), f32)],
        [
            attn_weights,
            VM((n_slots, PAIRS, EXTRA, D), bf16),
            VM((rows_held, length, D), bf16),
            dma_sems(n_slots, PAIRS),
            dma_sems(n_slots),
            pltpu.SemaphoreType.DMA,
        ],
        room=56,
        micros=30,
    )
    after_cross, normed_two, q_two, k_two, v_two, mix_two, sum_two, source_rows = call(
        functools.partial(cross_forward_kernel, n_slots, n_pieces, rows_held),
        [(tab, "smem")]
        + vmems((target_segments, encoder_segments, gain_rows, after_self))
        + anys(attn_slots + pieces),
        [
            shape(flat, f32),
            shape(flat, bf16),
            shape(paired, bf16),
            shape(wide, bf16),
            shape(wide, bf16),
            shape(paired, bf16),
            stats,
            shape((rows_held, source_length, D), bf16),
        ],
        [attn_weights, dma_sems(n_slots, PAIRS), dma_sems(n_pieces)],
        room=56,
        micros=11,
    )

    def grad_outs(extra, width_out):
        return [
            shape((count, PAIRS, D // n_slots + extra, width_out), bf16) for count in out_slots
        ]

    feed_result = call(
        functools.partial(feed_kernel, n_slots, n_outs, rows_held),
        [(tab, "smem")] + vmems((gain_rows, after_cross)) + anys([cotangent] + feed_slots),
        [shape(flat, bf16), shape(flat, f32), shape((1, D), f32)] + grad_outs(0, 2 * HIDDEN),
        [
            VM((PAIRS, D, 2 * HIDDEN), bf16),
            VM((rows_held, length, D), bf16),
            VM((D, tokens), bf16),
            VM((D, tokens), bf16),
            VM((D, tokens), bf16),
            VM((D, tokens), bf16),
            VM((n_slots, PAIRS, D // n_slots, 2 * HIDDEN), bf16),
            dma_sems(n_slots, PAIRS),
            pltpu.SemaphoreType.DMA,
            dma_sems(n_outs, PAIRS),
        ],
        any_outs=range(3, 3 + n_outs),
        room=56,
        micros=10,
    )
    low_out, grad_second, gain_three = feed_result[:3]
    core_feed = plan.reduce_core(feed_result[3:])
    grad_first, gain_two, dq_two, dk_two, dv_two = call(
        functools.partial(cross_back_kernel, n_slots, n_pieces, rows_held),
        [(tab, "smem")]
        + vmems((target_segments, encoder_segments, gain_rows, grad_second, after_self))
        + vmems((q_two, k_two, v_two, sum_two))
        + anys(attn_slots),
        [shape(flat, f32), shape((1, D), f32), shape(paired, bf16), shape(wide, bf16), shape(wide, bf16)],
        [attn_weights, dma_sems(n_slots, PAIRS)],
        room=56,
        micros=10,
    )
    self_result = call(
        functools.partial(self_back_kernel, n_slots, n_outs, 1, rows_held),
        [(tab, "smem")]
        + vmems((target_segments, onehot, gain_rows, falls, gain_two, gain_three, grad_first))
        + anys([inputs])
        + vmems((normed_one, q_one, k_one, v_one, mix_one, sum_one))
        + anys(attn_slots + [core_feed[0]]),
        [shape(flat, bf16)] + grad_outs(EXTRA, 4 * PAIR),
        [
            attn_weights,
            VM((rows_held, length, D), bf16),
            VM((D, tokens), bf16),
            VM((D, tokens), bf16),
            VM((D, tokens), bf16),
            VM((D, tokens), bf16),
            VM((8, length), f32),
            VM((n_slots, PAIRS, D // n_slots + EXTRA, 4 * PAIR), bf16),
            dma_sems(n_slots, PAIRS),
            pltpu.SemaphoreType.DMA,
            dma_sems(n_outs, 2 * PAIRS),
        ],
        any_outs=range(1, 1 + n_outs),
        room=12,
        micros=10,
    )
    out_pieces = plan.along_z(gate(low_out.reshape(rows_held, length, D), [core_feed[0]]))
    second_feed = plan.reduce_second(core_feed, out_pieces[1:])
    core_self = plan.reduce_core(self_result[1:], second_feed[:1], True, 20)
    out_pieces = plan.whole_z(out_pieces, second_feed[:1])
    cross_grads = call(
        functools.partial(cross_weights_kernel, n_slots, n_outs, 2),
        [(tab, "smem")]
        + vmems((grad_second, normed_two, mix_two, source_rows, dq_two, dk_two, dv_two))
        + anys([second_feed[0], core_self[0]]),
        grad_outs(0, 4 * PAIR),
        [
            VM((D, tokens), bf16),
            VM((D, tokens), bf16),
            VM((D, tokens), bf16),
            VM((D, tokens), bf16),
            VM((D, sources), bf16),
            VM((D, sources), bf16),
            VM((n_slots, PAIRS, D // n_slots, 4 * PAIR), bf16),
            dma_sems(n_outs, PAIRS),
        ],
        any_outs=range(n_outs),
        room=12,
        micros=7,
    )
    (outputs, input_grad), ((grad_feed, _), (grad_cross, _), (grad_self, tile)) = plan.finish(
        tab, out_pieces, self_result[0].reshape(rows_held, length, D), second_feed, cross_grads, core_self
    )

    def kind(grads, number):
        return grads[:rows, number * columns : (number + 1) * columns]

    hidden = inner_weight.shape[1]
    grads = (
        jnp.stack((kind(grad_self, 0), kind(grad_cross, 0))),
        jnp.stack(
            (
                jnp.stack((kind(grad_self, 1), kind(grad_self, 2))),
                jnp.stack((kind(grad_cross, 1), kind(grad_cross, 2))),
            )
        ),
        jnp.stack((kind(grad_self, 3).T, kind(grad_cross, 3).T)),
        grad_feed[:, :hidden],
        grad_feed[:, hidden:].T,
        lax.dynamic_slice_in_dim(tile[0:3], place_dp * width, width, 1),
        lax.dynamic_slice(tile, (8 + place_mp * heads, place_dp * bands), (heads, bands)).T,
    )
    params = (
        query_weight,
        keyval_weight,
        output_weight,
        inner_weight,
        outer_weight,
        gains,
        bias_table,
    )
    firsts = (
        query_first,
        keyval_first,
        output_first,
        inner_first,
        outer_first,
        gains_first,
        table_first,
    )
    seconds = (
        query_second,
        keyval_second,
        output_second,
        inner_second,
        outer_second,
        gains_second,
        table_second,
    )
    updated = [
        adam_step(*param_entry)
        for param_entry in zip(params, firsts, seconds, grads, step_rates(), step_decays)
    ]
    return (outputs, input_grad) + tuple(array for triple in updated for array in triple)


def solution(mesh):
    n_dp, n_mp = mesh.shape["dp"], mesh.shape["mp"]
    plan = (TreePlan if (n_dp, n_mp) == (8, 4) else PlainPlan)(n_dp, n_mp)
    by_query, by_keyval = P(None, "dp", "mp"), P(None, None, "dp", "mp")
    by_output, by_inner, by_outer = P(None, "mp", "dp"), P("dp", "mp"), P("mp", "dp")
    weights = (by_query,) * 3 + (by_keyval,) * 3 + (by_output,) * 3 + (by_inner,) * 3
    weights = weights + (by_outer,) * 3 + (P(None, "dp"),) * 3 + (P("dp", "mp"),) * 3
    tokens = P("dp", None, None)
    return jax.shard_map(
        functools.partial(shards, plan),
        mesh=mesh,
        in_specs=(tokens, P("dp", "mp", None), tokens, P("dp", None), P("dp", None)) + weights,
        out_specs=(tokens, tokens) + weights,
        check_vma=False,
    )
```

```python
import functools
import math

import jax
import jax.numpy as jnp
import numpy as np
from jax import lax
from jax.experimental import pallas as pl
from jax.experimental.pallas import tpu as pltpu
from jax.sharding import PartitionSpec as P

D = 512
HEADS = 8
HEAD_DIM = 64
FF = 2048
NB = 32
HD = 512
STEP = 10
PAIRS = HEADS // 2
PAIR = 2 * HEAD_DIM
HIDDEN = FF // PAIRS
EXTRA = 16
GROUPS = (tuple(range(PAIRS)),)
VMEM_BYTES = 56 * 1024 * 1024

norm_eps = 1e-06
beta_first = 0.9
beta_second = 0.95
adam_eps = 1e-08
decay_weight = 0.1
rate_factor = 0.6
masked_value = -1000000000.0
bucket_edges = tuple((math.ceil(16 * 8 ** (number / 16)) for number in range(1, 16)))
step_decays = (decay_weight, decay_weight, decay_weight, decay_weight, decay_weight, 0.0, 0.0)
gelu_slope = math.sqrt(2.0 / math.pi)
gelu_cubic = 0.044715

f32 = jnp.float32
bf16 = jnp.bfloat16
ALL = ("dp", "mp")
VM = pltpu.VMEM


def dot_nn(a, b):
    return lax.dot_general(a, b, (((1,), (0,)), ((), ())), preferred_element_type=f32)


def dot_nt(a, b):
    return lax.dot_general(a, b, (((1,), (1,)), ((), ())), preferred_element_type=f32)


def dot_tn(a, b):
    return lax.dot_general(a, b, (((0,), (0,)), ((), ())), preferred_element_type=f32)


def root_scale(values):
    return lax.rsqrt(jnp.mean(values * values, axis=-1, keepdims=True) + norm_eps)


def root_back(values, gain, grad):
    scale = root_scale(values)
    grad_gain = jnp.sum(grad * values * scale, axis=0, keepdims=True)
    weighted = grad * gain
    along = jnp.sum(weighted * values, axis=-1, keepdims=True)
    inverse = 1.0 / values.shape[-1]
    return scale * weighted - values * (scale * scale * scale * along * inverse), grad_gain


def stack_heads(pair):
    lane = lax.broadcasted_iota(jnp.int32, pair.shape, 1)
    zero = jnp.zeros_like(pair)
    return jnp.concatenate(
        (jnp.where(lane < HEAD_DIM, pair, zero), jnp.where(lane >= HEAD_DIM, pair, zero)), axis=0
    )


def unstack_heads(stacked):
    half = stacked.shape[0] // 2
    top, bottom = stacked[:half], stacked[half:]
    lane = lax.broadcasted_iota(jnp.int32, top.shape, 1)
    return jnp.where(lane < HEAD_DIM, top, bottom)


def column_of(row):
    return jnp.transpose(jnp.broadcast_to(row, (128, row.shape[1])))


def doubled(mask_value):
    return jnp.concatenate((mask_value, mask_value), axis=1)


def masked_scores(units):
    scores = [dot_nt(key, query) for query, key, _, _ in units]
    scores = [s if unit[2] is None else s + unit[2] for s, unit in zip(scores, units)]
    return [jnp.where(unit[3], s, masked_value) for s, unit in zip(scores, units)]


def attend(units):
    scores = masked_scores([(stack_heads(u[0]), u[1], u[3], u[4]) for u in units])
    peaks = [jnp.max(s, axis=0, keepdims=True) for s in scores]
    terms = [jnp.exp(s - peak) for s, peak in zip(scores, peaks)]
    sums = [jnp.sum(t, axis=0, keepdims=True) for t in terms]
    probs = [(t * (1.0 / total)).astype(bf16) for t, total in zip(terms, sums)]
    mixes = [dot_tn(p, u[2]) for p, u in zip(probs, units)]
    mixes = [unstack_heads(m).astype(bf16) for m in mixes]
    return mixes, [peak + jnp.log(total) for peak, total in zip(peaks, sums)]


def attend_back(units):
    queries = [stack_heads(u[0]) for u in units]
    grads = [stack_heads(u[6]) for u in units]
    scores = masked_scores([(q, u[1], u[3], u[4]) for q, u in zip(queries, units)])
    grad_probs = [dot_nt(u[2], g) for u, g in zip(units, grads)]
    probs = [jnp.exp(s - u[5]) for s, u in zip(scores, units)]
    grad_values = [dot_nn(p.astype(bf16), g).astype(bf16) for p, g in zip(probs, grads)]
    along = [jnp.sum(g * p, axis=0, keepdims=True) for g, p in zip(grad_probs, probs)]
    grad_scores = [p * (g - t) for p, g, t in zip(probs, grad_probs, along)]
    low = [g.astype(bf16) for g in grad_scores]
    grad_keys = [dot_nn(x, q).astype(bf16) for x, q in zip(low, queries)]
    grad_queries = [unstack_heads(dot_tn(x, u[1])).astype(bf16) for x, u in zip(low, units)]
    return grad_queries, grad_keys, grad_values, grad_scores


def weight_copies(slots, weights, tab, sems, first=0):
    copies = []
    for number, slot in enumerate(slots):
        rows = weights.shape[1] // len(slots)
        start = pl.multiple_of(tab[number] * rows, rows)
        copies.append(
            pltpu.make_async_copy(
                slot.at[:, pl.ds(0, rows), pl.ds(first, weights.shape[2])],
                weights.at[:, pl.ds(start, rows), :],
                sems.at[number, 0],
            )
        )
    for copy in copies:
        copy.start()
    return [copies] + [[]] * (PAIRS - 1)


def wait_for(copies):
    for copy in copies:
        copy.wait()


def extra_copies(slots, extras, rows, sems):
    return [
        pltpu.make_async_copy(slot.at[:, pl.ds(rows, EXTRA), pl.ds(0, D)], extras.at[number], sems.at[number])
        for number, slot in enumerate(slots)
    ]


def permute_rows(source, target, tab, n_slots):
    rows = source.shape[0] // n_slots
    for number in range(n_slots):
        start = pl.multiple_of(tab[number] * rows, rows)
        target[number * rows : (number + 1) * rows, :] = source[pl.ds(start, rows), :]


class SlotWriter:
    def __init__(self, outs, held, sems):
        self.outs, self.held, self.sems = outs, held, sems
        self.copies = []

    def send(self, pair, first, rows, sem):
        begin = 0
        for place, out in enumerate(self.outs):
            copy = pltpu.make_async_copy(
                self.held.at[pl.ds(begin, out.shape[0]), pair, pl.ds(first, rows), :],
                out.at[:, pair, pl.ds(first, rows), :],
                self.sems.at[place, sem],
            )
            copy.start()
            self.copies.append(copy)
            begin += out.shape[0]

    def write(self, pair, grads):
        n_slots = self.held.shape[0]
        first = 0
        for grad in grads:
            rows, width = grad.shape[0] // n_slots, grad.shape[1]
            low = grad.astype(bf16)
            for number in range(n_slots):
                part = low[number * rows : (number + 1) * rows]
                self.held[number, pair, 0:rows, first : first + width] = part
            first += width
        self.send(pair, 0, rows, pair)

    def finish(self):
        wait_for(self.copies)


def toeplitz(row, length):
    return pltpu.roll(jnp.broadcast_to(row, (length, row.shape[1])), 0, 1, stride=1, stride_axis=0)


def bias_of(tab, falls, pair, length):
    head = tab[16 + pair] * 2
    return jnp.concatenate(
        [toeplitz(falls[pl.ds(head + side, 1), :], length) for side in range(2)], axis=1
    )


def fold_diagonals(grad):
    length = grad.shape[1]
    folded = grad[0:8]
    for start in range(8, grad.shape[0], 8):
        folded = folded + pltpu.roll(grad[start : start + 8], length - start, 1)
    row = lax.broadcasted_iota(jnp.int32, folded.shape, 0)
    for bit in (1, 2, 4):
        folded = jnp.where(row & bit != 0, pltpu.roll(folded, length - bit, 1), folded)
    return jnp.sum(folded, axis=0, keepdims=True)


def self_masks(tab, targets, row, length):
    segments = targets[pl.ds(tab[24] + row, 1), :].astype(f32)
    column = column_of(segments)
    keys = lax.broadcasted_iota(jnp.int32, (length, length), 0)
    queries = lax.broadcasted_iota(jnp.int32, (length, length), 1)
    return doubled(
        jnp.where((column == segments) & (queries >= keys), 1.0, 0.0)
    ) > 0.5


def cross_masks(tab, targets, sources, row, n_pieces, piece_tab):
    segments = targets[pl.ds(tab[24] + row, 1), :].astype(f32)
    width = sources.shape[1] // n_pieces
    chosen = lax.broadcasted_iota(jnp.int32, (sources.shape[0], width), 0) == tab[24] + row
    parts = []
    for i in range(n_pieces):
        start = pl.multiple_of(tab[piece_tab + i] * width, 128)
        slab = sources[:, pl.ds(start, width)].astype(f32)
        parts.append(jnp.sum(jnp.where(chosen, slab, 0.0), axis=0, keepdims=True))
    column = column_of(jnp.concatenate(parts, axis=1) if n_pieces > 1 else parts[0])
    return doubled(jnp.where(column == segments, 1.0, 0.0)) > 0.5


def self_forward_kernel(n_slots, n_after, rows_held, tab, targets, onehot, x_all, *refs):
    slots, refs = refs[:n_slots], refs[n_slots + n_after :]
    after, normed, query, key, value, mixed, totals, gains, falls = refs[:9]
    weights, extras, x_rows, sems, extra_sems, x_sem = refs[9:]
    length = x_all.shape[1]
    fetch_x = pltpu.make_async_copy(x_all.at[pl.ds(tab[24], rows_held)], x_rows, x_sem)
    fetch_extra = extra_copies(slots, extras, D // n_slots, extra_sems)
    for copy in [fetch_x] + fetch_extra:
        copy.start()
    fetch = weight_copies(slots, weights, tab, sems)
    wait_for(fetch_extra)
    tile = jnp.zeros((EXTRA, D), f32)
    for number in range(n_slots):
        for pair in range(PAIRS):
            tile = tile + extras[number, pair].astype(f32)
    gains[...] = tile[0:8]
    falls[...] = dot_nn(tile[8:16, 0:128].astype(bf16), onehot[...])
    fetch_x.wait()
    resident = x_rows[...].reshape(rows_held * length, D).astype(f32)
    low = (resident * root_scale(resident) * tile[0:1]).astype(bf16)
    normed[...] = low
    allowed = [self_masks(tab, targets, row, length) for row in range(rows_held)]
    total = resident
    for group in GROUPS:
        for pair in group:
            wait_for(fetch[pair])
            projected = dot_nn(low, weights[pair, :, 0 : 3 * PAIR]).astype(bf16)
            query[pair] = projected[:, 0:PAIR]
            key[pair] = projected[:, PAIR : 2 * PAIR]
            value[pair] = projected[:, 2 * PAIR :]
        places = [(pair, row, slice(row * length, (row + 1) * length)) for pair in group for row in range(rows_held)]
        biases = {pair: bias_of(tab, falls, pair, length) for pair in group}
        mixes, logs = attend(
            [
                (query[pair, span], key[pair, span], value[pair, span], biases[pair], allowed[row])
                for pair, row, span in places
            ]
        )
        for (pair, row, span), mix, log_total in zip(places, mixes, logs):
            mixed[pair, span] = mix
            totals[pair, row : row + 1, :] = log_total
        for pair in group:
            total = total + dot_nt(mixed[pair], weights[pair, :, 3 * PAIR :])
    after[...] = total


def encoder_copies(pieces, encoder, tab, rows_held, sems):
    width = encoder.shape[1] // len(pieces)
    copies = []
    for number, piece in enumerate(pieces):
        start = tab[24] if piece.shape[0] > rows_held else 0
        copies.append(
            pltpu.make_async_copy(
                piece.at[pl.ds(start, rows_held)],
                encoder.at[:, pl.ds(number * width, width), :],
                sems.at[number],
            )
        )
    return copies


def cross_forward_kernel(n_slots, n_pieces, rows_held, tab, targets, sources, gains, before, *refs):
    slots, pieces, refs = refs[:n_slots], refs[n_slots : n_slots + n_pieces], refs[n_slots + n_pieces :]
    after, normed, query, key, value, mixed, totals, encoder = refs[:8]
    weights, sems, piece_sems = refs[8:]
    length = before.shape[0] // rows_held
    source_length = sources.shape[1]
    fetch_pieces = encoder_copies(pieces, encoder, tab, rows_held, piece_sems)
    for copy in fetch_pieces:
        copy.start()
    fetch = weight_copies(slots, weights, tab, sems, 4 * PAIR)
    resident = before[...]
    low = (resident * root_scale(resident) * gains[1:2]).astype(bf16)
    normed[...] = low
    allowed = [
        cross_masks(tab, targets, sources, row, n_pieces, 16 if n_pieces > 1 else 28)
        for row in range(rows_held)
    ]
    wait_for(fetch_pieces)
    source = encoder[...].reshape(rows_held * source_length, D)
    total = resident
    for group in GROUPS:
        for pair in group:
            wait_for(fetch[pair])
            query[pair] = dot_nn(low, weights[pair, :, 0:PAIR]).astype(bf16)
            projected = dot_nn(source, weights[pair, :, PAIR : 3 * PAIR]).astype(bf16)
            key[pair] = projected[:, 0:PAIR]
            value[pair] = projected[:, PAIR:]
        places = [(pair, row) for pair in group for row in range(rows_held)]
        spans = [slice(row * length, (row + 1) * length) for row in range(rows_held)]
        wides = [slice(row * source_length, (row + 1) * source_length) for row in range(rows_held)]
        mixes, logs = attend(
            [
                (query[pair, spans[row]], key[pair, wides[row]], value[pair, wides[row]], None, allowed[row])
                for pair, row in places
            ]
        )
        for (pair, row), mix, log_total in zip(places, mixes, logs):
            mixed[pair, spans[row]] = mix
            totals[pair, row : row + 1, :] = log_total
        for pair in group:
            total = total + dot_nt(mixed[pair], weights[pair, :, 3 * PAIR :])
    after[...] = total


def feed_kernel(n_slots, n_outs, rows_held, tab, gains, before, c_all, *refs):
    slots, refs = refs[:n_slots], refs[n_slots:]
    low_out, grad_before, grad_gain = refs[:3]
    outs, refs = refs[3 : 3 + n_outs], refs[3 + n_outs :]
    weights, c_rows, turned, normed_turned, again, c_turned, held, sems, c_sem, out_sems = refs
    fetch_c = pltpu.make_async_copy(c_all.at[pl.ds(tab[24], rows_held)], c_rows, c_sem)
    fetch = weight_copies(slots, weights, tab, sems)
    fetch_c.start()
    resident = before[...]
    gain = gains[2:3]
    low = (resident * root_scale(resident) * gain).astype(bf16)
    turned[...] = jnp.transpose(low)
    permute_rows(turned, normed_turned, tab, n_slots)
    fetch_c.wait()
    cotangent = c_rows[...].reshape(resident.shape)
    again[...] = jnp.transpose(cotangent)
    permute_rows(again, c_turned, tab, n_slots)
    writer = SlotWriter(outs, held, out_sems)
    total = resident
    grad_normed = jnp.zeros_like(resident)
    for pair in range(PAIRS):
        wait_for(fetch[pair])
        inner, outer = weights[pair, :, 0:HIDDEN], weights[pair, :, HIDDEN:]
        u = dot_nn(low, inner)
        squared = u * u
        bent = jnp.tanh(gelu_slope * (u + gelu_cubic * u * squared))
        hidden = (0.5 * u * (1.0 + bent)).astype(bf16)
        slope = 0.5 * (1.0 + bent) + 0.5 * u * (1.0 - bent * bent) * gelu_slope * (
            1.0 + 3.0 * gelu_cubic * squared
        )
        total = total + dot_nt(hidden, outer)
        grad_u = (dot_nn(cotangent, outer) * slope).astype(bf16)
        grad_normed = grad_normed + dot_nt(grad_u, inner)
        writer.write(pair, (dot_nn(normed_turned[...], grad_u), dot_nn(c_turned[...], hidden)))
    low_out[...] = total.astype(bf16)
    through, gain_part = root_back(resident, gain, grad_normed)
    grad_before[...] = cotangent.astype(f32) + through
    grad_gain[...] = gain_part
    writer.finish()


def cross_back_kernel(
    n_slots, n_pieces, rows_held, tab, targets, sources, gains, grad_after, before, *refs
):
    query, key, value, totals = refs[:4]
    slots, refs = refs[4 : 4 + n_slots], refs[4 + n_slots :]
    grad_before, grad_gain, d_query, d_key, d_value, weights, sems = refs
    length = before.shape[0] // rows_held
    source_length = sources.shape[1]
    fetch = weight_copies(slots, weights, tab, sems, 4 * PAIR)
    grad_in = grad_after[...]
    low = grad_in.astype(bf16)
    allowed = [
        cross_masks(tab, targets, sources, row, n_pieces, 16 if n_pieces > 1 else 28)
        for row in range(rows_held)
    ]
    spans = [slice(row * length, (row + 1) * length) for row in range(rows_held)]
    wides = [slice(row * source_length, (row + 1) * source_length) for row in range(rows_held)]
    grad_normed = jnp.zeros_like(grad_in)
    for group in GROUPS:
        wait_for([copy for pair in group for copy in fetch[pair]])
        grad_mixed = {pair: dot_nn(low, weights[pair, :, 3 * PAIR :]).astype(bf16) for pair in group}
        places = [(pair, row) for pair in group for row in range(rows_held)]
        results = attend_back(
            [
                (
                    query[pair, spans[row]],
                    key[pair, wides[row]],
                    value[pair, wides[row]],
                    None,
                    allowed[row],
                    totals[pair, row : row + 1, :],
                    grad_mixed[pair][spans[row]],
                )
                for pair, row in places
            ]
        )
        for (pair, row), one, two, three, _ in zip(places, *results):
            d_query[pair, spans[row]] = one
            d_key[pair, wides[row]] = two
            d_value[pair, wides[row]] = three
        for pair in group:
            grad_normed = grad_normed + dot_nt(d_query[pair], weights[pair, :, 0:PAIR])
    through, gain_part = root_back(before[...], gains[1:2], grad_normed)
    grad_before[...] = grad_in + through
    grad_gain[...] = gain_part


def cross_weights_kernel(
    n_slots, n_outs, n_after, tab, grad_after, normed, mixed, encoder, d_query, d_key, d_value, *refs
):
    refs = refs[n_after:]
    outs, refs = refs[:n_outs], refs[n_outs:]
    turned, low_turned, again, normed_turned, wide_turned, encoder_turned, held, out_sems = refs
    writer = SlotWriter(outs, held, out_sems)
    turned[...] = jnp.transpose(grad_after[...].astype(bf16))
    permute_rows(turned, low_turned, tab, n_slots)
    again[...] = jnp.transpose(normed[...])
    permute_rows(again, normed_turned, tab, n_slots)
    wide_turned[...] = jnp.transpose(encoder[...].reshape(wide_turned.shape[1], D))
    permute_rows(wide_turned, encoder_turned, tab, n_slots)
    for pair in range(PAIRS):
        writer.write(
            pair,
            (
                dot_nn(normed_turned[...], d_query[pair]),
                dot_nn(encoder_turned[...], d_key[pair]),
                dot_nn(encoder_turned[...], d_value[pair]),
                dot_nn(low_turned[...], mixed[pair]),
            ),
        )
    writer.finish()


def self_back_kernel(
    n_slots, n_outs, n_after, rows_held, tab, targets, onehot, gains, falls, gain_two, gain_three, grad_after, x_all, *refs
):
    normed, query, key, value, mixed, totals = refs[:6]
    slots, refs = refs[6 : 6 + n_slots], refs[6 + n_slots + n_after :]
    low_grad = refs[0]
    outs, refs = refs[1 : 1 + n_outs], refs[1 + n_outs :]
    weights, x_rows, turned, low_turned, again, normed_turned, bias_rows, held, sems, x_sem, out_sems = refs
    writer = SlotWriter(outs, held, out_sems)
    length = x_all.shape[1]
    fetch_x = pltpu.make_async_copy(x_all.at[pl.ds(tab[24], rows_held)], x_rows, x_sem)
    fetch = weight_copies(slots, weights, tab, sems)
    fetch_x.start()
    grad_in = grad_after[...]
    low = grad_in.astype(bf16)
    turned[...] = jnp.transpose(low)
    permute_rows(turned, low_turned, tab, n_slots)
    again[...] = jnp.transpose(normed[...])
    permute_rows(again, normed_turned, tab, n_slots)
    allowed = [self_masks(tab, targets, row, length) for row in range(rows_held)]
    grad_normed = jnp.zeros_like(grad_in)
    spans = [slice(row * length, (row + 1) * length) for row in range(rows_held)]
    for group in GROUPS:
        wait_for([copy for pair in group for copy in fetch[pair]])
        grad_mixed = {pair: dot_nn(low, weights[pair, :, 3 * PAIR :]).astype(bf16) for pair in group}
        biases = {pair: bias_of(tab, falls, pair, length) for pair in group}
        places = [(pair, row) for pair in group for row in range(rows_held)]
        results = attend_back(
            [
                (
                    query[pair, spans[row]],
                    key[pair, spans[row]],
                    value[pair, spans[row]],
                    biases[pair],
                    allowed[row],
                    totals[pair, row : row + 1, :],
                    grad_mixed[pair][spans[row]],
                )
                for pair, row in places
            ]
        )
        parts = {place: result for place, *result in zip(places, *results)}
        for pair in group:
            joined = [jnp.concatenate(parts[pair, row][:3], axis=1) for row in range(rows_held)]
            joined = jnp.concatenate(joined, axis=0) if rows_held > 1 else joined[0]
            grad_normed = grad_normed + dot_nt(joined, weights[pair, :, 0 : 3 * PAIR])
            writer.write(
                pair, (dot_nn(normed_turned[...], joined), dot_nn(low_turned[...], mixed[pair]))
            )
            grad_bias = sum(parts[pair, row][3] for row in range(rows_held))
            for side in range(2):
                diagonal = fold_diagonals(grad_bias[:, side * length : (side + 1) * length])
                bias_rows[pl.ds(tab[16 + pair] * 2 + side, 1), :] = diagonal
    fetch_x.wait()
    resident = x_rows[...].reshape(grad_in.shape).astype(f32)
    through, gain_one = root_back(resident, gains[0:1], grad_normed)
    low_grad[...] = (grad_in + through).astype(bf16)
    table = lax.dot_general(
        bias_rows[...],
        onehot[...].astype(f32),
        (((1,), (1,)), ((), ())),
        precision=lax.Precision.HIGHEST,
        preferred_element_type=f32,
    )
    blank = jnp.zeros((5, D), f32)
    table = jnp.concatenate((table, jnp.zeros((8, D - 128), f32)), axis=1)
    tile = jnp.concatenate((gain_one, gain_two[...], gain_three[...], blank, table), axis=0).astype(bf16)
    rows = D // n_slots
    for pair in range(PAIRS):
        for number in range(n_slots):
            held[number, pair, rows : rows + EXTRA, :] = tile
        writer.send(pair, rows, EXTRA, PAIRS + pair)
    writer.finish()


def pack_attention_kernel(n_dp, tab, query, keyval, output, gains, table, own):
    rows, width = query.shape[1], gains.shape[1]
    place_dp, place_mp = tab[25], tab[26]
    parts = []
    for number in range(2):
        parts += [query[number], keyval[number, 0], keyval[number, 1], output[number]]
    own[0:rows, :] = jnp.concatenate(parts, axis=1).astype(bf16)
    wide = jnp.concatenate([gains[...]] * n_dp, axis=1)
    lane = lax.broadcasted_iota(jnp.int32, wide.shape, 1)
    wide = jnp.where((lane // width == place_dp) & (place_mp == 0), wide, 0.0)
    heads, bands = table.shape
    lane = lax.broadcasted_iota(jnp.int32, (bands, D), 1)
    band = lax.broadcasted_iota(jnp.int32, (bands, D), 0)
    at_band = jnp.where(lane == place_dp * bands + band, 1.0, 0.0).astype(bf16)
    head = lax.broadcasted_iota(jnp.int32, (HEADS, heads), 0)
    column = lax.broadcasted_iota(jnp.int32, (HEADS, heads), 1)
    at_head = jnp.where(head == place_mp * heads + column, 1.0, 0.0).astype(bf16)
    placed = dot_nn(at_head, dot_nn(table[...].astype(bf16), at_band).astype(bf16))
    blank = jnp.zeros((HEADS - wide.shape[0], D), f32)
    tile = jnp.concatenate((wide, blank, placed), axis=0).astype(bf16)
    own[rows : rows + EXTRA, 0:D] = tile
    own[rows : rows + EXTRA, D:] = jnp.zeros_like(tile)


def pack_feed_kernel(inner, outer, *refs):
    refs[-1][...] = jnp.concatenate((inner[...], outer[...]), axis=1).astype(bf16)


def split_encoder_kernel(rows_held, tab, encoder, *refs):
    outs, sems = refs[:-1], refs[-1]
    copies = [
        pltpu.make_async_copy(
            encoder.at[pl.ds(tab[17 + number] * rows_held, rows_held)], out, sems.at[number]
        )
        for number, out in enumerate(outs)
    ]
    for copy in copies:
        copy.start()
    for copy in copies:
        copy.wait()


def stack_kernel(count, *refs):
    out = refs[-1]
    for number in range(count):
        out[number] = refs[number][...]


def stack_through_kernel(count, *refs):
    stack_kernel(count, *refs[:-1])


def spread_kernel(rows_held, tab, *refs):
    for side, out in enumerate(refs[-2:]):
        for number, piece in enumerate(refs[4 * side : 4 * side + 4]):
            out[pl.ds(tab[16 + number] * rows_held, rows_held)] = piece[...]


def shape(dims, dtype):
    return jax.ShapeDtypeStruct(dims, dtype)


def dma_sems(*counts):
    return pltpu.SemaphoreType.DMA(counts)


def anys(arrays):
    return [(array, "any") for array in arrays]


def vmems(arrays):
    return [(array, "vmem") for array in arrays]


def call(kernel, operands, outs, scratch, micros=1, aliases=None, any_outs=(), room=2):
    spaces = {"smem": pltpu.SMEM, "vmem": pltpu.VMEM, "any": pl.ANY}
    arrays = [array for array, _ in operands]
    held = [a for a, place in operands if place == "vmem"]
    held += [o for i, o in enumerate(outs) if i not in any_outs and i not in (aliases or {}).values()]
    held += [x for x in scratch if hasattr(x, "shape") and hasattr(x, "dtype") and x.dtype in (f32, bf16)]
    vmem = sum(math.prod(x.shape) * jnp.dtype(x.dtype).itemsize for x in held) + room * 2**20
    moved = sum(a.size * a.dtype.itemsize for a in arrays) + sum(
        math.prod(o.shape) * o.dtype.itemsize for o in outs
    )
    return pl.pallas_call(
        kernel,
        out_shape=tuple(outs),
        in_specs=[pl.BlockSpec(memory_space=spaces[place]) for _, place in operands],
        out_specs=tuple(
            pl.BlockSpec(memory_space=pl.ANY if i in any_outs or i in (aliases or {}).values() else pltpu.VMEM)
            for i in range(len(outs))
        ),
        input_output_aliases=aliases or {},
        scratch_shapes=scratch,
        compiler_params=pltpu.CompilerParams(vmem_limit_bytes=min(vmem, VMEM_BYTES)),
        cost_estimate=pl.CostEstimate(flops=int(micros * 1.15e9), bytes_accessed=moved if micros else 0, transcendentals=0),
    )(*arrays)


def bucket_onehot(length):
    distance = np.arange(length)
    bucket = np.minimum(distance, 16)
    for edge_value in bucket_edges:
        bucket = bucket + (distance >= edge_value)
    return jnp.asarray(np.arange(128)[:, None] == bucket[None, :], bf16)


def adam_step(weight, first, second, grad, rate, decay):
    new_first = beta_first * first + (1.0 - beta_first) * grad
    new_second = beta_second * second + (1.0 - beta_second) * grad * grad
    ratio = (
        new_first
        / (1.0 - beta_first**STEP)
        / (jnp.sqrt(new_second / (1.0 - beta_second**STEP)) + adam_eps)
    )
    return (new_first, new_second, weight - rate * (ratio + decay * weight))


def step_rates():
    return (
        rate_factor * (16 * D) ** (-0.5),
        rate_factor * D ** (-0.5),
        rate_factor * (HD // 8) ** (-0.5),
        rate_factor * D ** (-0.5),
        rate_factor * (FF // 2) ** (-0.5),
        rate_factor,
        rate_factor,
    )


def gate_kernel(*refs):
    pass


def gate(array, after, micros=1):
    (same,) = call(
        gate_kernel,
        anys([array] + list(after)),
        [shape(array.shape, array.dtype)],
        [],
        micros=micros,
        aliases={0: 0},
    )
    return same


def fold_kernel(arrived, kept, *refs):
    sent, stays = refs[-2:]
    half = arrived.shape[0] // 2
    both = [(arrived[i : i + half], kept[i : i + half]) for i in (half, 0)]
    for out, (x, y) in zip((sent, stays), both):
        out[...] = (x.astype(f32) + y.astype(f32)).astype(bf16).reshape(out.shape)


def fold(arrived, kept, after=(), plain=True, micros=1):
    half = arrived.shape[0] // 2
    dims = ((half,) if half > 1 else ()) + arrived.shape[1:]
    if not plain:
        if micros > 1:
            kept, after = gate(kept, after, micros), ()
        return call(
            fold_kernel, vmems((arrived, kept)) + anys(after), [shape(dims, bf16)] * 2, [], micros=0
        )
    if after:
        kept = gate(kept, after, micros)
    parts = [(arrived[i : i + half].reshape(dims), kept[i : i + half].reshape(dims)) for i in (half, 0)]
    return [(x.astype(f32) + y.astype(f32)).astype(bf16) for x, y in parts]


class TreePlan:
    n_slots = 8
    out_slots = (4, 4)
    order = (0, 2, 1, 3)

    def __init__(self, n_dp, n_mp):
        self.n_dp, self.n_mp = n_dp, n_mp

    def pairs(self, target):
        n_mp = self.n_mp
        return [
            (d * n_mp + m, t * n_mp + s)
            for d in range(self.n_dp)
            for m in range(n_mp)
            for t, s in (target(d, m),)
        ]

    def hop_z(self, array, number):
        return lax.ppermute(array, ALL, self.pairs(lambda d, m: (d, m ^ number)))

    def hop_core(self, array):
        return lax.ppermute(array, ALL, self.pairs(lambda d, m: (d ^ 1, m)))

    def hop_first(self, array):
        return lax.ppermute(array, ALL, self.pairs(lambda d, m: (d ^ (4 if d & 1 else 2), m)))

    def hop_second(self, array):
        return lax.ppermute(array, ALL, self.pairs(lambda d, m: (d ^ (2 if d & 1 else 4), m)))

    def table(self, place_dp, place_mp, rows_held):
        core = place_dp & 1
        first, second = 2 + 2 * core, 4 - 2 * core
        own = [place_dp ^ (a * first) ^ (b * second) for b in range(2) for a in range(2)]
        peer = [place_dp ^ 1 ^ (a * second) ^ (b * first) for b in range(2) for a in range(2)]
        return own + peer, [place_mp ^ j for j in self.order]

    def along_z(self, own):
        return [own, self.hop_z(own, 2), self.hop_z(own, 1)]

    def whole_z(self, pieces, after=()):
        own, across, near = pieces
        if after:
            across = gate(across, after)
        return [own, across, near, self.hop_z(across, 1)]

    def stack(self, pieces, after=()):
        (base,) = call(
            functools.partial(stack_kernel, len(pieces)),
            vmems(pieces) + anys(after),
            [shape((len(pieces),) + pieces[0].shape, bf16)],
            [],
        )
        return base

    def stack_through(self, pieces, through):
        return call(
            functools.partial(stack_through_kernel, len(pieces)),
            vmems(pieces) + anys([through]),
            [shape((len(pieces),) + pieces[0].shape, bf16), shape(through.shape, bf16)],
            [],
            aliases={len(pieces): 1},
        )

    def in_plane(self, base, near, far):
        slots = [base, near, far, self.hop_second(near)]
        return slots + [self.hop_core(slot) for slot in slots]

    def attention_shard(self, tab, query, keyval, output, gains, table):
        rows, columns = query.shape[1:]
        (own,) = call(
            functools.partial(pack_attention_kernel, self.n_dp),
            [(tab, "smem")] + vmems((query, keyval, output, gains, table)),
            [shape((rows + EXTRA, 8 * columns), bf16)],
            [],
            room=56,
        )
        return own

    def feed_shard(self, inner, outer, after):
        (own,) = call(
            pack_feed_kernel,
            vmems((inner, outer)) + anys(after),
            [shape((inner.shape[0], 2 * inner.shape[1]), bf16)],
            [],
        )
        return own

    def weights(self, tab, query, keyval, output, inner, outer, gains, table, encoder, rows_held):
        attention = self.whole_z(
            self.along_z(self.attention_shard(tab, query, keyval, output, gains, table))
        )
        parts = call(
            functools.partial(split_encoder_kernel, rows_held),
            [(tab, "smem")] + anys([encoder]),
            [shape((rows_held,) + encoder.shape[1:], bf16)] * 3,
            [dma_sems(3)],
        )
        own_feed = self.feed_shard(inner, outer, [attention[1], parts[0]])
        feed = self.whole_z(self.along_z(own_feed))
        base = self.stack(attention, [own_feed])
        near, far = self.hop_first(base), self.hop_second(base)
        feed_base, near = self.stack_through(feed, near)
        attention = self.in_plane(base, near, far)
        sources = [encoder] + [self.hop_z(part, j) for part, j in zip(parts, self.order[1:])]
        feed = self.in_plane(feed_base, self.hop_first(feed_base), self.hop_second(feed_base))
        return attention, feed, sources, feed_base

    def reduce_core(self, parts, *how):
        own, peer = parts
        return fold(self.hop_core(peer), own, *how)

    def reduce_second(self, pair, *how):
        return fold(self.hop_second(pair[0]), pair[1], *how)

    def reduce_first(self, pair, *how):
        return fold(self.hop_first(pair[0]), pair[1], *how)

    def reduce_near(self, pair, *how):
        return fold(self.hop_z(pair[0], 1), pair[1], *how)

    def reduce_across(self, pair, after=()):
        sent, kept = pair
        if after:
            kept = gate(kept, after)
        total = self.hop_z(sent, 2).astype(f32) + kept.astype(f32)
        return total, total[D // self.n_dp :]

    def finish(self, tab, outputs, row_grads, feed, cross, own):
        row_grads = self.along_z(row_grads)
        cross = self.reduce_core(cross, [own[0]] + row_grads[1:], False, 20)
        row_grads = self.whole_z(row_grads, [cross[0]])
        feed = self.reduce_first(feed, [cross[0]])
        own = self.reduce_second(own, [feed[0]])
        cross = self.reduce_second(cross, [own[0], outputs[3]])
        own = self.reduce_first(own, [cross[0]])
        feed = self.reduce_near(feed, [own[0]])
        cross = self.reduce_first(cross, [feed[0]])
        rows = self.spread(tab, outputs + row_grads, [cross[0]])
        own = self.reduce_near(own, [cross[0], rows[0]])
        cross = self.reduce_near(cross, [own[0]])
        feed = self.reduce_across(feed, [cross[0]])
        own = self.reduce_across(own, [feed[0]])
        return rows, [feed, self.reduce_across(cross, [own[0]]), own]

    def spread(self, tab, pieces, after):
        rows_held = pieces[0].shape[0]
        out = shape((rows_held * self.n_mp,) + pieces[0].shape[1:], pieces[0].dtype)
        return call(
            functools.partial(spread_kernel, rows_held),
            [(tab, "smem")] + vmems(pieces) + anys(after),
            [out, out],
            [],
            micros=0,
        )


class PlainPlan:
    n_slots = 1
    out_slots = (1,)

    def __init__(self, n_dp, n_mp):
        self.n_dp, self.n_mp = n_dp, n_mp

    def table(self, place_dp, place_mp, rows_held):
        return [0], [0, 1, 2, 3]

    def gather(self, own, kinds):
        full = lax.all_gather(own, ("mp", "dp"), axis=0, tiled=True)
        full = full.reshape(self.n_mp, D, kinds, -1).transpose(2, 1, 0, 3)
        return full.reshape(kinds, D, PAIRS, -1).transpose(2, 1, 0, 3).reshape(PAIRS, D, -1)

    def weights(self, tab, query, keyval, output, inner, outer, gains, table, encoder, rows_held):
        place_dp, place_mp = lax.axis_index("dp"), lax.axis_index("mp")
        parts = []
        for i in range(2):
            parts += [query[i], keyval[i, 0], keyval[i, 1], output[i]]
        attention = self.gather(jnp.concatenate(parts, axis=1).astype(bf16), 8)
        feed = self.gather(jnp.concatenate((inner, outer), axis=1).astype(bf16), 2)
        width = gains.shape[1]
        tile = jnp.zeros((EXTRA, D), f32)
        spot = jnp.where(place_mp == 0, gains, 0.0)
        tile = lax.dynamic_update_slice(tile, spot, (0, place_dp * width))
        heads, bands = table.shape
        tile = lax.dynamic_update_slice(tile, table, (8 + place_mp * heads, place_dp * bands))
        tile = lax.psum(tile.astype(bf16).astype(f32), ALL).astype(bf16)
        tile = jnp.concatenate((tile, jnp.zeros_like(tile)), axis=1)[None]
        tile = jnp.concatenate((tile, jnp.zeros((PAIRS - 1,) + tile.shape[1:], bf16)))
        sources = lax.all_to_all(encoder, "mp", split_axis=0, concat_axis=1, tiled=True)
        return [jnp.concatenate((attention, tile), axis=1)], [feed], [sources], feed

    def reduce_core(self, parts, *how):
        return parts

    def reduce(self, grads):
        kinds = 4 if grads.shape[2] == 4 * PAIR else 2
        full = grads[:, :D].reshape(PAIRS, D, kinds, -1).transpose(2, 1, 0, 3)
        full = full.reshape(kinds, D, self.n_mp, -1).transpose(2, 1, 0, 3)
        total = lax.psum_scatter(
            full.reshape(self.n_mp * D, -1), ("mp", "dp"), scatter_dimension=0, tiled=True
        ).astype(f32)
        return total, lax.psum(grads[0, D:].astype(f32), ALL) if grads.shape[1] > D else None

    def along_z(self, own):
        return [own]

    def finish(self, tab, outputs, row_grads, feed, cross, own):
        rows = [lax.all_gather(x, "mp", axis=0, tiled=True) for x in (outputs[0], row_grads)]
        return rows, [self.reduce(parts[0][0]) for parts in (feed, cross, own)]

    def reduce_second(self, parts, after):
        return parts

    def whole_z(self, pieces, after):
        return pieces


def shards(
    plan,
    inputs,
    encoder,
    cotangent,
    target_segments,
    encoder_segments,
    query_weight,
    query_first,
    query_second,
    keyval_weight,
    keyval_first,
    keyval_second,
    output_weight,
    output_first,
    output_second,
    inner_weight,
    inner_first,
    inner_second,
    outer_weight,
    outer_first,
    outer_second,
    gains,
    gains_first,
    gains_second,
    bias_table,
    table_first,
    table_second,
):
    n_slots, out_slots = plan.n_slots, plan.out_slots
    n_outs = len(out_slots)
    seq_count, length, _ = inputs.shape
    source_length = encoder_segments.shape[1]
    rows_held = seq_count // plan.n_mp
    tokens, sources = rows_held * length, rows_held * source_length
    place_dp, place_mp = lax.axis_index("dp"), lax.axis_index("mp")
    slot_table, pair_table = plan.table(place_dp, place_mp, rows_held)
    entries = slot_table + [0] * (16 - len(slot_table)) + pair_table + [0] * 4
    entries = entries + [place_mp * rows_held, place_dp, place_mp] + [0] * 5
    tab = jnp.stack([jnp.asarray(entry, jnp.int32) for entry in entries])
    onehot = bucket_onehot(length)
    attn_slots, feed_slots, pieces, feed_base = plan.weights(
        tab,
        query_weight,
        keyval_weight,
        output_weight.transpose(0, 2, 1),
        inner_weight,
        outer_weight.T,
        gains,
        bias_table.T,
        encoder,
        rows_held,
    )
    n_pieces = len(pieces)
    rows, columns = query_weight.shape[1:]
    width = gains.shape[1]
    bands, heads = bias_table.shape

    flat = (tokens, D)
    paired = (PAIRS, tokens, PAIR)
    wide = (PAIRS, sources, PAIR)
    stats = shape((PAIRS, rows_held, 2 * length), f32)
    attn_weights = VM((PAIRS, D, 4 * PAIR), bf16)

    after_self, normed_one, q_one, k_one, v_one, mix_one, sum_one, gain_rows, falls = call(
        functools.partial(self_forward_kernel, n_slots, 1, rows_held),
        [(tab, "smem")] + vmems((target_segments, onehot)) + anys([inputs] + attn_slots + [feed_base]),
        [shape(flat, f32), shape(flat, bf16)]
        + [shape(paired, bf16)] * 4
        + [stats, shape((8, D), f32), shape((8, length), f32)],
        [
            attn_weights,
            VM((n_slots, PAIRS, EXTRA, D), bf16),
            VM((rows_held, length, D), bf16),
            dma_sems(n_slots, PAIRS),
            dma_sems(n_slots),
            pltpu.SemaphoreType.DMA,
        ],
        room=56,
        micros=30,
    )
    after_cross, normed_two, q_two, k_two, v_two, mix_two, sum_two, source_rows = call(
        functools.partial(cross_forward_kernel, n_slots, n_pieces, rows_held),
        [(tab, "smem")]
        + vmems((target_segments, encoder_segments, gain_rows, after_self))
        + anys(attn_slots + pieces),
        [
            shape(flat, f32),
            shape(flat, bf16),
            shape(paired, bf16),
            shape(wide, bf16),
            shape(wide, bf16),
            shape(paired, bf16),
            stats,
            shape((rows_held, source_length, D), bf16),
        ],
        [attn_weights, dma_sems(n_slots, PAIRS), dma_sems(n_pieces)],
        room=56,
        micros=11,
    )

    def grad_outs(extra, width_out):
        return [
            shape((count, PAIRS, D // n_slots + extra, width_out), bf16) for count in out_slots
        ]

    feed_result = call(
        functools.partial(feed_kernel, n_slots, n_outs, rows_held),
        [(tab, "smem")] + vmems((gain_rows, after_cross)) + anys([cotangent] + feed_slots),
        [shape(flat, bf16), shape(flat, f32), shape((1, D), f32)] + grad_outs(0, 2 * HIDDEN),
        [
            VM((PAIRS, D, 2 * HIDDEN), bf16),
            VM((rows_held, length, D), bf16),
            VM((D, tokens), bf16),
            VM((D, tokens), bf16),
            VM((D, tokens), bf16),
            VM((D, tokens), bf16),
            VM((n_slots, PAIRS, D // n_slots, 2 * HIDDEN), bf16),
            dma_sems(n_slots, PAIRS),
            pltpu.SemaphoreType.DMA,
            dma_sems(n_outs, PAIRS),
        ],
        any_outs=range(3, 3 + n_outs),
        room=56,
        micros=10,
    )
    low_out, grad_second, gain_three = feed_result[:3]
    core_feed = plan.reduce_core(feed_result[3:], (), True)
    grad_first, gain_two, dq_two, dk_two, dv_two = call(
        functools.partial(cross_back_kernel, n_slots, n_pieces, rows_held),
        [(tab, "smem")]
        + vmems((target_segments, encoder_segments, gain_rows, grad_second, after_self))
        + vmems((q_two, k_two, v_two, sum_two))
        + anys(attn_slots),
        [shape(flat, f32), shape((1, D), f32), shape(paired, bf16), shape(wide, bf16), shape(wide, bf16)],
        [attn_weights, dma_sems(n_slots, PAIRS)],
        room=56,
        micros=10,
    )
    self_result = call(
        functools.partial(self_back_kernel, n_slots, n_outs, 1, rows_held),
        [(tab, "smem")]
        + vmems((target_segments, onehot, gain_rows, falls, gain_two, gain_three, grad_first))
        + anys([inputs])
        + vmems((normed_one, q_one, k_one, v_one, mix_one, sum_one))
        + anys(attn_slots + [core_feed[0]]),
        [shape(flat, bf16)] + grad_outs(EXTRA, 4 * PAIR),
        [
            attn_weights,
            VM((rows_held, length, D), bf16),
            VM((D, tokens), bf16),
            VM((D, tokens), bf16),
            VM((D, tokens), bf16),
            VM((D, tokens), bf16),
            VM((8, length), f32),
            VM((n_slots, PAIRS, D // n_slots + EXTRA, 4 * PAIR), bf16),
            dma_sems(n_slots, PAIRS),
            pltpu.SemaphoreType.DMA,
            dma_sems(n_outs, 2 * PAIRS),
        ],
        any_outs=range(1, 1 + n_outs),
        room=12,
        micros=10,
    )
    cross_grads = call(
        functools.partial(cross_weights_kernel, n_slots, n_outs, 1),
        [(tab, "smem")]
        + vmems((grad_second, normed_two, mix_two, source_rows, dq_two, dk_two, dv_two))
        + anys([self_result[1]]),
        grad_outs(0, 4 * PAIR),
        [
            VM((D, tokens), bf16),
            VM((D, tokens), bf16),
            VM((D, tokens), bf16),
            VM((D, tokens), bf16),
            VM((D, sources), bf16),
            VM((D, sources), bf16),
            VM((n_slots, PAIRS, D // n_slots, 4 * PAIR), bf16),
            dma_sems(n_outs, PAIRS),
        ],
        any_outs=range(n_outs),
        room=12,
        micros=7,
    )
    out_pieces = plan.along_z(gate(low_out.reshape(rows_held, length, D), [core_feed[0]]))
    second_feed = plan.reduce_second(core_feed, out_pieces[1:] + [cross_grads[0]])
    core_self = plan.reduce_core(self_result[1:], second_feed[:1], True, 20)
    out_pieces = plan.whole_z(out_pieces, second_feed[:1])
    (outputs, input_grad), ((grad_feed, _), (grad_cross, _), (grad_self, tile)) = plan.finish(
        tab, out_pieces, self_result[0].reshape(rows_held, length, D), second_feed, cross_grads, core_self
    )

    def kind(grads, number):
        return grads[:rows, number * columns : (number + 1) * columns]

    hidden = inner_weight.shape[1]
    grads = (
        jnp.stack((kind(grad_self, 0), kind(grad_cross, 0))),
        jnp.stack(
            (
                jnp.stack((kind(grad_self, 1), kind(grad_self, 2))),
                jnp.stack((kind(grad_cross, 1), kind(grad_cross, 2))),
            )
        ),
        jnp.stack((kind(grad_self, 3).T, kind(grad_cross, 3).T)),
        grad_feed[:, :hidden],
        grad_feed[:, hidden:].T,
        lax.dynamic_slice_in_dim(tile[0:3], place_dp * width, width, 1),
        lax.dynamic_slice(tile, (8 + place_mp * heads, place_dp * bands), (heads, bands)).T,
    )
    params = (
        query_weight,
        keyval_weight,
        output_weight,
        inner_weight,
        outer_weight,
        gains,
        bias_table,
    )
    firsts = (
        query_first,
        keyval_first,
        output_first,
        inner_first,
        outer_first,
        gains_first,
        table_first,
    )
    seconds = (
        query_second,
        keyval_second,
        output_second,
        inner_second,
        outer_second,
        gains_second,
        table_second,
    )
    updated = [
        adam_step(*param_entry)
        for param_entry in zip(params, firsts, seconds, grads, step_rates(), step_decays)
    ]
    return (outputs, input_grad) + tuple(array for triple in updated for array in triple)


def solution(mesh):
    n_dp, n_mp = mesh.shape["dp"], mesh.shape["mp"]
    plan = (TreePlan if (n_dp, n_mp) == (8, 4) else PlainPlan)(n_dp, n_mp)
    by_query, by_keyval = P(None, "dp", "mp"), P(None, None, "dp", "mp")
    by_output, by_inner, by_outer = P(None, "mp", "dp"), P("dp", "mp"), P("mp", "dp")
    weights = (by_query,) * 3 + (by_keyval,) * 3 + (by_output,) * 3 + (by_inner,) * 3
    weights = weights + (by_outer,) * 3 + (P(None, "dp"),) * 3 + (P("dp", "mp"),) * 3
    tokens = P("dp", None, None)
    return jax.shard_map(
        functools.partial(shards, plan),
        mesh=mesh,
        in_specs=(tokens, P("dp", "mp", None), tokens, P("dp", None), P("dp", None)) + weights,
        out_specs=(tokens, tokens) + weights,
        check_vma=False,
    )
```

```python
import functools
import math

import jax
import jax.numpy as jnp
import numpy as np
from jax import lax
from jax.experimental import pallas as pl
from jax.experimental.pallas import tpu as pltpu
from jax.sharding import PartitionSpec as P

D = 512
HEADS = 8
HEAD_DIM = 64
FF = 2048
NB = 32
HD = 512
STEP = 10
PAIRS = HEADS // 2
PAIR = 2 * HEAD_DIM
HIDDEN = FF // PAIRS
EXTRA = 16
GROUPS = (tuple(range(PAIRS)),)
VMEM_BYTES = 56 * 1024 * 1024

norm_eps = 1e-06
beta_first = 0.9
beta_second = 0.95
adam_eps = 1e-08
decay_weight = 0.1
rate_factor = 0.6
masked_value = -1000000000.0
bucket_edges = tuple((math.ceil(16 * 8 ** (number / 16)) for number in range(1, 16)))
step_decays = (decay_weight, decay_weight, decay_weight, decay_weight, decay_weight, 0.0, 0.0)
gelu_slope = math.sqrt(2.0 / math.pi)
gelu_cubic = 0.044715

f32 = jnp.float32
bf16 = jnp.bfloat16
ALL = ("dp", "mp")
VM = pltpu.VMEM


def dot_nn(a, b):
    return lax.dot_general(a, b, (((1,), (0,)), ((), ())), preferred_element_type=f32)


def dot_nt(a, b):
    return lax.dot_general(a, b, (((1,), (1,)), ((), ())), preferred_element_type=f32)


def dot_tn(a, b):
    return lax.dot_general(a, b, (((0,), (0,)), ((), ())), preferred_element_type=f32)


def root_scale(values):
    return lax.rsqrt(jnp.mean(values * values, axis=-1, keepdims=True) + norm_eps)


def root_back(values, gain, grad):
    scale = root_scale(values)
    grad_gain = jnp.sum(grad * values * scale, axis=0, keepdims=True)
    weighted = grad * gain
    along = jnp.sum(weighted * values, axis=-1, keepdims=True)
    inverse = 1.0 / values.shape[-1]
    return scale * weighted - values * (scale * scale * scale * along * inverse), grad_gain


def stack_heads(pair):
    lane = lax.broadcasted_iota(jnp.int32, pair.shape, 1)
    zero = jnp.zeros_like(pair)
    return jnp.concatenate(
        (jnp.where(lane < HEAD_DIM, pair, zero), jnp.where(lane >= HEAD_DIM, pair, zero)), axis=0
    )


def unstack_heads(stacked):
    half = stacked.shape[0] // 2
    top, bottom = stacked[:half], stacked[half:]
    lane = lax.broadcasted_iota(jnp.int32, top.shape, 1)
    return jnp.where(lane < HEAD_DIM, top, bottom)


def column_of(row):
    return jnp.transpose(jnp.broadcast_to(row, (128, row.shape[1])))


def doubled(mask_value):
    return jnp.concatenate((mask_value, mask_value), axis=1)


def masked_scores(units):
    scores = [dot_nt(key, query) for query, key, _, _ in units]
    scores = [s if unit[2] is None else s + unit[2] for s, unit in zip(scores, units)]
    return [jnp.where(unit[3], s, masked_value) for s, unit in zip(scores, units)]


def attend(units):
    scores = masked_scores([(stack_heads(u[0]), u[1], u[3], u[4]) for u in units])
    peaks = [jnp.max(s, axis=0, keepdims=True) for s in scores]
    terms = [jnp.exp(s - peak) for s, peak in zip(scores, peaks)]
    sums = [jnp.sum(t, axis=0, keepdims=True) for t in terms]
    probs = [(t * (1.0 / total)).astype(bf16) for t, total in zip(terms, sums)]
    mixes = [dot_tn(p, u[2]) for p, u in zip(probs, units)]
    mixes = [unstack_heads(m).astype(bf16) for m in mixes]
    return mixes, [peak + jnp.log(total) for peak, total in zip(peaks, sums)]


def attend_back(units):
    queries = [stack_heads(u[0]) for u in units]
    grads = [stack_heads(u[6]) for u in units]
    scores = masked_scores([(q, u[1], u[3], u[4]) for q, u in zip(queries, units)])
    grad_probs = [dot_nt(u[2], g) for u, g in zip(units, grads)]
    probs = [jnp.exp(s - u[5]) for s, u in zip(scores, units)]
    grad_values = [dot_nn(p.astype(bf16), g).astype(bf16) for p, g in zip(probs, grads)]
    along = [jnp.sum(g * p, axis=0, keepdims=True) for g, p in zip(grad_probs, probs)]
    grad_scores = [p * (g - t) for p, g, t in zip(probs, grad_probs, along)]
    low = [g.astype(bf16) for g in grad_scores]
    grad_keys = [dot_nn(x, q).astype(bf16) for x, q in zip(low, queries)]
    grad_queries = [unstack_heads(dot_tn(x, u[1])).astype(bf16) for x, u in zip(low, units)]
    return grad_queries, grad_keys, grad_values, grad_scores


def weight_copies(slots, weights, tab, sems, first=0):
    copies = []
    for number, slot in enumerate(slots):
        rows = weights.shape[1] // len(slots)
        start = pl.multiple_of(tab[number] * rows, rows)
        copies.append(
            pltpu.make_async_copy(
                slot.at[:, pl.ds(0, rows), pl.ds(first, weights.shape[2])],
                weights.at[:, pl.ds(start, rows), :],
                sems.at[number, 0],
            )
        )
    for copy in copies:
        copy.start()
    return [copies] + [[]] * (PAIRS - 1)


def wait_for(copies):
    for copy in copies:
        copy.wait()


def extra_copies(slots, extras, rows, sems):
    return [
        pltpu.make_async_copy(slot.at[:, pl.ds(rows, EXTRA), pl.ds(0, D)], extras.at[number], sems.at[number])
        for number, slot in enumerate(slots)
    ]


def permute_rows(source, target, tab, n_slots):
    rows = source.shape[0] // n_slots
    for number in range(n_slots):
        start = pl.multiple_of(tab[number] * rows, rows)
        target[number * rows : (number + 1) * rows, :] = source[pl.ds(start, rows), :]


class SlotWriter:
    def __init__(self, outs, held, sems):
        self.outs, self.held, self.sems = outs, held, sems
        self.copies = []

    def send(self, pair, first, rows, sem):
        begin = 0
        for place, out in enumerate(self.outs):
            copy = pltpu.make_async_copy(
                self.held.at[pl.ds(begin, out.shape[0]), pair, pl.ds(first, rows), :],
                out.at[:, pair, pl.ds(first, rows), :],
                self.sems.at[place, sem],
            )
            copy.start()
            self.copies.append(copy)
            begin += out.shape[0]

    def write(self, pair, grads):
        n_slots = self.held.shape[0]
        first = 0
        for grad in grads:
            rows, width = grad.shape[0] // n_slots, grad.shape[1]
            low = grad.astype(bf16)
            for number in range(n_slots):
                part = low[number * rows : (number + 1) * rows]
                self.held[number, pair, 0:rows, first : first + width] = part
            first += width
        self.send(pair, 0, rows, pair)

    def finish(self):
        wait_for(self.copies)


def toeplitz(row, length):
    return pltpu.roll(jnp.broadcast_to(row, (length, row.shape[1])), 0, 1, stride=1, stride_axis=0)


def bias_of(tab, falls, pair, length):
    head = tab[16 + pair] * 2
    return jnp.concatenate(
        [toeplitz(falls[pl.ds(head + side, 1), :], length) for side in range(2)], axis=1
    )


def fold_diagonals(grad):
    length = grad.shape[1]
    folded = grad[0:8]
    for start in range(8, grad.shape[0], 8):
        folded = folded + pltpu.roll(grad[start : start + 8], length - start, 1)
    row = lax.broadcasted_iota(jnp.int32, folded.shape, 0)
    for bit in (1, 2, 4):
        folded = jnp.where(row & bit != 0, pltpu.roll(folded, length - bit, 1), folded)
    return jnp.sum(folded, axis=0, keepdims=True)


def self_masks(tab, targets, row, length):
    segments = targets[pl.ds(tab[24] + row, 1), :].astype(f32)
    column = column_of(segments)
    keys = lax.broadcasted_iota(jnp.int32, (length, length), 0)
    queries = lax.broadcasted_iota(jnp.int32, (length, length), 1)
    return doubled(
        jnp.where((column == segments) & (queries >= keys), 1.0, 0.0)
    ) > 0.5


def cross_masks(tab, targets, sources, row, n_pieces, piece_tab):
    segments = targets[pl.ds(tab[24] + row, 1), :].astype(f32)
    width = sources.shape[1] // n_pieces
    chosen = lax.broadcasted_iota(jnp.int32, (sources.shape[0], width), 0) == tab[24] + row
    parts = []
    for i in range(n_pieces):
        start = pl.multiple_of(tab[piece_tab + i] * width, 128)
        slab = sources[:, pl.ds(start, width)].astype(f32)
        parts.append(jnp.sum(jnp.where(chosen, slab, 0.0), axis=0, keepdims=True))
    column = column_of(jnp.concatenate(parts, axis=1) if n_pieces > 1 else parts[0])
    return doubled(jnp.where(column == segments, 1.0, 0.0)) > 0.5


def self_forward_kernel(n_slots, n_after, rows_held, tab, targets, onehot, x_all, *refs):
    slots, refs = refs[:n_slots], refs[n_slots + n_after :]
    after, normed, query, key, value, mixed, totals, gains, falls = refs[:9]
    weights, extras, x_rows, sems, extra_sems, x_sem = refs[9:]
    length = x_all.shape[1]
    fetch_x = pltpu.make_async_copy(x_all.at[pl.ds(tab[24], rows_held)], x_rows, x_sem)
    fetch_extra = extra_copies(slots, extras, D // n_slots, extra_sems)
    for copy in [fetch_x] + fetch_extra:
        copy.start()
    fetch = weight_copies(slots, weights, tab, sems)
    wait_for(fetch_extra)
    tile = jnp.zeros((EXTRA, D), f32)
    for number in range(n_slots):
        for pair in range(PAIRS):
            tile = tile + extras[number, pair].astype(f32)
    gains[...] = tile[0:8]
    falls[...] = dot_nn(tile[8:16, 0:128].astype(bf16), onehot[...])
    fetch_x.wait()
    resident = x_rows[...].reshape(rows_held * length, D).astype(f32)
    low = (resident * root_scale(resident) * tile[0:1]).astype(bf16)
    normed[...] = low
    allowed = [self_masks(tab, targets, row, length) for row in range(rows_held)]
    total = resident
    for group in GROUPS:
        for pair in group:
            wait_for(fetch[pair])
            projected = dot_nn(low, weights[pair, :, 0 : 3 * PAIR]).astype(bf16)
            query[pair] = projected[:, 0:PAIR]
            key[pair] = projected[:, PAIR : 2 * PAIR]
            value[pair] = projected[:, 2 * PAIR :]
        places = [(pair, row, slice(row * length, (row + 1) * length)) for pair in group for row in range(rows_held)]
        biases = {pair: bias_of(tab, falls, pair, length) for pair in group}
        mixes, logs = attend(
            [
                (query[pair, span], key[pair, span], value[pair, span], biases[pair], allowed[row])
                for pair, row, span in places
            ]
        )
        for (pair, row, span), mix, log_total in zip(places, mixes, logs):
            mixed[pair, span] = mix
            totals[pair, row : row + 1, :] = log_total
        for pair in group:
            total = total + dot_nt(mixed[pair], weights[pair, :, 3 * PAIR :])
    after[...] = total


def encoder_copies(pieces, encoder, tab, rows_held, sems):
    width = encoder.shape[1] // len(pieces)
    copies = []
    for number, piece in enumerate(pieces):
        start = tab[24] if piece.shape[0] > rows_held else 0
        copies.append(
            pltpu.make_async_copy(
                piece.at[pl.ds(start, rows_held)],
                encoder.at[:, pl.ds(number * width, width), :],
                sems.at[number],
            )
        )
    return copies


def cross_forward_kernel(n_slots, n_pieces, rows_held, tab, targets, sources, gains, before, *refs):
    slots, pieces, refs = refs[:n_slots], refs[n_slots : n_slots + n_pieces], refs[n_slots + n_pieces :]
    after, normed, query, key, value, mixed, totals, encoder = refs[:8]
    weights, sems, piece_sems = refs[8:]
    length = before.shape[0] // rows_held
    source_length = sources.shape[1]
    fetch_pieces = encoder_copies(pieces, encoder, tab, rows_held, piece_sems)
    for copy in fetch_pieces:
        copy.start()
    fetch = weight_copies(slots, weights, tab, sems, 4 * PAIR)
    resident = before[...]
    low = (resident * root_scale(resident) * gains[1:2]).astype(bf16)
    normed[...] = low
    allowed = [
        cross_masks(tab, targets, sources, row, n_pieces, 16 if n_pieces > 1 else 28)
        for row in range(rows_held)
    ]
    wait_for(fetch_pieces)
    source = encoder[...].reshape(rows_held * source_length, D)
    total = resident
    for group in GROUPS:
        for pair in group:
            wait_for(fetch[pair])
            query[pair] = dot_nn(low, weights[pair, :, 0:PAIR]).astype(bf16)
            projected = dot_nn(source, weights[pair, :, PAIR : 3 * PAIR]).astype(bf16)
            key[pair] = projected[:, 0:PAIR]
            value[pair] = projected[:, PAIR:]
        places = [(pair, row) for pair in group for row in range(rows_held)]
        spans = [slice(row * length, (row + 1) * length) for row in range(rows_held)]
        wides = [slice(row * source_length, (row + 1) * source_length) for row in range(rows_held)]
        mixes, logs = attend(
            [
                (query[pair, spans[row]], key[pair, wides[row]], value[pair, wides[row]], None, allowed[row])
                for pair, row in places
            ]
        )
        for (pair, row), mix, log_total in zip(places, mixes, logs):
            mixed[pair, spans[row]] = mix
            totals[pair, row : row + 1, :] = log_total
        for pair in group:
            total = total + dot_nt(mixed[pair], weights[pair, :, 3 * PAIR :])
    after[...] = total


def feed_kernel(n_slots, n_outs, rows_held, tab, gains, before, c_all, *refs):
    slots, refs = refs[:n_slots], refs[n_slots:]
    low_out, grad_before, grad_gain = refs[:3]
    outs, refs = refs[3 : 3 + n_outs], refs[3 + n_outs :]
    weights, c_rows, turned, normed_turned, again, c_turned, held, sems, c_sem, out_sems = refs
    fetch_c = pltpu.make_async_copy(c_all.at[pl.ds(tab[24], rows_held)], c_rows, c_sem)
    fetch = weight_copies(slots, weights, tab, sems)
    fetch_c.start()
    resident = before[...]
    gain = gains[2:3]
    low = (resident * root_scale(resident) * gain).astype(bf16)
    turned[...] = jnp.transpose(low)
    permute_rows(turned, normed_turned, tab, n_slots)
    fetch_c.wait()
    cotangent = c_rows[...].reshape(resident.shape)
    again[...] = jnp.transpose(cotangent)
    permute_rows(again, c_turned, tab, n_slots)
    writer = SlotWriter(outs, held, out_sems)
    total = resident
    grad_normed = jnp.zeros_like(resident)
    for pair in range(PAIRS):
        wait_for(fetch[pair])
        inner, outer = weights[pair, :, 0:HIDDEN], weights[pair, :, HIDDEN:]
        u = dot_nn(low, inner)
        squared = u * u
        bent = jnp.tanh(gelu_slope * (u + gelu_cubic * u * squared))
        hidden = (0.5 * u * (1.0 + bent)).astype(bf16)
        slope = 0.5 * (1.0 + bent) + 0.5 * u * (1.0 - bent * bent) * gelu_slope * (
            1.0 + 3.0 * gelu_cubic * squared
        )
        total = total + dot_nt(hidden, outer)
        grad_u = (dot_nn(cotangent, outer) * slope).astype(bf16)
        grad_normed = grad_normed + dot_nt(grad_u, inner)
        writer.write(pair, (dot_nn(normed_turned[...], grad_u), dot_nn(c_turned[...], hidden)))
    low_out[...] = total.astype(bf16)
    through, gain_part = root_back(resident, gain, grad_normed)
    grad_before[...] = cotangent.astype(f32) + through
    grad_gain[...] = gain_part
    writer.finish()


def cross_back_kernel(
    n_slots, n_pieces, rows_held, tab, targets, sources, gains, grad_after, before, *refs
):
    query, key, value, totals = refs[:4]
    slots, refs = refs[4 : 4 + n_slots], refs[4 + n_slots :]
    grad_before, grad_gain, d_query, d_key, d_value, weights, sems = refs
    length = before.shape[0] // rows_held
    source_length = sources.shape[1]
    fetch = weight_copies(slots, weights, tab, sems, 4 * PAIR)
    grad_in = grad_after[...]
    low = grad_in.astype(bf16)
    allowed = [
        cross_masks(tab, targets, sources, row, n_pieces, 16 if n_pieces > 1 else 28)
        for row in range(rows_held)
    ]
    spans = [slice(row * length, (row + 1) * length) for row in range(rows_held)]
    wides = [slice(row * source_length, (row + 1) * source_length) for row in range(rows_held)]
    grad_normed = jnp.zeros_like(grad_in)
    for group in GROUPS:
        wait_for([copy for pair in group for copy in fetch[pair]])
        grad_mixed = {pair: dot_nn(low, weights[pair, :, 3 * PAIR :]).astype(bf16) for pair in group}
        places = [(pair, row) for pair in group for row in range(rows_held)]
        results = attend_back(
            [
                (
                    query[pair, spans[row]],
                    key[pair, wides[row]],
                    value[pair, wides[row]],
                    None,
                    allowed[row],
                    totals[pair, row : row + 1, :],
                    grad_mixed[pair][spans[row]],
                )
                for pair, row in places
            ]
        )
        for (pair, row), one, two, three, _ in zip(places, *results):
            d_query[pair, spans[row]] = one
            d_key[pair, wides[row]] = two
            d_value[pair, wides[row]] = three
        for pair in group:
            grad_normed = grad_normed + dot_nt(d_query[pair], weights[pair, :, 0:PAIR])
    through, gain_part = root_back(before[...], gains[1:2], grad_normed)
    grad_before[...] = grad_in + through
    grad_gain[...] = gain_part


def cross_weights_kernel(
    n_slots, n_outs, n_after, tab, grad_after, normed, mixed, encoder, d_query, d_key, d_value, *refs
):
    refs = refs[n_after:]
    outs, refs = refs[:n_outs], refs[n_outs:]
    turned, low_turned, again, normed_turned, wide_turned, encoder_turned, held, out_sems = refs
    writer = SlotWriter(outs, held, out_sems)
    turned[...] = jnp.transpose(grad_after[...].astype(bf16))
    permute_rows(turned, low_turned, tab, n_slots)
    again[...] = jnp.transpose(normed[...])
    permute_rows(again, normed_turned, tab, n_slots)
    wide_turned[...] = jnp.transpose(encoder[...].reshape(wide_turned.shape[1], D))
    permute_rows(wide_turned, encoder_turned, tab, n_slots)
    for pair in range(PAIRS):
        writer.write(
            pair,
            (
                dot_nn(normed_turned[...], d_query[pair]),
                dot_nn(encoder_turned[...], d_key[pair]),
                dot_nn(encoder_turned[...], d_value[pair]),
                dot_nn(low_turned[...], mixed[pair]),
            ),
        )
    writer.finish()


def self_back_kernel(
    n_slots, n_outs, n_after, rows_held, tab, targets, onehot, gains, falls, gain_two, gain_three, grad_after, x_all, *refs
):
    normed, query, key, value, mixed, totals = refs[:6]
    slots, refs = refs[6 : 6 + n_slots], refs[6 + n_slots + n_after :]
    low_grad = refs[0]
    outs, refs = refs[1 : 1 + n_outs], refs[1 + n_outs :]
    weights, x_rows, turned, low_turned, again, normed_turned, bias_rows, held, sems, x_sem, out_sems = refs
    writer = SlotWriter(outs, held, out_sems)
    length = x_all.shape[1]
    fetch_x = pltpu.make_async_copy(x_all.at[pl.ds(tab[24], rows_held)], x_rows, x_sem)
    fetch = weight_copies(slots, weights, tab, sems)
    fetch_x.start()
    grad_in = grad_after[...]
    low = grad_in.astype(bf16)
    turned[...] = jnp.transpose(low)
    permute_rows(turned, low_turned, tab, n_slots)
    again[...] = jnp.transpose(normed[...])
    permute_rows(again, normed_turned, tab, n_slots)
    allowed = [self_masks(tab, targets, row, length) for row in range(rows_held)]
    grad_normed = jnp.zeros_like(grad_in)
    spans = [slice(row * length, (row + 1) * length) for row in range(rows_held)]
    for group in GROUPS:
        wait_for([copy for pair in group for copy in fetch[pair]])
        grad_mixed = {pair: dot_nn(low, weights[pair, :, 3 * PAIR :]).astype(bf16) for pair in group}
        biases = {pair: bias_of(tab, falls, pair, length) for pair in group}
        places = [(pair, row) for pair in group for row in range(rows_held)]
        results = attend_back(
            [
                (
                    query[pair, spans[row]],
                    key[pair, spans[row]],
                    value[pair, spans[row]],
                    biases[pair],
                    allowed[row],
                    totals[pair, row : row + 1, :],
                    grad_mixed[pair][spans[row]],
                )
                for pair, row in places
            ]
        )
        parts = {place: result for place, *result in zip(places, *results)}
        for pair in group:
            joined = [jnp.concatenate(parts[pair, row][:3], axis=1) for row in range(rows_held)]
            joined = jnp.concatenate(joined, axis=0) if rows_held > 1 else joined[0]
            grad_normed = grad_normed + dot_nt(joined, weights[pair, :, 0 : 3 * PAIR])
            writer.write(
                pair, (dot_nn(normed_turned[...], joined), dot_nn(low_turned[...], mixed[pair]))
            )
            grad_bias = sum(parts[pair, row][3] for row in range(rows_held))
            for side in range(2):
                diagonal = fold_diagonals(grad_bias[:, side * length : (side + 1) * length])
                bias_rows[pl.ds(tab[16 + pair] * 2 + side, 1), :] = diagonal
    fetch_x.wait()
    resident = x_rows[...].reshape(grad_in.shape).astype(f32)
    through, gain_one = root_back(resident, gains[0:1], grad_normed)
    low_grad[...] = (grad_in + through).astype(bf16)
    table = lax.dot_general(
        bias_rows[...],
        onehot[...].astype(f32),
        (((1,), (1,)), ((), ())),
        precision=lax.Precision.HIGHEST,
        preferred_element_type=f32,
    )
    blank = jnp.zeros((5, D), f32)
    table = jnp.concatenate((table, jnp.zeros((8, D - 128), f32)), axis=1)
    tile = jnp.concatenate((gain_one, gain_two[...], gain_three[...], blank, table), axis=0).astype(bf16)
    rows = D // n_slots
    for pair in range(PAIRS):
        for number in range(n_slots):
            held[number, pair, rows : rows + EXTRA, :] = tile
        writer.send(pair, rows, EXTRA, PAIRS + pair)
    writer.finish()


def pack_attention_kernel(n_dp, tab, query, keyval, output, gains, table, own):
    rows, width = query.shape[1], gains.shape[1]
    place_dp, place_mp = tab[25], tab[26]
    parts = []
    for number in range(2):
        parts += [query[number], keyval[number, 0], keyval[number, 1], output[number]]
    own[0:rows, :] = jnp.concatenate(parts, axis=1).astype(bf16)
    wide = jnp.concatenate([gains[...]] * n_dp, axis=1)
    lane = lax.broadcasted_iota(jnp.int32, wide.shape, 1)
    wide = jnp.where((lane // width == place_dp) & (place_mp == 0), wide, 0.0)
    heads, bands = table.shape
    lane = lax.broadcasted_iota(jnp.int32, (bands, D), 1)
    band = lax.broadcasted_iota(jnp.int32, (bands, D), 0)
    at_band = jnp.where(lane == place_dp * bands + band, 1.0, 0.0).astype(bf16)
    head = lax.broadcasted_iota(jnp.int32, (HEADS, heads), 0)
    column = lax.broadcasted_iota(jnp.int32, (HEADS, heads), 1)
    at_head = jnp.where(head == place_mp * heads + column, 1.0, 0.0).astype(bf16)
    placed = dot_nn(at_head, dot_nn(table[...].astype(bf16), at_band).astype(bf16))
    blank = jnp.zeros((HEADS - wide.shape[0], D), f32)
    tile = jnp.concatenate((wide, blank, placed), axis=0).astype(bf16)
    own[rows : rows + EXTRA, 0:D] = tile
    own[rows : rows + EXTRA, D:] = jnp.zeros_like(tile)


def pack_feed_kernel(inner, outer, *refs):
    refs[-1][...] = jnp.concatenate((inner[...], outer[...]), axis=1).astype(bf16)


def split_encoder_kernel(rows_held, tab, encoder, *refs):
    outs, sems = refs[:-1], refs[-1]
    copies = [
        pltpu.make_async_copy(
            encoder.at[pl.ds(tab[17 + number] * rows_held, rows_held)], out, sems.at[number]
        )
        for number, out in enumerate(outs)
    ]
    for copy in copies:
        copy.start()
    for copy in copies:
        copy.wait()


def stack_kernel(count, *refs):
    out = refs[-1]
    for number in range(count):
        out[number] = refs[number][...]


def stack_through_kernel(count, *refs):
    stack_kernel(count, *refs[:-1])


def spread_kernel(rows_held, tab, *refs):
    for side, out in enumerate(refs[-2:]):
        for number, piece in enumerate(refs[4 * side : 4 * side + 4]):
            out[pl.ds(tab[16 + number] * rows_held, rows_held)] = piece[...]


def shape(dims, dtype):
    return jax.ShapeDtypeStruct(dims, dtype)


def dma_sems(*counts):
    return pltpu.SemaphoreType.DMA(counts)


def anys(arrays):
    return [(array, "any") for array in arrays]


def vmems(arrays):
    return [(array, "vmem") for array in arrays]


def call(kernel, operands, outs, scratch, micros=1, aliases=None, any_outs=(), room=2):
    spaces = {"smem": pltpu.SMEM, "vmem": pltpu.VMEM, "any": pl.ANY}
    arrays = [array for array, _ in operands]
    held = [a for a, place in operands if place == "vmem"]
    held += [o for i, o in enumerate(outs) if i not in any_outs and i not in (aliases or {}).values()]
    held += [x for x in scratch if hasattr(x, "shape") and hasattr(x, "dtype") and x.dtype in (f32, bf16)]
    vmem = sum(math.prod(x.shape) * jnp.dtype(x.dtype).itemsize for x in held) + room * 2**20
    moved = sum(a.size * a.dtype.itemsize for a in arrays) + sum(
        math.prod(o.shape) * o.dtype.itemsize for o in outs
    )
    return pl.pallas_call(
        kernel,
        out_shape=tuple(outs),
        in_specs=[pl.BlockSpec(memory_space=spaces[place]) for _, place in operands],
        out_specs=tuple(
            pl.BlockSpec(memory_space=pl.ANY if i in any_outs or i in (aliases or {}).values() else pltpu.VMEM)
            for i in range(len(outs))
        ),
        input_output_aliases=aliases or {},
        scratch_shapes=scratch,
        compiler_params=pltpu.CompilerParams(vmem_limit_bytes=min(vmem, VMEM_BYTES)),
        cost_estimate=pl.CostEstimate(flops=int(micros * 1.15e9), bytes_accessed=moved if micros else 0, transcendentals=0),
    )(*arrays)


def bucket_onehot(length):
    distance = np.arange(length)
    bucket = np.minimum(distance, 16)
    for edge_value in bucket_edges:
        bucket = bucket + (distance >= edge_value)
    return jnp.asarray(np.arange(128)[:, None] == bucket[None, :], bf16)


def adam_step(weight, first, second, grad, rate, decay):
    new_first = beta_first * first + (1.0 - beta_first) * grad
    new_second = beta_second * second + (1.0 - beta_second) * grad * grad
    ratio = (
        new_first
        / (1.0 - beta_first**STEP)
        / (jnp.sqrt(new_second / (1.0 - beta_second**STEP)) + adam_eps)
    )
    return (new_first, new_second, weight - rate * (ratio + decay * weight))


def step_rates():
    return (
        rate_factor * (16 * D) ** (-0.5),
        rate_factor * D ** (-0.5),
        rate_factor * (HD // 8) ** (-0.5),
        rate_factor * D ** (-0.5),
        rate_factor * (FF // 2) ** (-0.5),
        rate_factor,
        rate_factor,
    )


def gate_kernel(*refs):
    pass


def gate(array, after, micros=1):
    (same,) = call(
        gate_kernel,
        anys([array] + list(after)),
        [shape(array.shape, array.dtype)],
        [],
        micros=micros,
        aliases={0: 0},
    )
    return same


def fold_kernel(arrived, kept, *refs):
    sent, stays = refs[-2:]
    half = arrived.shape[0] // 2
    both = [(arrived[i : i + half], kept[i : i + half]) for i in (half, 0)]
    for out, (x, y) in zip((sent, stays), both):
        out[...] = (x.astype(f32) + y.astype(f32)).astype(bf16).reshape(out.shape)


def fold(arrived, kept, after=(), plain=True, micros=1):
    half = arrived.shape[0] // 2
    dims = ((half,) if half > 1 else ()) + arrived.shape[1:]
    if not plain:
        if micros > 1:
            kept, after = gate(kept, after, micros), ()
        return call(
            fold_kernel, vmems((arrived, kept)) + anys(after), [shape(dims, bf16)] * 2, [], micros=0
        )
    if after:
        kept = gate(kept, after, micros)
    parts = [(arrived[i : i + half].reshape(dims), kept[i : i + half].reshape(dims)) for i in (half, 0)]
    return [(x.astype(f32) + y.astype(f32)).astype(bf16) for x, y in parts]


class TreePlan:
    n_slots = 8
    out_slots = (4, 4)
    order = (0, 2, 1, 3)

    def __init__(self, n_dp, n_mp):
        self.n_dp, self.n_mp = n_dp, n_mp

    def pairs(self, target):
        n_mp = self.n_mp
        return [
            (d * n_mp + m, t * n_mp + s)
            for d in range(self.n_dp)
            for m in range(n_mp)
            for t, s in (target(d, m),)
        ]

    def hop_z(self, array, number):
        return lax.ppermute(array, ALL, self.pairs(lambda d, m: (d, m ^ number)))

    def hop_core(self, array):
        return lax.ppermute(array, ALL, self.pairs(lambda d, m: (d ^ 1, m)))

    def hop_first(self, array):
        return lax.ppermute(array, ALL, self.pairs(lambda d, m: (d ^ (4 if d & 1 else 2), m)))

    def hop_second(self, array):
        return lax.ppermute(array, ALL, self.pairs(lambda d, m: (d ^ (2 if d & 1 else 4), m)))

    def table(self, place_dp, place_mp, rows_held):
        core = place_dp & 1
        first, second = 2 + 2 * core, 4 - 2 * core
        own = [place_dp ^ (a * first) ^ (b * second) for b in range(2) for a in range(2)]
        peer = [place_dp ^ 1 ^ (a * second) ^ (b * first) for b in range(2) for a in range(2)]
        return own + peer, [place_mp ^ j for j in self.order]

    def along_z(self, own):
        return [own, self.hop_z(own, 2), self.hop_z(own, 1)]

    def whole_z(self, pieces, after=()):
        own, across, near = pieces
        if after:
            across = gate(across, after)
        return [own, across, near, self.hop_z(across, 1)]

    def stack(self, pieces, after=()):
        (base,) = call(
            functools.partial(stack_kernel, len(pieces)),
            vmems(pieces) + anys(after),
            [shape((len(pieces),) + pieces[0].shape, bf16)],
            [],
        )
        return base

    def stack_through(self, pieces, through):
        return call(
            functools.partial(stack_through_kernel, len(pieces)),
            vmems(pieces) + anys([through]),
            [shape((len(pieces),) + pieces[0].shape, bf16), shape(through.shape, bf16)],
            [],
            aliases={len(pieces): 1},
        )

    def in_plane(self, base, near, far, after=()):
        both = self.hop_second(near)
        if after:
            both = gate(both, after, 0)
        slots = [base, near, far, both]
        return slots + [self.hop_core(slot) for slot in slots]

    def attention_shard(self, tab, query, keyval, output, gains, table):
        rows, columns = query.shape[1:]
        (own,) = call(
            functools.partial(pack_attention_kernel, self.n_dp),
            [(tab, "smem")] + vmems((query, keyval, output, gains, table)),
            [shape((rows + EXTRA, 8 * columns), bf16)],
            [],
            room=56,
        )
        return own

    def feed_shard(self, inner, outer, after):
        (own,) = call(
            pack_feed_kernel,
            vmems((inner, outer)) + anys(after),
            [shape((inner.shape[0], 2 * inner.shape[1]), bf16)],
            [],
        )
        return own

    def weights(self, tab, query, keyval, output, inner, outer, gains, table, encoder, rows_held):
        attention = self.whole_z(
            self.along_z(self.attention_shard(tab, query, keyval, output, gains, table))
        )
        parts = call(
            functools.partial(split_encoder_kernel, rows_held),
            [(tab, "smem")] + anys([encoder]),
            [shape((rows_held,) + encoder.shape[1:], bf16)] * 3,
            [dma_sems(3)],
        )
        own_feed = self.feed_shard(inner, outer, [attention[1], parts[0]])
        feed = self.whole_z(self.along_z(own_feed))
        base = self.stack(attention, [own_feed])
        near, far = self.hop_first(base), self.hop_second(base)
        feed_base, near = self.stack_through(feed, near)
        sources = [encoder] + [self.hop_z(part, j) for part, j in zip(parts, self.order[1:])]
        attention = self.in_plane(base, near, far, sources[3:4])
        near = self.hop_first(feed_base)
        feed = [feed_base, near, self.hop_second(feed_base), self.hop_second(near)]
        return attention, feed, sources, feed_base

    def feed_slots(self, feed, after):
        base, near, far, both = feed
        slots = [base, near, gate(far, after, 0), gate(both, after, 0)]
        return slots + [self.hop_core(slot) for slot in slots]

    def reduce_core(self, parts, *how):
        own, peer = parts
        return fold(self.hop_core(peer), own, *how)

    def reduce_second(self, pair, *how):
        return fold(self.hop_second(pair[0]), pair[1], *how)

    def reduce_first(self, pair, *how):
        return fold(self.hop_first(pair[0]), pair[1], *how)

    def reduce_near(self, pair, *how):
        return fold(self.hop_z(pair[0], 1), pair[1], *how)

    def reduce_across(self, pair, after=()):
        sent, kept = pair
        if after:
            kept = gate(kept, after)
        total = self.hop_z(sent, 2).astype(f32) + kept.astype(f32)
        return total, total[D // self.n_dp :]

    def finish(self, tab, outputs, row_grads, feed, cross, own):
        row_grads = self.along_z(row_grads)
        cross = self.reduce_core(cross, [own[0]] + row_grads[1:], False, 20)
        row_grads = self.whole_z(row_grads, [cross[0]])
        feed = self.reduce_first(feed, [cross[0]])
        own = self.reduce_second(own, [feed[0]])
        cross = self.reduce_second(cross, [own[0], outputs[3]])
        own = self.reduce_first(own, [cross[0]])
        feed = self.reduce_near(feed, [own[0]])
        cross = self.reduce_first(cross, [feed[0]])
        rows = self.spread(tab, outputs + row_grads, [cross[0]])
        own = self.reduce_near(own, [cross[0], rows[0]])
        cross = self.reduce_near(cross, [own[0]])
        feed = self.reduce_across(feed, [cross[0]])
        own = self.reduce_across(own, [feed[0]])
        return rows, [feed, self.reduce_across(cross, [own[0]]), own]

    def spread(self, tab, pieces, after):
        rows_held = pieces[0].shape[0]
        out = shape((rows_held * self.n_mp,) + pieces[0].shape[1:], pieces[0].dtype)
        return call(
            functools.partial(spread_kernel, rows_held),
            [(tab, "smem")] + vmems(pieces) + anys(after),
            [out, out],
            [],
            micros=0,
        )


class PlainPlan:
    n_slots = 1
    out_slots = (1,)

    def __init__(self, n_dp, n_mp):
        self.n_dp, self.n_mp = n_dp, n_mp

    def table(self, place_dp, place_mp, rows_held):
        return [0], [0, 1, 2, 3]

    def gather(self, own, kinds):
        full = lax.all_gather(own, ("mp", "dp"), axis=0, tiled=True)
        full = full.reshape(self.n_mp, D, kinds, -1).transpose(2, 1, 0, 3)
        return full.reshape(kinds, D, PAIRS, -1).transpose(2, 1, 0, 3).reshape(PAIRS, D, -1)

    def weights(self, tab, query, keyval, output, inner, outer, gains, table, encoder, rows_held):
        place_dp, place_mp = lax.axis_index("dp"), lax.axis_index("mp")
        parts = []
        for i in range(2):
            parts += [query[i], keyval[i, 0], keyval[i, 1], output[i]]
        attention = self.gather(jnp.concatenate(parts, axis=1).astype(bf16), 8)
        feed = self.gather(jnp.concatenate((inner, outer), axis=1).astype(bf16), 2)
        width = gains.shape[1]
        tile = jnp.zeros((EXTRA, D), f32)
        spot = jnp.where(place_mp == 0, gains, 0.0)
        tile = lax.dynamic_update_slice(tile, spot, (0, place_dp * width))
        heads, bands = table.shape
        tile = lax.dynamic_update_slice(tile, table, (8 + place_mp * heads, place_dp * bands))
        tile = lax.psum(tile.astype(bf16).astype(f32), ALL).astype(bf16)
        tile = jnp.concatenate((tile, jnp.zeros_like(tile)), axis=1)[None]
        tile = jnp.concatenate((tile, jnp.zeros((PAIRS - 1,) + tile.shape[1:], bf16)))
        sources = lax.all_to_all(encoder, "mp", split_axis=0, concat_axis=1, tiled=True)
        return [jnp.concatenate((attention, tile), axis=1)], [feed], [sources], feed

    def feed_slots(self, feed, after):
        return feed

    def reduce_core(self, parts, *how):
        return parts

    def reduce(self, grads):
        kinds = 4 if grads.shape[2] == 4 * PAIR else 2
        full = grads[:, :D].reshape(PAIRS, D, kinds, -1).transpose(2, 1, 0, 3)
        full = full.reshape(kinds, D, self.n_mp, -1).transpose(2, 1, 0, 3)
        total = lax.psum_scatter(
            full.reshape(self.n_mp * D, -1), ("mp", "dp"), scatter_dimension=0, tiled=True
        ).astype(f32)
        return total, lax.psum(grads[0, D:].astype(f32), ALL) if grads.shape[1] > D else None

    def along_z(self, own):
        return [own]

    def finish(self, tab, outputs, row_grads, feed, cross, own):
        rows = [lax.all_gather(x, "mp", axis=0, tiled=True) for x in (outputs[0], row_grads)]
        return rows, [self.reduce(parts[0][0]) for parts in (feed, cross, own)]

    def reduce_second(self, parts, after):
        return parts

    def whole_z(self, pieces, after):
        return pieces


def shards(
    plan,
    inputs,
    encoder,
    cotangent,
    target_segments,
    encoder_segments,
    query_weight,
    query_first,
    query_second,
    keyval_weight,
    keyval_first,
    keyval_second,
    output_weight,
    output_first,
    output_second,
    inner_weight,
    inner_first,
    inner_second,
    outer_weight,
    outer_first,
    outer_second,
    gains,
    gains_first,
    gains_second,
    bias_table,
    table_first,
    table_second,
):
    n_slots, out_slots = plan.n_slots, plan.out_slots
    n_outs = len(out_slots)
    seq_count, length, _ = inputs.shape
    source_length = encoder_segments.shape[1]
    rows_held = seq_count // plan.n_mp
    tokens, sources = rows_held * length, rows_held * source_length
    place_dp, place_mp = lax.axis_index("dp"), lax.axis_index("mp")
    slot_table, pair_table = plan.table(place_dp, place_mp, rows_held)
    entries = slot_table + [0] * (16 - len(slot_table)) + pair_table + [0] * 4
    entries = entries + [place_mp * rows_held, place_dp, place_mp] + [0] * 5
    tab = jnp.stack([jnp.asarray(entry, jnp.int32) for entry in entries])
    onehot = bucket_onehot(length)
    attn_slots, feed, pieces, feed_base = plan.weights(
        tab,
        query_weight,
        keyval_weight,
        output_weight.transpose(0, 2, 1),
        inner_weight,
        outer_weight.T,
        gains,
        bias_table.T,
        encoder,
        rows_held,
    )
    n_pieces = len(pieces)
    rows, columns = query_weight.shape[1:]
    width = gains.shape[1]
    bands, heads = bias_table.shape

    flat = (tokens, D)
    paired = (PAIRS, tokens, PAIR)
    wide = (PAIRS, sources, PAIR)
    stats = shape((PAIRS, rows_held, 2 * length), f32)
    attn_weights = VM((PAIRS, D, 4 * PAIR), bf16)

    after_self, normed_one, q_one, k_one, v_one, mix_one, sum_one, gain_rows, falls = call(
        functools.partial(self_forward_kernel, n_slots, 1, rows_held),
        [(tab, "smem")] + vmems((target_segments, onehot)) + anys([inputs] + attn_slots + [feed_base]),
        [shape(flat, f32), shape(flat, bf16)]
        + [shape(paired, bf16)] * 4
        + [stats, shape((8, D), f32), shape((8, length), f32)],
        [
            attn_weights,
            VM((n_slots, PAIRS, EXTRA, D), bf16),
            VM((rows_held, length, D), bf16),
            dma_sems(n_slots, PAIRS),
            dma_sems(n_slots),
            pltpu.SemaphoreType.DMA,
        ],
        room=56,
        micros=30,
    )
    after_cross, normed_two, q_two, k_two, v_two, mix_two, sum_two, source_rows = call(
        functools.partial(cross_forward_kernel, n_slots, n_pieces, rows_held),
        [(tab, "smem")]
        + vmems((target_segments, encoder_segments, gain_rows, after_self))
        + anys(attn_slots + pieces),
        [
            shape(flat, f32),
            shape(flat, bf16),
            shape(paired, bf16),
            shape(wide, bf16),
            shape(wide, bf16),
            shape(paired, bf16),
            stats,
            shape((rows_held, source_length, D), bf16),
        ],
        [attn_weights, dma_sems(n_slots, PAIRS), dma_sems(n_pieces)],
        room=56,
        micros=11,
    )

    def grad_outs(extra, width_out):
        return [
            shape((count, PAIRS, D // n_slots + extra, width_out), bf16) for count in out_slots
        ]

    feed_slots = plan.feed_slots(feed, [after_cross])
    feed_result = call(
        functools.partial(feed_kernel, n_slots, n_outs, rows_held),
        [(tab, "smem")] + vmems((gain_rows, after_cross)) + anys([cotangent] + feed_slots),
        [shape(flat, bf16), shape(flat, f32), shape((1, D), f32)] + grad_outs(0, 2 * HIDDEN),
        [
            VM((PAIRS, D, 2 * HIDDEN), bf16),
            VM((rows_held, length, D), bf16),
            VM((D, tokens), bf16),
            VM((D, tokens), bf16),
            VM((D, tokens), bf16),
            VM((D, tokens), bf16),
            VM((n_slots, PAIRS, D // n_slots, 2 * HIDDEN), bf16),
            dma_sems(n_slots, PAIRS),
            pltpu.SemaphoreType.DMA,
            dma_sems(n_outs, PAIRS),
        ],
        any_outs=range(3, 3 + n_outs),
        room=56,
        micros=10,
    )
    low_out, grad_second, gain_three = feed_result[:3]
    core_feed = plan.reduce_core(feed_result[3:], (), True)
    grad_first, gain_two, dq_two, dk_two, dv_two = call(
        functools.partial(cross_back_kernel, n_slots, n_pieces, rows_held),
        [(tab, "smem")]
        + vmems((target_segments, encoder_segments, gain_rows, grad_second, after_self))
        + vmems((q_two, k_two, v_two, sum_two))
        + anys(attn_slots),
        [shape(flat, f32), shape((1, D), f32), shape(paired, bf16), shape(wide, bf16), shape(wide, bf16)],
        [attn_weights, dma_sems(n_slots, PAIRS)],
        room=56,
        micros=10,
    )
    self_result = call(
        functools.partial(self_back_kernel, n_slots, n_outs, 1, rows_held),
        [(tab, "smem")]
        + vmems((target_segments, onehot, gain_rows, falls, gain_two, gain_three, grad_first))
        + anys([inputs])
        + vmems((normed_one, q_one, k_one, v_one, mix_one, sum_one))
        + anys(attn_slots + [core_feed[0]]),
        [shape(flat, bf16)] + grad_outs(EXTRA, 4 * PAIR),
        [
            attn_weights,
            VM((rows_held, length, D), bf16),
            VM((D, tokens), bf16),
            VM((D, tokens), bf16),
            VM((D, tokens), bf16),
            VM((D, tokens), bf16),
            VM((8, length), f32),
            VM((n_slots, PAIRS, D // n_slots + EXTRA, 4 * PAIR), bf16),
            dma_sems(n_slots, PAIRS),
            pltpu.SemaphoreType.DMA,
            dma_sems(n_outs, 2 * PAIRS),
        ],
        any_outs=range(1, 1 + n_outs),
        room=12,
        micros=10,
    )
    cross_grads = call(
        functools.partial(cross_weights_kernel, n_slots, n_outs, 1),
        [(tab, "smem")]
        + vmems((grad_second, normed_two, mix_two, source_rows, dq_two, dk_two, dv_two))
        + anys([self_result[1]]),
        grad_outs(0, 4 * PAIR),
        [
            VM((D, tokens), bf16),
            VM((D, tokens), bf16),
            VM((D, tokens), bf16),
            VM((D, tokens), bf16),
            VM((D, sources), bf16),
            VM((D, sources), bf16),
            VM((n_slots, PAIRS, D // n_slots, 4 * PAIR), bf16),
            dma_sems(n_outs, PAIRS),
        ],
        any_outs=range(n_outs),
        room=12,
        micros=7,
    )
    out_pieces = plan.along_z(gate(low_out.reshape(rows_held, length, D), [core_feed[0]]))
    second_feed = plan.reduce_second(core_feed, out_pieces[1:] + [cross_grads[0]])
    core_self = plan.reduce_core(self_result[1:], second_feed[:1], True, 20)
    out_pieces = plan.whole_z(out_pieces, second_feed[:1])
    (outputs, input_grad), ((grad_feed, _), (grad_cross, _), (grad_self, tile)) = plan.finish(
        tab, out_pieces, self_result[0].reshape(rows_held, length, D), second_feed, cross_grads, core_self
    )

    def kind(grads, number):
        return grads[:rows, number * columns : (number + 1) * columns]

    hidden = inner_weight.shape[1]
    grads = (
        jnp.stack((kind(grad_self, 0), kind(grad_cross, 0))),
        jnp.stack(
            (
                jnp.stack((kind(grad_self, 1), kind(grad_self, 2))),
                jnp.stack((kind(grad_cross, 1), kind(grad_cross, 2))),
            )
        ),
        jnp.stack((kind(grad_self, 3).T, kind(grad_cross, 3).T)),
        grad_feed[:, :hidden],
        grad_feed[:, hidden:].T,
        lax.dynamic_slice_in_dim(tile[0:3], place_dp * width, width, 1),
        lax.dynamic_slice(tile, (8 + place_mp * heads, place_dp * bands), (heads, bands)).T,
    )
    params = (
        query_weight,
        keyval_weight,
        output_weight,
        inner_weight,
        outer_weight,
        gains,
        bias_table,
    )
    firsts = (
        query_first,
        keyval_first,
        output_first,
        inner_first,
        outer_first,
        gains_first,
        table_first,
    )
    seconds = (
        query_second,
        keyval_second,
        output_second,
        inner_second,
        outer_second,
        gains_second,
        table_second,
    )
    updated = [
        adam_step(*param_entry)
        for param_entry in zip(params, firsts, seconds, grads, step_rates(), step_decays)
    ]
    return (outputs, input_grad) + tuple(array for triple in updated for array in triple)


def solution(mesh):
    n_dp, n_mp = mesh.shape["dp"], mesh.shape["mp"]
    plan = (TreePlan if (n_dp, n_mp) == (8, 4) else PlainPlan)(n_dp, n_mp)
    by_query, by_keyval = P(None, "dp", "mp"), P(None, None, "dp", "mp")
    by_output, by_inner, by_outer = P(None, "mp", "dp"), P("dp", "mp"), P("mp", "dp")
    weights = (by_query,) * 3 + (by_keyval,) * 3 + (by_output,) * 3 + (by_inner,) * 3
    weights = weights + (by_outer,) * 3 + (P(None, "dp"),) * 3 + (P("dp", "mp"),) * 3
    tokens = P("dp", None, None)
    return jax.shard_map(
        functools.partial(shards, plan),
        mesh=mesh,
        in_specs=(tokens, P("dp", "mp", None), tokens, P("dp", None), P("dp", None)) + weights,
        out_specs=(tokens, tokens) + weights,
        check_vma=False,
    )
```

```python
import functools
import math

import jax
import jax.numpy as jnp
import numpy as np
from jax import lax
from jax.experimental import pallas as pl
from jax.experimental.pallas import tpu as pltpu
from jax.sharding import PartitionSpec as P

D = 512
HEADS = 8
HEAD_DIM = 64
FF = 2048
NB = 32
HD = 512
STEP = 10
PAIRS = HEADS // 2
PAIR = 2 * HEAD_DIM
HIDDEN = FF // PAIRS
EXTRA = 16
GROUPS = (tuple(range(PAIRS)),)
VMEM_BYTES = 56 * 1024 * 1024

norm_eps = 1e-06
beta_first = 0.9
beta_second = 0.95
adam_eps = 1e-08
decay_weight = 0.1
rate_factor = 0.6
masked_value = -1000000000.0
bucket_edges = tuple((math.ceil(16 * 8 ** (number / 16)) for number in range(1, 16)))
step_decays = (decay_weight, decay_weight, decay_weight, decay_weight, decay_weight, 0.0, 0.0)
gelu_slope = math.sqrt(2.0 / math.pi)
gelu_cubic = 0.044715

f32 = jnp.float32
bf16 = jnp.bfloat16
ALL = ("dp", "mp")
VM = pltpu.VMEM


def dot_nn(a, b):
    return lax.dot_general(a, b, (((1,), (0,)), ((), ())), preferred_element_type=f32)


def dot_nt(a, b):
    return lax.dot_general(a, b, (((1,), (1,)), ((), ())), preferred_element_type=f32)


def dot_tn(a, b):
    return lax.dot_general(a, b, (((0,), (0,)), ((), ())), preferred_element_type=f32)


def root_scale(values):
    return lax.rsqrt(jnp.mean(values * values, axis=-1, keepdims=True) + norm_eps)


def root_back(values, gain, grad):
    scale = root_scale(values)
    grad_gain = jnp.sum(grad * values * scale, axis=0, keepdims=True)
    weighted = grad * gain
    along = jnp.sum(weighted * values, axis=-1, keepdims=True)
    inverse = 1.0 / values.shape[-1]
    return scale * weighted - values * (scale * scale * scale * along * inverse), grad_gain


def stack_heads(pair):
    lane = lax.broadcasted_iota(jnp.int32, pair.shape, 1)
    zero = jnp.zeros_like(pair)
    return jnp.concatenate(
        (jnp.where(lane < HEAD_DIM, pair, zero), jnp.where(lane >= HEAD_DIM, pair, zero)), axis=0
    )


def unstack_heads(stacked):
    half = stacked.shape[0] // 2
    top, bottom = stacked[:half], stacked[half:]
    lane = lax.broadcasted_iota(jnp.int32, top.shape, 1)
    return jnp.where(lane < HEAD_DIM, top, bottom)


def column_of(row):
    return jnp.transpose(jnp.broadcast_to(row, (128, row.shape[1])))


def doubled(mask_value):
    return jnp.concatenate((mask_value, mask_value), axis=1)


def masked_scores(units):
    scores = [dot_nt(key, query) for query, key, _, _ in units]
    scores = [s if unit[2] is None else s + unit[2] for s, unit in zip(scores, units)]
    return [jnp.where(unit[3], s, masked_value) for s, unit in zip(scores, units)]


def attend(units):
    scores = masked_scores([(stack_heads(u[0]), u[1], u[3], u[4]) for u in units])
    peaks = [jnp.max(s, axis=0, keepdims=True) for s in scores]
    terms = [jnp.exp(s - peak) for s, peak in zip(scores, peaks)]
    sums = [jnp.sum(t, axis=0, keepdims=True) for t in terms]
    probs = [(t * (1.0 / total)).astype(bf16) for t, total in zip(terms, sums)]
    mixes = [dot_tn(p, u[2]) for p, u in zip(probs, units)]
    mixes = [unstack_heads(m).astype(bf16) for m in mixes]
    return mixes, [peak + jnp.log(total) for peak, total in zip(peaks, sums)]


def attend_back(units):
    queries = [stack_heads(u[0]) for u in units]
    grads = [stack_heads(u[6]) for u in units]
    scores = masked_scores([(q, u[1], u[3], u[4]) for q, u in zip(queries, units)])
    grad_probs = [dot_nt(u[2], g) for u, g in zip(units, grads)]
    probs = [jnp.exp(s - u[5]) for s, u in zip(scores, units)]
    grad_values = [dot_nn(p.astype(bf16), g).astype(bf16) for p, g in zip(probs, grads)]
    along = [jnp.sum(g * p, axis=0, keepdims=True) for g, p in zip(grad_probs, probs)]
    grad_scores = [p * (g - t) for p, g, t in zip(probs, grad_probs, along)]
    low = [g.astype(bf16) for g in grad_scores]
    grad_keys = [dot_nn(x, q).astype(bf16) for x, q in zip(low, queries)]
    grad_queries = [unstack_heads(dot_tn(x, u[1])).astype(bf16) for x, u in zip(low, units)]
    return grad_queries, grad_keys, grad_values, grad_scores


def weight_copies(slots, weights, tab, sems, first=0):
    copies = []
    for number, slot in enumerate(slots):
        rows = weights.shape[1] // len(slots)
        start = pl.multiple_of(tab[number] * rows, rows)
        copies.append(
            pltpu.make_async_copy(
                slot.at[:, pl.ds(0, rows), pl.ds(first, weights.shape[2])],
                weights.at[:, pl.ds(start, rows), :],
                sems.at[number, 0],
            )
        )
    for copy in copies:
        copy.start()
    return [copies] + [[]] * (PAIRS - 1)


def wait_for(copies):
    for copy in copies:
        copy.wait()


def extra_copies(slots, extras, rows, sems):
    return [
        pltpu.make_async_copy(slot.at[:, pl.ds(rows, EXTRA), pl.ds(0, D)], extras.at[number], sems.at[number])
        for number, slot in enumerate(slots)
    ]


def permute_rows(source, target, tab, n_slots):
    rows = source.shape[0] // n_slots
    for number in range(n_slots):
        start = pl.multiple_of(tab[number] * rows, rows)
        target[number * rows : (number + 1) * rows, :] = source[pl.ds(start, rows), :]


class SlotWriter:
    def __init__(self, outs, held, sems):
        self.outs, self.held, self.sems = outs, held, sems
        self.copies = []

    def send(self, pair, first, rows, sem):
        begin = 0
        for place, out in enumerate(self.outs):
            copy = pltpu.make_async_copy(
                self.held.at[pl.ds(begin, out.shape[0]), pair, pl.ds(first, rows), :],
                out.at[:, pair, pl.ds(first, rows), :],
                self.sems.at[place, sem],
            )
            copy.start()
            self.copies.append(copy)
            begin += out.shape[0]

    def write(self, pair, grads):
        n_slots = self.held.shape[0]
        first = 0
        for grad in grads:
            rows, width = grad.shape[0] // n_slots, grad.shape[1]
            low = grad.astype(bf16)
            for number in range(n_slots):
                part = low[number * rows : (number + 1) * rows]
                self.held[number, pair, 0:rows, first : first + width] = part
            first += width
        self.send(pair, 0, rows, pair)

    def finish(self):
        wait_for(self.copies)


def toeplitz(row, length):
    return pltpu.roll(jnp.broadcast_to(row, (length, row.shape[1])), 0, 1, stride=1, stride_axis=0)


def bias_of(tab, falls, pair, length):
    head = tab[16 + pair] * 2
    return jnp.concatenate(
        [toeplitz(falls[pl.ds(head + side, 1), :], length) for side in range(2)], axis=1
    )


def fold_diagonals(grad):
    length = grad.shape[1]
    folded = grad[0:8]
    for start in range(8, grad.shape[0], 8):
        folded = folded + pltpu.roll(grad[start : start + 8], length - start, 1)
    row = lax.broadcasted_iota(jnp.int32, folded.shape, 0)
    for bit in (1, 2, 4):
        folded = jnp.where(row & bit != 0, pltpu.roll(folded, length - bit, 1), folded)
    return jnp.sum(folded, axis=0, keepdims=True)


def self_masks(tab, targets, row, length):
    segments = targets[pl.ds(tab[24] + row, 1), :].astype(f32)
    column = column_of(segments)
    keys = lax.broadcasted_iota(jnp.int32, (length, length), 0)
    queries = lax.broadcasted_iota(jnp.int32, (length, length), 1)
    return doubled(
        jnp.where((column == segments) & (queries >= keys), 1.0, 0.0)
    ) > 0.5


def cross_masks(tab, targets, sources, row, n_pieces, piece_tab):
    segments = targets[pl.ds(tab[24] + row, 1), :].astype(f32)
    width = sources.shape[1] // n_pieces
    chosen = lax.broadcasted_iota(jnp.int32, (sources.shape[0], width), 0) == tab[24] + row
    parts = []
    for i in range(n_pieces):
        start = pl.multiple_of(tab[piece_tab + i] * width, 128)
        slab = sources[:, pl.ds(start, width)].astype(f32)
        parts.append(jnp.sum(jnp.where(chosen, slab, 0.0), axis=0, keepdims=True))
    column = column_of(jnp.concatenate(parts, axis=1) if n_pieces > 1 else parts[0])
    return doubled(jnp.where(column == segments, 1.0, 0.0)) > 0.5


def self_forward_kernel(n_slots, n_after, rows_held, tab, targets, onehot, x_all, *refs):
    slots, refs = refs[:n_slots], refs[n_slots + n_after :]
    after, normed, query, key, value, mixed, totals, gains, falls = refs[:9]
    weights, extras, x_rows, sems, extra_sems, x_sem = refs[9:]
    length = x_all.shape[1]
    fetch_x = pltpu.make_async_copy(x_all.at[pl.ds(tab[24], rows_held)], x_rows, x_sem)
    fetch_extra = extra_copies(slots, extras, D // n_slots, extra_sems)
    for copy in [fetch_x] + fetch_extra:
        copy.start()
    fetch = weight_copies(slots, weights, tab, sems)
    wait_for(fetch_extra)
    tile = jnp.zeros((EXTRA, D), f32)
    for number in range(n_slots):
        for pair in range(PAIRS):
            tile = tile + extras[number, pair].astype(f32)
    gains[...] = tile[0:8]
    falls[...] = dot_nn(tile[8:16, 0:128].astype(bf16), onehot[...])
    fetch_x.wait()
    resident = x_rows[...].reshape(rows_held * length, D).astype(f32)
    low = (resident * root_scale(resident) * tile[0:1]).astype(bf16)
    normed[...] = low
    allowed = [self_masks(tab, targets, row, length) for row in range(rows_held)]
    total = resident
    for group in GROUPS:
        for pair in group:
            wait_for(fetch[pair])
            projected = dot_nn(low, weights[pair, :, 0 : 3 * PAIR]).astype(bf16)
            query[pair] = projected[:, 0:PAIR]
            key[pair] = projected[:, PAIR : 2 * PAIR]
            value[pair] = projected[:, 2 * PAIR :]
        places = [(pair, row, slice(row * length, (row + 1) * length)) for pair in group for row in range(rows_held)]
        biases = {pair: bias_of(tab, falls, pair, length) for pair in group}
        mixes, logs = attend(
            [
                (query[pair, span], key[pair, span], value[pair, span], biases[pair], allowed[row])
                for pair, row, span in places
            ]
        )
        for (pair, row, span), mix, log_total in zip(places, mixes, logs):
            mixed[pair, span] = mix
            totals[pair, row : row + 1, :] = log_total
        for pair in group:
            total = total + dot_nt(mixed[pair], weights[pair, :, 3 * PAIR :])
    after[...] = total


def encoder_copies(pieces, encoder, tab, rows_held, sems):
    width = encoder.shape[1] // len(pieces)
    copies = []
    for number, piece in enumerate(pieces):
        start = tab[24] if piece.shape[0] > rows_held else 0
        copies.append(
            pltpu.make_async_copy(
                piece.at[pl.ds(start, rows_held)],
                encoder.at[:, pl.ds(number * width, width), :],
                sems.at[number],
            )
        )
    return copies


def cross_forward_kernel(n_slots, n_pieces, rows_held, tab, targets, sources, gains, before, *refs):
    slots, pieces, refs = refs[:n_slots], refs[n_slots : n_slots + n_pieces], refs[n_slots + n_pieces :]
    after, normed, query, key, value, mixed, totals, encoder = refs[:8]
    weights, sems, piece_sems = refs[8:]
    length = before.shape[0] // rows_held
    source_length = sources.shape[1]
    fetch_pieces = encoder_copies(pieces, encoder, tab, rows_held, piece_sems)
    for copy in fetch_pieces:
        copy.start()
    fetch = weight_copies(slots, weights, tab, sems, 4 * PAIR)
    resident = before[...]
    low = (resident * root_scale(resident) * gains[1:2]).astype(bf16)
    normed[...] = low
    allowed = [
        cross_masks(tab, targets, sources, row, n_pieces, 16 if n_pieces > 1 else 28)
        for row in range(rows_held)
    ]
    wait_for(fetch_pieces)
    source = encoder[...].reshape(rows_held * source_length, D)
    total = resident
    for group in GROUPS:
        for pair in group:
            wait_for(fetch[pair])
            query[pair] = dot_nn(low, weights[pair, :, 0:PAIR]).astype(bf16)
            projected = dot_nn(source, weights[pair, :, PAIR : 3 * PAIR]).astype(bf16)
            key[pair] = projected[:, 0:PAIR]
            value[pair] = projected[:, PAIR:]
        places = [(pair, row) for pair in group for row in range(rows_held)]
        spans = [slice(row * length, (row + 1) * length) for row in range(rows_held)]
        wides = [slice(row * source_length, (row + 1) * source_length) for row in range(rows_held)]
        mixes, logs = attend(
            [
                (query[pair, spans[row]], key[pair, wides[row]], value[pair, wides[row]], None, allowed[row])
                for pair, row in places
            ]
        )
        for (pair, row), mix, log_total in zip(places, mixes, logs):
            mixed[pair, spans[row]] = mix
            totals[pair, row : row + 1, :] = log_total
        for pair in group:
            total = total + dot_nt(mixed[pair], weights[pair, :, 3 * PAIR :])
    after[...] = total


def feed_kernel(n_slots, n_outs, rows_held, tab, gains, before, c_all, *refs):
    slots, refs = refs[:n_slots], refs[n_slots:]
    low_out, grad_before, grad_gain = refs[:3]
    outs, refs = refs[3 : 3 + n_outs], refs[3 + n_outs :]
    weights, c_rows, turned, normed_turned, again, c_turned, held, sems, c_sem, out_sems = refs
    fetch_c = pltpu.make_async_copy(c_all.at[pl.ds(tab[24], rows_held)], c_rows, c_sem)
    fetch = weight_copies(slots, weights, tab, sems)
    fetch_c.start()
    resident = before[...]
    gain = gains[2:3]
    low = (resident * root_scale(resident) * gain).astype(bf16)
    turned[...] = jnp.transpose(low)
    permute_rows(turned, normed_turned, tab, n_slots)
    fetch_c.wait()
    cotangent = c_rows[...].reshape(resident.shape)
    again[...] = jnp.transpose(cotangent)
    permute_rows(again, c_turned, tab, n_slots)
    writer = SlotWriter(outs, held, out_sems)
    total = resident
    grad_normed = jnp.zeros_like(resident)
    for pair in range(PAIRS):
        wait_for(fetch[pair])
        inner, outer = weights[pair, :, 0:HIDDEN], weights[pair, :, HIDDEN:]
        u = dot_nn(low, inner)
        squared = u * u
        bent = jnp.tanh(gelu_slope * (u + gelu_cubic * u * squared))
        hidden = (0.5 * u * (1.0 + bent)).astype(bf16)
        slope = 0.5 * (1.0 + bent) + 0.5 * u * (1.0 - bent * bent) * gelu_slope * (
            1.0 + 3.0 * gelu_cubic * squared
        )
        total = total + dot_nt(hidden, outer)
        grad_u = (dot_nn(cotangent, outer) * slope).astype(bf16)
        grad_normed = grad_normed + dot_nt(grad_u, inner)
        writer.write(pair, (dot_nn(normed_turned[...], grad_u), dot_nn(c_turned[...], hidden)))
    low_out[...] = total.astype(bf16)
    through, gain_part = root_back(resident, gain, grad_normed)
    grad_before[...] = cotangent.astype(f32) + through
    grad_gain[...] = gain_part
    writer.finish()


def cross_back_kernel(
    n_slots, n_pieces, rows_held, tab, targets, sources, gains, grad_after, before, *refs
):
    query, key, value, totals = refs[:4]
    slots, refs = refs[4 : 4 + n_slots], refs[4 + n_slots :]
    grad_before, grad_gain, d_query, d_key, d_value, weights, sems = refs
    length = before.shape[0] // rows_held
    source_length = sources.shape[1]
    fetch = weight_copies(slots, weights, tab, sems, 4 * PAIR)
    grad_in = grad_after[...]
    low = grad_in.astype(bf16)
    allowed = [
        cross_masks(tab, targets, sources, row, n_pieces, 16 if n_pieces > 1 else 28)
        for row in range(rows_held)
    ]
    spans = [slice(row * length, (row + 1) * length) for row in range(rows_held)]
    wides = [slice(row * source_length, (row + 1) * source_length) for row in range(rows_held)]
    grad_normed = jnp.zeros_like(grad_in)
    for group in GROUPS:
        wait_for([copy for pair in group for copy in fetch[pair]])
        grad_mixed = {pair: dot_nn(low, weights[pair, :, 3 * PAIR :]).astype(bf16) for pair in group}
        places = [(pair, row) for pair in group for row in range(rows_held)]
        results = attend_back(
            [
                (
                    query[pair, spans[row]],
                    key[pair, wides[row]],
                    value[pair, wides[row]],
                    None,
                    allowed[row],
                    totals[pair, row : row + 1, :],
                    grad_mixed[pair][spans[row]],
                )
                for pair, row in places
            ]
        )
        for (pair, row), one, two, three, _ in zip(places, *results):
            d_query[pair, spans[row]] = one
            d_key[pair, wides[row]] = two
            d_value[pair, wides[row]] = three
        for pair in group:
            grad_normed = grad_normed + dot_nt(d_query[pair], weights[pair, :, 0:PAIR])
    through, gain_part = root_back(before[...], gains[1:2], grad_normed)
    grad_before[...] = grad_in + through
    grad_gain[...] = gain_part


def cross_weights_kernel(
    n_slots, n_outs, n_after, tab, grad_after, normed, mixed, encoder, d_query, d_key, d_value, *refs
):
    refs = refs[n_after:]
    outs, refs = refs[:n_outs], refs[n_outs:]
    turned, low_turned, again, normed_turned, wide_turned, encoder_turned, held, out_sems = refs
    writer = SlotWriter(outs, held, out_sems)
    turned[...] = jnp.transpose(grad_after[...].astype(bf16))
    permute_rows(turned, low_turned, tab, n_slots)
    again[...] = jnp.transpose(normed[...])
    permute_rows(again, normed_turned, tab, n_slots)
    wide_turned[...] = jnp.transpose(encoder[...].reshape(wide_turned.shape[1], D))
    permute_rows(wide_turned, encoder_turned, tab, n_slots)
    for pair in range(PAIRS):
        writer.write(
            pair,
            (
                dot_nn(normed_turned[...], d_query[pair]),
                dot_nn(encoder_turned[...], d_key[pair]),
                dot_nn(encoder_turned[...], d_value[pair]),
                dot_nn(low_turned[...], mixed[pair]),
            ),
        )
    writer.finish()


def self_back_kernel(
    n_slots, n_outs, n_after, rows_held, tab, targets, onehot, gains, falls, gain_two, gain_three, grad_after, x_all, *refs
):
    normed, query, key, value, mixed, totals = refs[:6]
    slots, refs = refs[6 : 6 + n_slots], refs[6 + n_slots + n_after :]
    low_grad = refs[0]
    outs, refs = refs[1 : 1 + n_outs], refs[1 + n_outs :]
    weights, x_rows, turned, low_turned, again, normed_turned, bias_rows, held, sems, x_sem, out_sems = refs
    writer = SlotWriter(outs, held, out_sems)
    length = x_all.shape[1]
    fetch_x = pltpu.make_async_copy(x_all.at[pl.ds(tab[24], rows_held)], x_rows, x_sem)
    fetch = weight_copies(slots, weights, tab, sems)
    fetch_x.start()
    grad_in = grad_after[...]
    low = grad_in.astype(bf16)
    turned[...] = jnp.transpose(low)
    permute_rows(turned, low_turned, tab, n_slots)
    again[...] = jnp.transpose(normed[...])
    permute_rows(again, normed_turned, tab, n_slots)
    allowed = [self_masks(tab, targets, row, length) for row in range(rows_held)]
    grad_normed = jnp.zeros_like(grad_in)
    spans = [slice(row * length, (row + 1) * length) for row in range(rows_held)]
    for group in GROUPS:
        wait_for([copy for pair in group for copy in fetch[pair]])
        grad_mixed = {pair: dot_nn(low, weights[pair, :, 3 * PAIR :]).astype(bf16) for pair in group}
        biases = {pair: bias_of(tab, falls, pair, length) for pair in group}
        places = [(pair, row) for pair in group for row in range(rows_held)]
        results = attend_back(
            [
                (
                    query[pair, spans[row]],
                    key[pair, spans[row]],
                    value[pair, spans[row]],
                    biases[pair],
                    allowed[row],
                    totals[pair, row : row + 1, :],
                    grad_mixed[pair][spans[row]],
                )
                for pair, row in places
            ]
        )
        parts = {place: result for place, *result in zip(places, *results)}
        for pair in group:
            joined = [jnp.concatenate(parts[pair, row][:3], axis=1) for row in range(rows_held)]
            joined = jnp.concatenate(joined, axis=0) if rows_held > 1 else joined[0]
            grad_normed = grad_normed + dot_nt(joined, weights[pair, :, 0 : 3 * PAIR])
            writer.write(
                pair, (dot_nn(normed_turned[...], joined), dot_nn(low_turned[...], mixed[pair]))
            )
            grad_bias = sum(parts[pair, row][3] for row in range(rows_held))
            for side in range(2):
                diagonal = fold_diagonals(grad_bias[:, side * length : (side + 1) * length])
                bias_rows[pl.ds(tab[16 + pair] * 2 + side, 1), :] = diagonal
    fetch_x.wait()
    resident = x_rows[...].reshape(grad_in.shape).astype(f32)
    through, gain_one = root_back(resident, gains[0:1], grad_normed)
    low_grad[...] = (grad_in + through).astype(bf16)
    table = lax.dot_general(
        bias_rows[...],
        onehot[...].astype(f32),
        (((1,), (1,)), ((), ())),
        precision=lax.Precision.HIGHEST,
        preferred_element_type=f32,
    )
    blank = jnp.zeros((5, D), f32)
    table = jnp.concatenate((table, jnp.zeros((8, D - 128), f32)), axis=1)
    tile = jnp.concatenate((gain_one, gain_two[...], gain_three[...], blank, table), axis=0).astype(bf16)
    rows = D // n_slots
    for pair in range(PAIRS):
        for number in range(n_slots):
            held[number, pair, rows : rows + EXTRA, :] = tile
        writer.send(pair, rows, EXTRA, PAIRS + pair)
    writer.finish()


def pack_attention_kernel(n_dp, tab, query, keyval, output, gains, table, own):
    rows, width = query.shape[1], gains.shape[1]
    place_dp, place_mp = tab[25], tab[26]
    parts = []
    for number in range(2):
        parts += [query[number], keyval[number, 0], keyval[number, 1], output[number]]
    own[0:rows, :] = jnp.concatenate(parts, axis=1).astype(bf16)
    wide = jnp.concatenate([gains[...]] * n_dp, axis=1)
    lane = lax.broadcasted_iota(jnp.int32, wide.shape, 1)
    wide = jnp.where((lane // width == place_dp) & (place_mp == 0), wide, 0.0)
    heads, bands = table.shape
    lane = lax.broadcasted_iota(jnp.int32, (bands, D), 1)
    band = lax.broadcasted_iota(jnp.int32, (bands, D), 0)
    at_band = jnp.where(lane == place_dp * bands + band, 1.0, 0.0).astype(bf16)
    head = lax.broadcasted_iota(jnp.int32, (HEADS, heads), 0)
    column = lax.broadcasted_iota(jnp.int32, (HEADS, heads), 1)
    at_head = jnp.where(head == place_mp * heads + column, 1.0, 0.0).astype(bf16)
    placed = dot_nn(at_head, dot_nn(table[...].astype(bf16), at_band).astype(bf16))
    blank = jnp.zeros((HEADS - wide.shape[0], D), f32)
    tile = jnp.concatenate((wide, blank, placed), axis=0).astype(bf16)
    own[rows : rows + EXTRA, 0:D] = tile
    own[rows : rows + EXTRA, D:] = jnp.zeros_like(tile)


def pack_feed_kernel(inner, outer, *refs):
    refs[-1][...] = jnp.concatenate((inner[...], outer[...]), axis=1).astype(bf16)


def split_encoder_kernel(rows_held, tab, encoder, *refs):
    outs, sems = refs[:-1], refs[-1]
    copies = [
        pltpu.make_async_copy(
            encoder.at[pl.ds(tab[17 + number] * rows_held, rows_held)], out, sems.at[number]
        )
        for number, out in enumerate(outs)
    ]
    for copy in copies:
        copy.start()
    for copy in copies:
        copy.wait()


def stack_kernel(count, *refs):
    out = refs[-1]
    for number in range(count):
        out[number] = refs[number][...]


def stack_through_kernel(count, *refs):
    stack_kernel(count, *refs[:-1])


def spread_kernel(rows_held, tab, *refs):
    for side, out in enumerate(refs[-2:]):
        for number, piece in enumerate(refs[4 * side : 4 * side + 4]):
            out[pl.ds(tab[16 + number] * rows_held, rows_held)] = piece[...]


def shape(dims, dtype):
    return jax.ShapeDtypeStruct(dims, dtype)


def dma_sems(*counts):
    return pltpu.SemaphoreType.DMA(counts)


def anys(arrays):
    return [(array, "any") for array in arrays]


def vmems(arrays):
    return [(array, "vmem") for array in arrays]


def call(kernel, operands, outs, scratch, micros=1, aliases=None, any_outs=(), room=2):
    spaces = {"smem": pltpu.SMEM, "vmem": pltpu.VMEM, "any": pl.ANY}
    arrays = [array for array, _ in operands]
    held = [a for a, place in operands if place == "vmem"]
    held += [o for i, o in enumerate(outs) if i not in any_outs and i not in (aliases or {}).values()]
    held += [x for x in scratch if hasattr(x, "shape") and hasattr(x, "dtype") and x.dtype in (f32, bf16)]
    vmem = sum(math.prod(x.shape) * jnp.dtype(x.dtype).itemsize for x in held) + room * 2**20
    moved = sum(a.size * a.dtype.itemsize for a in arrays) + sum(
        math.prod(o.shape) * o.dtype.itemsize for o in outs
    )
    return pl.pallas_call(
        kernel,
        out_shape=tuple(outs),
        in_specs=[pl.BlockSpec(memory_space=spaces[place]) for _, place in operands],
        out_specs=tuple(
            pl.BlockSpec(memory_space=pl.ANY if i in any_outs or i in (aliases or {}).values() else pltpu.VMEM)
            for i in range(len(outs))
        ),
        input_output_aliases=aliases or {},
        scratch_shapes=scratch,
        compiler_params=pltpu.CompilerParams(vmem_limit_bytes=min(vmem, VMEM_BYTES)),
        cost_estimate=pl.CostEstimate(flops=int(micros * 1.15e9), bytes_accessed=moved if micros else 0, transcendentals=0),
    )(*arrays)


def bucket_onehot(length):
    distance = np.arange(length)
    bucket = np.minimum(distance, 16)
    for edge_value in bucket_edges:
        bucket = bucket + (distance >= edge_value)
    return jnp.asarray(np.arange(128)[:, None] == bucket[None, :], bf16)


def adam_step(weight, first, second, grad, rate, decay):
    new_first = beta_first * first + (1.0 - beta_first) * grad
    new_second = beta_second * second + (1.0 - beta_second) * grad * grad
    ratio = (
        new_first
        / (1.0 - beta_first**STEP)
        / (jnp.sqrt(new_second / (1.0 - beta_second**STEP)) + adam_eps)
    )
    return (new_first, new_second, weight - rate * (ratio + decay * weight))


def step_rates():
    return (
        rate_factor * (16 * D) ** (-0.5),
        rate_factor * D ** (-0.5),
        rate_factor * (HD // 8) ** (-0.5),
        rate_factor * D ** (-0.5),
        rate_factor * (FF // 2) ** (-0.5),
        rate_factor,
        rate_factor,
    )


def gate_kernel(*refs):
    pass


def gate(array, after, micros=1):
    (same,) = call(
        gate_kernel,
        anys([array] + list(after)),
        [shape(array.shape, array.dtype)],
        [],
        micros=micros,
        aliases={0: 0},
    )
    return same


def fold_kernel(arrived, kept, *refs):
    sent, stays = refs[-2:]
    half = arrived.shape[0] // 2
    both = [(arrived[i : i + half], kept[i : i + half]) for i in (half, 0)]
    for out, (x, y) in zip((sent, stays), both):
        out[...] = (x.astype(f32) + y.astype(f32)).astype(bf16).reshape(out.shape)


def fold(arrived, kept, after=(), plain=True, micros=1):
    half = arrived.shape[0] // 2
    dims = ((half,) if half > 1 else ()) + arrived.shape[1:]
    if not plain:
        if micros > 1:
            kept, after = gate(kept, after, micros), ()
        return call(
            fold_kernel, vmems((arrived, kept)) + anys(after), [shape(dims, bf16)] * 2, [], micros=0
        )
    if after:
        kept = gate(kept, after, micros)
    parts = [(arrived[i : i + half].reshape(dims), kept[i : i + half].reshape(dims)) for i in (half, 0)]
    return [(x.astype(f32) + y.astype(f32)).astype(bf16) for x, y in parts]


class TreePlan:
    n_slots = 8
    out_slots = (4, 4)
    order = (0, 2, 1, 3)

    def __init__(self, n_dp, n_mp):
        self.n_dp, self.n_mp = n_dp, n_mp

    def pairs(self, target):
        n_mp = self.n_mp
        return [
            (d * n_mp + m, t * n_mp + s)
            for d in range(self.n_dp)
            for m in range(n_mp)
            for t, s in (target(d, m),)
        ]

    def hop_z(self, array, number):
        return lax.ppermute(array, ALL, self.pairs(lambda d, m: (d, m ^ number)))

    def hop_core(self, array):
        return lax.ppermute(array, ALL, self.pairs(lambda d, m: (d ^ 1, m)))

    def hop_first(self, array):
        return lax.ppermute(array, ALL, self.pairs(lambda d, m: (d ^ (4 if d & 1 else 2), m)))

    def hop_second(self, array):
        return lax.ppermute(array, ALL, self.pairs(lambda d, m: (d ^ (2 if d & 1 else 4), m)))

    def table(self, place_dp, place_mp, rows_held):
        core = place_dp & 1
        first, second = 2 + 2 * core, 4 - 2 * core
        own = [place_dp ^ (a * first) ^ (b * second) for b in range(2) for a in range(2)]
        peer = [place_dp ^ 1 ^ (a * second) ^ (b * first) for b in range(2) for a in range(2)]
        return own + peer, [place_mp ^ j for j in self.order]

    def along_z(self, own):
        return [own, self.hop_z(own, 2), self.hop_z(own, 1)]

    def whole_z(self, pieces, after=()):
        own, across, near = pieces
        if after:
            across = gate(across, after)
        return [own, across, near, self.hop_z(across, 1)]

    def stack(self, pieces, after=()):
        (base,) = call(
            functools.partial(stack_kernel, len(pieces)),
            vmems(pieces) + anys(after),
            [shape((len(pieces),) + pieces[0].shape, bf16)],
            [],
        )
        return base

    def stack_through(self, pieces, through):
        return call(
            functools.partial(stack_through_kernel, len(pieces)),
            vmems(pieces) + anys([through]),
            [shape((len(pieces),) + pieces[0].shape, bf16), shape(through.shape, bf16)],
            [],
            aliases={len(pieces): 1},
        )

    def in_plane(self, base, near, far, after=()):
        both = self.hop_second(near)
        if after:
            both = gate(both, after, 0)
        slots = [base, near, far, both]
        return slots + [self.hop_core(slot) for slot in slots]

    def attention_shard(self, tab, query, keyval, output, gains, table):
        rows, columns = query.shape[1:]
        (own,) = call(
            functools.partial(pack_attention_kernel, self.n_dp),
            [(tab, "smem")] + vmems((query, keyval, output, gains, table)),
            [shape((rows + EXTRA, 8 * columns), bf16)],
            [],
            room=56,
        )
        return own

    def feed_shard(self, inner, outer, after):
        (own,) = call(
            pack_feed_kernel,
            vmems((inner, outer)) + anys(after),
            [shape((inner.shape[0], 2 * inner.shape[1]), bf16)],
            [],
        )
        return own

    def weights(self, tab, query, keyval, output, inner, outer, gains, table, encoder, rows_held):
        attention = self.whole_z(
            self.along_z(self.attention_shard(tab, query, keyval, output, gains, table))
        )
        parts = call(
            functools.partial(split_encoder_kernel, rows_held),
            [(tab, "smem")] + anys([encoder]),
            [shape((rows_held,) + encoder.shape[1:], bf16)] * 3,
            [dma_sems(3)],
        )
        own_feed = self.feed_shard(inner, outer, [attention[1], parts[0]])
        feed = self.whole_z(self.along_z(own_feed))
        base = self.stack(attention, [own_feed])
        near, far = self.hop_first(base), self.hop_second(base)
        feed_base, near = self.stack_through(feed, near)
        sources = [encoder] + [self.hop_z(part, j) for part, j in zip(parts, self.order[1:])]
        attention = self.in_plane(base, near, far, sources[3:4])
        near = self.hop_first(feed_base)
        feed = [feed_base, near, self.hop_second(feed_base), self.hop_second(near)]
        return attention, feed, sources, feed_base

    def feed_slots(self, feed, after):
        base, near, far, both = feed
        slots = [base, near, gate(far, after, 0), gate(both, after, 0)]
        return slots + [self.hop_core(slot) for slot in slots]

    def reduce_core(self, parts, *how):
        own, peer = parts
        return fold(self.hop_core(peer), own, *how)

    def reduce_second(self, pair, *how):
        return fold(self.hop_second(pair[0]), pair[1], *how)

    def reduce_first(self, pair, *how):
        return fold(self.hop_first(pair[0]), pair[1], *how)

    def reduce_near(self, pair, *how):
        return fold(self.hop_z(pair[0], 1), pair[1], *how)

    def reduce_across(self, pair, after=()):
        sent, kept = pair
        if after:
            kept = gate(kept, after)
        total = self.hop_z(sent, 2).astype(f32) + kept.astype(f32)
        return total, total[D // self.n_dp :]

    def finish(self, tab, outputs, row_grads, feed, cross, own):
        row_grads = self.along_z(row_grads)
        cross = self.reduce_core(cross, [own[0]] + row_grads[1:], False, 20)
        row_grads = self.whole_z(row_grads, [cross[0]])
        feed = self.reduce_first(feed, [cross[0]])
        own = self.reduce_second(own, [feed[0]])
        cross = self.reduce_second(cross, [own[0], outputs[3]])
        own = self.reduce_first(own, [cross[0]])
        feed = self.reduce_near(feed, [own[0]])
        cross = self.reduce_first(cross, [feed[0]])
        rows = self.spread(tab, outputs + row_grads, [cross[0]])
        own = self.reduce_near(own, [cross[0], rows[0]])
        cross = self.reduce_near(cross, [own[0]])
        feed = self.reduce_across(feed, [cross[0]])
        own = self.reduce_across(own, [feed[0]])
        return rows, [feed, self.reduce_across(cross, [own[0]]), own]

    def spread(self, tab, pieces, after):
        rows_held = pieces[0].shape[0]
        out = shape((rows_held * self.n_mp,) + pieces[0].shape[1:], pieces[0].dtype)
        return call(
            functools.partial(spread_kernel, rows_held),
            [(tab, "smem")] + vmems(pieces) + anys(after),
            [out, out],
            [],
            micros=0,
        )


class PlainPlan:
    n_slots = 1
    out_slots = (1,)

    def __init__(self, n_dp, n_mp):
        self.n_dp, self.n_mp = n_dp, n_mp

    def table(self, place_dp, place_mp, rows_held):
        return [0], [0, 1, 2, 3]

    def gather(self, own, kinds):
        full = lax.all_gather(own, ("mp", "dp"), axis=0, tiled=True)
        full = full.reshape(self.n_mp, D, kinds, -1).transpose(2, 1, 0, 3)
        return full.reshape(kinds, D, PAIRS, -1).transpose(2, 1, 0, 3).reshape(PAIRS, D, -1)

    def weights(self, tab, query, keyval, output, inner, outer, gains, table, encoder, rows_held):
        place_dp, place_mp = lax.axis_index("dp"), lax.axis_index("mp")
        parts = []
        for i in range(2):
            parts += [query[i], keyval[i, 0], keyval[i, 1], output[i]]
        attention = self.gather(jnp.concatenate(parts, axis=1).astype(bf16), 8)
        feed = self.gather(jnp.concatenate((inner, outer), axis=1).astype(bf16), 2)
        width = gains.shape[1]
        tile = jnp.zeros((EXTRA, D), f32)
        spot = jnp.where(place_mp == 0, gains, 0.0)
        tile = lax.dynamic_update_slice(tile, spot, (0, place_dp * width))
        heads, bands = table.shape
        tile = lax.dynamic_update_slice(tile, table, (8 + place_mp * heads, place_dp * bands))
        tile = lax.psum(tile.astype(bf16).astype(f32), ALL).astype(bf16)
        tile = jnp.concatenate((tile, jnp.zeros_like(tile)), axis=1)[None]
        tile = jnp.concatenate((tile, jnp.zeros((PAIRS - 1,) + tile.shape[1:], bf16)))
        sources = lax.all_to_all(encoder, "mp", split_axis=0, concat_axis=1, tiled=True)
        return [jnp.concatenate((attention, tile), axis=1)], [feed], [sources], feed

    def feed_slots(self, feed, after):
        return feed

    def reduce_core(self, parts, *how):
        return parts

    def reduce(self, grads):
        kinds = 4 if grads.shape[2] == 4 * PAIR else 2
        full = grads[:, :D].reshape(PAIRS, D, kinds, -1).transpose(2, 1, 0, 3)
        full = full.reshape(kinds, D, self.n_mp, -1).transpose(2, 1, 0, 3)
        total = lax.psum_scatter(
            full.reshape(self.n_mp * D, -1), ("mp", "dp"), scatter_dimension=0, tiled=True
        ).astype(f32)
        return total, lax.psum(grads[0, D:].astype(f32), ALL) if grads.shape[1] > D else None

    def along_z(self, own):
        return [own]

    def finish(self, tab, outputs, row_grads, feed, cross, own):
        rows = [lax.all_gather(x, "mp", axis=0, tiled=True) for x in (outputs[0], row_grads)]
        return rows, [self.reduce(parts[0][0]) for parts in (feed, cross, own)]

    def reduce_second(self, parts, after):
        return parts

    def whole_z(self, pieces, after):
        return pieces


def shards(
    plan,
    inputs,
    encoder,
    cotangent,
    target_segments,
    encoder_segments,
    query_weight,
    query_first,
    query_second,
    keyval_weight,
    keyval_first,
    keyval_second,
    output_weight,
    output_first,
    output_second,
    inner_weight,
    inner_first,
    inner_second,
    outer_weight,
    outer_first,
    outer_second,
    gains,
    gains_first,
    gains_second,
    bias_table,
    table_first,
    table_second,
):
    n_slots, out_slots = plan.n_slots, plan.out_slots
    n_outs = len(out_slots)
    seq_count, length, _ = inputs.shape
    source_length = encoder_segments.shape[1]
    rows_held = seq_count // plan.n_mp
    tokens, sources = rows_held * length, rows_held * source_length
    place_dp, place_mp = lax.axis_index("dp"), lax.axis_index("mp")
    slot_table, pair_table = plan.table(place_dp, place_mp, rows_held)
    entries = slot_table + [0] * (16 - len(slot_table)) + pair_table + [0] * 4
    entries = entries + [place_mp * rows_held, place_dp, place_mp] + [0] * 5
    tab = jnp.stack([jnp.asarray(entry, jnp.int32) for entry in entries])
    onehot = bucket_onehot(length)
    attn_slots, feed, pieces, feed_base = plan.weights(
        tab,
        query_weight,
        keyval_weight,
        output_weight.transpose(0, 2, 1),
        inner_weight,
        outer_weight.T,
        gains,
        bias_table.T,
        encoder,
        rows_held,
    )
    n_pieces = len(pieces)
    rows, columns = query_weight.shape[1:]
    width = gains.shape[1]
    bands, heads = bias_table.shape

    flat = (tokens, D)
    paired = (PAIRS, tokens, PAIR)
    wide = (PAIRS, sources, PAIR)
    stats = shape((PAIRS, rows_held, 2 * length), f32)
    attn_weights = VM((PAIRS, D, 4 * PAIR), bf16)

    after_self, normed_one, q_one, k_one, v_one, mix_one, sum_one, gain_rows, falls = call(
        functools.partial(self_forward_kernel, n_slots, 1, rows_held),
        [(tab, "smem")] + vmems((target_segments, onehot)) + anys([inputs] + attn_slots + [feed_base]),
        [shape(flat, f32), shape(flat, bf16)]
        + [shape(paired, bf16)] * 4
        + [stats, shape((8, D), f32), shape((8, length), f32)],
        [
            attn_weights,
            VM((n_slots, PAIRS, EXTRA, D), bf16),
            VM((rows_held, length, D), bf16),
            dma_sems(n_slots, PAIRS),
            dma_sems(n_slots),
            pltpu.SemaphoreType.DMA,
        ],
        room=56,
        micros=6,
    )
    after_cross, normed_two, q_two, k_two, v_two, mix_two, sum_two, source_rows = call(
        functools.partial(cross_forward_kernel, n_slots, n_pieces, rows_held),
        [(tab, "smem")]
        + vmems((target_segments, encoder_segments, gain_rows, after_self))
        + anys(attn_slots + pieces),
        [
            shape(flat, f32),
            shape(flat, bf16),
            shape(paired, bf16),
            shape(wide, bf16),
            shape(wide, bf16),
            shape(paired, bf16),
            stats,
            shape((rows_held, source_length, D), bf16),
        ],
        [attn_weights, dma_sems(n_slots, PAIRS), dma_sems(n_pieces)],
        room=56,
        micros=11,
    )

    def grad_outs(extra, width_out):
        return [
            shape((count, PAIRS, D // n_slots + extra, width_out), bf16) for count in out_slots
        ]

    feed_slots = plan.feed_slots(feed, [after_cross])
    feed_result = call(
        functools.partial(feed_kernel, n_slots, n_outs, rows_held),
        [(tab, "smem")] + vmems((gain_rows, after_cross)) + anys([cotangent] + feed_slots),
        [shape(flat, bf16), shape(flat, f32), shape((1, D), f32)] + grad_outs(0, 2 * HIDDEN),
        [
            VM((PAIRS, D, 2 * HIDDEN), bf16),
            VM((rows_held, length, D), bf16),
            VM((D, tokens), bf16),
            VM((D, tokens), bf16),
            VM((D, tokens), bf16),
            VM((D, tokens), bf16),
            VM((n_slots, PAIRS, D // n_slots, 2 * HIDDEN), bf16),
            dma_sems(n_slots, PAIRS),
            pltpu.SemaphoreType.DMA,
            dma_sems(n_outs, PAIRS),
        ],
        any_outs=range(3, 3 + n_outs),
        room=56,
        micros=10,
    )
    low_out, grad_second, gain_three = feed_result[:3]
    core_feed = plan.reduce_core(feed_result[3:], (), True)
    grad_first, gain_two, dq_two, dk_two, dv_two = call(
        functools.partial(cross_back_kernel, n_slots, n_pieces, rows_held),
        [(tab, "smem")]
        + vmems((target_segments, encoder_segments, gain_rows, grad_second, after_self))
        + vmems((q_two, k_two, v_two, sum_two))
        + anys(attn_slots),
        [shape(flat, f32), shape((1, D), f32), shape(paired, bf16), shape(wide, bf16), shape(wide, bf16)],
        [attn_weights, dma_sems(n_slots, PAIRS)],
        room=56,
        micros=10,
    )
    self_result = call(
        functools.partial(self_back_kernel, n_slots, n_outs, 1, rows_held),
        [(tab, "smem")]
        + vmems((target_segments, onehot, gain_rows, falls, gain_two, gain_three, grad_first))
        + anys([inputs])
        + vmems((normed_one, q_one, k_one, v_one, mix_one, sum_one))
        + anys(attn_slots + [core_feed[0]]),
        [shape(flat, bf16)] + grad_outs(EXTRA, 4 * PAIR),
        [
            attn_weights,
            VM((rows_held, length, D), bf16),
            VM((D, tokens), bf16),
            VM((D, tokens), bf16),
            VM((D, tokens), bf16),
            VM((D, tokens), bf16),
            VM((8, length), f32),
            VM((n_slots, PAIRS, D // n_slots + EXTRA, 4 * PAIR), bf16),
            dma_sems(n_slots, PAIRS),
            pltpu.SemaphoreType.DMA,
            dma_sems(n_outs, 2 * PAIRS),
        ],
        any_outs=range(1, 1 + n_outs),
        room=12,
        micros=10,
    )
    cross_grads = call(
        functools.partial(cross_weights_kernel, n_slots, n_outs, 1),
        [(tab, "smem")]
        + vmems((grad_second, normed_two, mix_two, source_rows, dq_two, dk_two, dv_two))
        + anys([self_result[1]]),
        grad_outs(0, 4 * PAIR),
        [
            VM((D, tokens), bf16),
            VM((D, tokens), bf16),
            VM((D, tokens), bf16),
            VM((D, tokens), bf16),
            VM((D, sources), bf16),
            VM((D, sources), bf16),
            VM((n_slots, PAIRS, D // n_slots, 4 * PAIR), bf16),
            dma_sems(n_outs, PAIRS),
        ],
        any_outs=range(n_outs),
        room=12,
        micros=7,
    )
    out_pieces = plan.along_z(gate(low_out.reshape(rows_held, length, D), [core_feed[0]]))
    second_feed = plan.reduce_second(core_feed, out_pieces[1:] + [cross_grads[0]])
    core_self = plan.reduce_core(self_result[1:], second_feed[:1], True, 20)
    out_pieces = plan.whole_z(out_pieces, second_feed[:1])
    (outputs, input_grad), ((grad_feed, _), (grad_cross, _), (grad_self, tile)) = plan.finish(
        tab, out_pieces, self_result[0].reshape(rows_held, length, D), second_feed, cross_grads, core_self
    )

    def kind(grads, number):
        return grads[:rows, number * columns : (number + 1) * columns]

    hidden = inner_weight.shape[1]
    grads = (
        jnp.stack((kind(grad_self, 0), kind(grad_cross, 0))),
        jnp.stack(
            (
                jnp.stack((kind(grad_self, 1), kind(grad_self, 2))),
                jnp.stack((kind(grad_cross, 1), kind(grad_cross, 2))),
            )
        ),
        jnp.stack((kind(grad_self, 3).T, kind(grad_cross, 3).T)),
        grad_feed[:, :hidden],
        grad_feed[:, hidden:].T,
        lax.dynamic_slice_in_dim(tile[0:3], place_dp * width, width, 1),
        lax.dynamic_slice(tile, (8 + place_mp * heads, place_dp * bands), (heads, bands)).T,
    )
    params = (
        query_weight,
        keyval_weight,
        output_weight,
        inner_weight,
        outer_weight,
        gains,
        bias_table,
    )
    firsts = (
        query_first,
        keyval_first,
        output_first,
        inner_first,
        outer_first,
        gains_first,
        table_first,
    )
    seconds = (
        query_second,
        keyval_second,
        output_second,
        inner_second,
        outer_second,
        gains_second,
        table_second,
    )
    updated = [
        adam_step(*param_entry)
        for param_entry in zip(params, firsts, seconds, grads, step_rates(), step_decays)
    ]
    return (outputs, input_grad) + tuple(array for triple in updated for array in triple)


def solution(mesh):
    n_dp, n_mp = mesh.shape["dp"], mesh.shape["mp"]
    plan = (TreePlan if (n_dp, n_mp) == (8, 4) else PlainPlan)(n_dp, n_mp)
    by_query, by_keyval = P(None, "dp", "mp"), P(None, None, "dp", "mp")
    by_output, by_inner, by_outer = P(None, "mp", "dp"), P("dp", "mp"), P("mp", "dp")
    weights = (by_query,) * 3 + (by_keyval,) * 3 + (by_output,) * 3 + (by_inner,) * 3
    weights = weights + (by_outer,) * 3 + (P(None, "dp"),) * 3 + (P("dp", "mp"),) * 3
    tokens = P("dp", None, None)
    return jax.shard_map(
        functools.partial(shards, plan),
        mesh=mesh,
        in_specs=(tokens, P("dp", "mp", None), tokens, P("dp", None), P("dp", None)) + weights,
        out_specs=(tokens, tokens) + weights,
        check_vma=False,
    )
```
